32 devices in a mesh: replica: 4 (over y, x), sparse: 8 (over z, core).
Axes of the slice: x: 2, y: 2, z: 4, core: 2. Of those that a mesh axis runs over, the one named last changes fastest.
Arguments:
- item_table: bfloat16 [4096, 512], P('sparse'), may hold values from -5 to 5
- action_table: bfloat16 [4096, 512], P('sparse'), may hold values from -5 to 5
- item_owner: int32 [16384, 1], P(('replica', 'sparse')), may hold values from 0 to 7; in each aligned block of 512 rows (0 to 511, 512 to 1023, ...) at most 128 rows name the same one
- item_row: int32 [16384], P(('replica', 'sparse')), may hold values from 0 to 511
- action_owner: int32 [16384, 1], P(('replica', 'sparse')), may hold values from 0 to 7; in each aligned block of 512 rows (0 to 511, 512 to 1023, ...) at most 128 rows name the same one
- action_row: int32 [16384], P(('replica', 'sparse')), may hold values from 0 to 511
- input_norm_gain: float32 [512], replicated, may hold values from 0.4 to 1.6
- w_proj: bfloat16 [512, 2048], replicated, may hold values from -0.25 to 0.25
- w_out: bfloat16 [512, 512], replicated, may hold values from -0.25 to 0.25
- cotangent: bfloat16 [16384, 512], P(('replica', 'sparse')), may hold values from -0.59765625 to 0.59765625
Outputs:
- layer_out: bfloat16 [16384, 512], P(('replica', 'sparse'))
- item_grad: float32 [4096, 512], P('sparse', 'replica')
- action_grad: float32 [4096, 512], P('sparse', 'replica')
- grad_proj: float32 [512, 2048], P('sparse')
- grad_out: float32 [512, 512], P('sparse')
The draws below stay inside these ranges and needn't reach their ends.
Inputs may be any that keep to these rules, and one draw needn't show every extreme that they name: `item_owner`: in the rows of one device, no owner is named by more than 128 rows, a bound that some block reaches. `action_owner`: in the rows of one device, no owner is named by more than 128 rows, a bound that some block reaches.
All inputs are finite; a program needn't handle non-finite values.
Results may differ from the reference program's by a relative error of at most 0.015.
Values may be sent and summed in bfloat16 or wider, within the bound.
No kernel may reach another device: no remote copies, remote signals or barrier semaphores. Data moves between devices by JAX's collectives and lax.ppermute only.
A program may use at most 64 MiB of HBM per device.

```python
import math
import jax
import jax.numpy as jnp
import numpy as np
from jax import lax

D = 512
HEADS = 4
SEQ_LEN = 512
ROWS_DEV = 512
SHARDS = 8
CAP = 128
ROWS = 4096
TOKENS = 16384


def place_ends(array, own_key, smallest, high):
    extent = array.shape
    spot = [jax.random.randint(jax.random.fold_in(own_key, axis), (), 0, extent[axis]) for axis in range(len(extent))]
    array = array.at[tuple(spot)].set(smallest)
    longest = extent.index(max(extent))
    spot[longest] = (spot[longest] + 1) % extent[longest]
    return array.at[tuple(spot)].set(high)


def shard_levels(key, extent, cuts, smallest, high):
    loudness = 1.0
    for axis_at, shards_of in cuts:
        draws = jax.random.uniform(jax.random.fold_in(jax.random.fold_in(key, 6), axis_at), (shards_of,), jnp.float32, smallest / len(cuts), high / len(cuts))
        loudness = loudness * jnp.repeat(jnp.exp(draws), extent[axis_at] // shards_of).reshape((-1,) + (1,) * (len(extent) - 1 - axis_at))
    return loudness


def cumulative_ranks(amount, lean):
    portions = [(1 << 20) // math.isqrt(grade ** lean) + 1 for grade in range(1, amount + 1)]
    scale = 1 + sum(portions) // (1 << 30)
    return np.cumsum(np.array([max(1, weight // scale) for weight in portions]))


def skewed_ids(rng, extent, count, slope):
    listing = cumulative_ranks(count, slope)
    lot = jax.random.randint(jax.random.fold_in(rng, 1), extent, 0, int(listing[count - 1]))
    grade = jnp.searchsorted(jnp.asarray(listing, jnp.int32), lot, side="right")
    return jax.random.permutation(jax.random.fold_in(rng, 2), count)[grade].astype(jnp.int32)


def shared_out(stream_key, own, number, rows, amount, top, reach, slope):
    order = jax.random.permutation(stream_key, amount)
    packed, ordinary = portions_of(amount, rows * top, reach, slope, True), portions_of(amount, rows * top, reach, slope, False)
    places = jnp.arange(amount)

    def named(tallies, offset_by):
        used = int((tallies > 0).sum())
        fixed = max(1, used // 4)
        passed = fixed + (places - fixed + offset_by * (used - fixed)) % max(1, amount - fixed)
        return jnp.zeros((amount,), jnp.int32).at[order[jnp.where(places < fixed, places, passed)]].set(jnp.asarray(tallies, jnp.int32))

    tallies = jnp.where(number % 4 == 0, named(packed, number // 4), named(ordinary, number - number // 4 - 1))
    mixed = jax.random.permutation(jax.random.fold_in(own, 3), amount)
    donor, sink = mixed[0:amount // 2 * 2:2], mixed[1:amount // 2 * 2:2]
    margin = jnp.minimum(tallies[donor] - 1, reach - tallies[sink]) // 2
    margin = jnp.where((donor == order[0]) | (sink == order[0]) | (tallies[sink] == 0), 0, jnp.maximum(margin, 0))
    passed = jax.random.randint(jax.random.fold_in(own, 4), (amount // 2,), 0, 1 << 20) % (margin + 1)
    tallies = tallies.at[donor].add(-passed).at[sink].add(passed)
    labels = jnp.searchsorted(jnp.cumsum(tallies), jnp.arange(rows * top), side="right").astype(jnp.int32)
    listing = labels.reshape(top, rows).T
    listing = listing[jax.random.permutation(jax.random.fold_in(own, 1), rows)]
    offset_by = jax.random.randint(jax.random.fold_in(own, 2), (rows, 1), 0, top)
    return jnp.take_along_axis(listing, (jnp.arange(top)[None, :] + offset_by) % top, axis=1)


def portions_of(count, total, reach, lean, full):
    portions = [(1 << 20) // math.isqrt(rank ** lean) + 1 for rank in range(1, count + 1)]
    largest = reach if full else min(reach, max(-(-total // count), total * portions[0] // sum(portions)))
    least = 1 if total - largest >= count - 1 else 0
    given, surplus = [largest] + [least] * (count - 1), total - largest - least * (count - 1)
    while surplus > 0:
        free = [i for i in range(1, count) if given[i] < largest] or [i for i in range(1, count) if given[i] < reach]
        pool, left = sum([portions[i] for i in free]), surplus
        for i in free:
            addition = min(reach - given[i], max(1, left * portions[i] // pool), surplus)
            given[i] = given[i] + addition
            surplus = surplus - addition
    return np.array(given)


def centred(stream_key, shape, spread, bound, shards=(), dtype=jnp.bfloat16):
    drawn = jax.random.normal(stream_key, shape, jnp.float32) * spread
    if len(shards) > 0:
        drawn = shard_levels(stream_key, shape, shards, -0.22, 0.18) * drawn
    return jnp.clip(drawn, min=-bound, max=bound).astype(dtype)


def setup_inputs(seed: int = 0) -> dict:
    key_of = jax.random.split(jax.random.key(seed), 11)
    item_table = centred(key_of[0], (ROWS, D), 0.7, 5.0, ((0, 8),))
    action_table = centred(key_of[1], (ROWS, D), 0.7, 5.0, ((0, 8),))
    item_owner_keys = jax.random.split(jax.random.fold_in(key_of[2], 1), TOKENS // SEQ_LEN)
    item_owner_turns = jax.random.permutation(jax.random.fold_in(key_of[2], 3), TOKENS // SEQ_LEN)
    item_owner = jax.vmap(lambda own, number: shared_out(jax.random.fold_in(key_of[2], 2), own, number, SEQ_LEN, SHARDS, 1, CAP, 2))(item_owner_keys, item_owner_turns).reshape((TOKENS, 1))
    item_row = place_ends(skewed_ids(key_of[3], (TOKENS,), ROWS_DEV, 2), jax.random.fold_in(key_of[3], 3), 0, ROWS_DEV - 1).astype(jnp.int32)
    action_owner_keys = jax.random.split(jax.random.fold_in(key_of[4], 1), TOKENS // SEQ_LEN)
    action_owner_turns = jax.random.permutation(jax.random.fold_in(key_of[4], 3), TOKENS // SEQ_LEN)
    action_owner = jax.vmap(lambda own, number: shared_out(jax.random.fold_in(key_of[4], 2), own, number, SEQ_LEN, SHARDS, 1, CAP, 2))(action_owner_keys, action_owner_turns).reshape((TOKENS, 1))
    action_row = place_ends(skewed_ids(key_of[5], (TOKENS,), ROWS_DEV, 2), jax.random.fold_in(key_of[5], 3), 0, ROWS_DEV - 1).astype(jnp.int32)
    input_norm_gain = jnp.clip(1.0 + 0.12 * jax.random.normal(key_of[6], (D,), jnp.float32), 0.4, 1.6)
    w_proj = centred(key_of[7], (D, 4 * D), D ** -0.5, 0.25)
    w_out = centred(key_of[8], (D, D), D ** -0.5, 0.25)
    cotangent = centred(key_of[9], (TOKENS, D), 0.1, 0.59765625, ((0, 32),))
    return dict(item_table=item_table, action_table=action_table, item_owner=item_owner, item_row=item_row, action_owner=action_owner, action_row=action_row, input_norm_gain=input_norm_gain, w_proj=w_proj, w_out=w_out, cotangent=cotangent)


EPS = 1e-05

def silu_grad(value):
    sig = jax.nn.sigmoid(value)
    return sig * (1.0 + value * (1.0 - sig))

def apply_input_norm(value):
    centered = value - lax.optimization_barrier(jnp.mean(value, axis=-1, keepdims=True))
    scale = lax.rsqrt(lax.optimization_barrier(jnp.mean(centered * centered, axis=-1, keepdims=True)) + EPS)
    return (centered * scale, scale)

def norm_backward(upper, hat, scale):
    return scale * (upper - lax.optimization_barrier(jnp.mean(upper, axis=-1, keepdims=True)) - hat * lax.optimization_barrier(jnp.mean(upper * hat, axis=-1, keepdims=True)))

def mix(form, left, right):
    return jnp.einsum(form, left.astype(jnp.float32), right.astype(jnp.float32))

def sequence_pass(embedded, cotangent, input_norm_gain, w_proj, w_out):
    length, width = embedded.shape
    head_dim = width // HEADS
    factor = head_dim ** (-0.5)
    full_input_rows = embedded.astype(jnp.float32)
    centered_scaled_input, input_inverse_scale = apply_input_norm(full_input_rows)
    normalized_rows = (centered_scaled_input * input_norm_gain).astype(jnp.bfloat16)
    proj = jnp.dot(normalized_rows, w_proj, preferred_element_type=jnp.float32)
    act = jax.nn.silu(proj).astype(jnp.bfloat16)
    upart = act[:, :width]
    vheads = act[:, width:2 * width].reshape(length, HEADS, head_dim)
    qheads = act[:, 2 * width:3 * width].reshape(length, HEADS, head_dim)
    kheads = act[:, 3 * width:].reshape(length, HEADS, head_dim)
    causal = (jnp.arange(length)[None, :] <= jnp.arange(length)[:, None]).astype(jnp.float32)
    scores = mix('qhd,khd->hqk', qheads, kheads) * factor
    attn = (jax.nn.silu(scores) * causal / length).astype(jnp.bfloat16)
    attended = mix('hqk,khd->qhd', attn, vheads).reshape(length, width)
    ohat, oscale = apply_input_norm(attended)
    gated = (ohat * upart.astype(jnp.float32)).astype(jnp.bfloat16)
    layer_out = (full_input_rows + jnp.dot(gated, w_out, preferred_element_type=jnp.float32)).astype(jnp.bfloat16)
    dgated = jnp.dot(cotangent, w_out.T, preferred_element_type=jnp.float32)
    dupart = dgated * ohat
    dattended = norm_backward(dgated * upart.astype(jnp.float32), ohat, oscale).astype(jnp.bfloat16)
    dheads = dattended.reshape(length, HEADS, head_dim)
    dattn = mix('qhd,khd->hqk', dheads, vheads)
    dvalues = mix('hqk,qhd->khd', attn, dheads).reshape(length, width)
    dscores = (dattn * causal * silu_grad(scores) * (factor / length)).astype(jnp.bfloat16)
    dquery = mix('hqk,khd->qhd', dscores, kheads).reshape(length, width)
    dkeys = mix('hqk,qhd->khd', dscores, qheads).reshape(length, width)
    dact = jnp.concatenate([dupart, dvalues, dquery, dkeys], axis=1)
    dproj = (dact * silu_grad(proj)).astype(jnp.bfloat16)
    normalized_gradient = jnp.dot(dproj, w_proj.T, preferred_element_type=jnp.float32)
    token_gradient = (cotangent.astype(jnp.float32) + norm_backward(normalized_gradient * input_norm_gain, centered_scaled_input, input_inverse_scale)).astype(jnp.bfloat16)
    grad_proj = jnp.dot(normalized_rows.T, dproj, preferred_element_type=jnp.float32)
    grad_out = jnp.dot(gated.T, cotangent, preferred_element_type=jnp.float32)
    return (layer_out, token_gradient, grad_proj, grad_out)

def reference(item_table, action_table, item_owner, item_row, action_owner, action_row, input_norm_gain, w_proj, w_out, cotangent):
    item_index = (item_owner[:, 0] * ROWS_DEV + item_row).astype(jnp.int32)
    action_index = (action_owner[:, 0] * ROWS_DEV + action_row).astype(jnp.int32)
    embedded = (item_table[item_index].astype(jnp.float32) + action_table[action_index].astype(jnp.float32)).astype(jnp.bfloat16)
    count = TOKENS // SEQ_LEN
    seq_embedded = embedded.reshape(count, SEQ_LEN, D)
    seq_cotangent = cotangent.reshape(count, SEQ_LEN, D)

    def advance(carry, pair):
        layer_out, token_gradient, grad_proj, grad_out = sequence_pass(pair[0], pair[1], input_norm_gain, w_proj, w_out)
        return ((carry[0] + grad_proj, carry[1] + grad_out), (layer_out, token_gradient))
    start = (jnp.zeros((D, 4 * D), jnp.float32), jnp.zeros((D, D), jnp.float32))
    totals, results = lax.scan(advance, start, (seq_embedded, seq_cotangent))
    layer_out = results[0].reshape(TOKENS, D)
    token_gradient = results[1].reshape(TOKENS, D).astype(jnp.float32)
    item_grad = jax.ops.segment_sum(token_gradient, item_index, num_segments=ROWS)
    action_grad = jax.ops.segment_sum(token_gradient, action_index, num_segments=ROWS)
    return (layer_out, item_grad, action_grad, totals[0], totals[1])
```

```python
import jax
import jax.numpy as jnp
from jax import lax
from jax.experimental import pallas as pl
from jax.experimental.pallas import tpu as pltpu
from jax.sharding import PartitionSpec as P

HEADS = 4
EPS = 1e-05
LANES = 128
F32 = jnp.float32
BF16 = jnp.bfloat16
I32 = jnp.int32
VMEM_BYTES = 48 * 1024 * 1024

NN = ((1,), (0,))
NT = ((1,), (1,))
TN = ((0,), (0,))


def dot(left, right, dims=NN):
    return lax.dot_general(left, right, (dims, ((), ())), preferred_element_type=F32)


def sigmoid(value):
    return 0.5 * jnp.tanh(0.5 * value) + 0.5


def run(name, body, outs, args, smem=0, scratch=(), flops=0):
    outs = [jax.ShapeDtypeStruct(shape, dtype) for shape, dtype in outs]
    size = sum(a.size * a.dtype.itemsize for a in args)
    size += sum(o.size * o.dtype.itemsize for o in outs)
    in_smem = pl.BlockSpec(memory_space=pltpu.SMEM)
    in_vmem = pl.BlockSpec(memory_space=pltpu.VMEM)
    results = pl.pallas_call(
        body,
        out_shape=outs,
        in_specs=[in_smem] * smem + [in_vmem] * (len(args) - smem),
        out_specs=[in_vmem] * len(outs),
        scratch_shapes=list(scratch),
        compiler_params=pltpu.CompilerParams(vmem_limit_bytes=VMEM_BYTES),
        cost_estimate=pl.CostEstimate(flops=flops, bytes_accessed=size, transcendentals=0),
        name=name,
    )(*args)
    return list(results)


class Grid:
    def __init__(self):
        self.replicas = lax.axis_size("replica")
        self.shards = lax.axis_size("sparse")
        self.cores = 2 if self.shards % 2 == 0 else 1
        self.line = self.shards // self.cores
        self.r = lax.axis_index("replica")
        self.s = lax.axis_index("sparse")
        self.z = self.s // self.cores
        self.c = self.s % self.cores

    def peer(self, index, size, step):
        if size & (size - 1) == 0:
            return index ^ step
        return (step - index) % size

    def over_replica(self, value, step):
        n = self.replicas
        return lax.ppermute(value, "replica", [(i, self.peer(i, n, step)) for i in range(n)])

    def over_line(self, value, step):
        n, c = self.line, self.cores
        pairs = [(i, self.peer(i // c, n, step) * c + i % c) for i in range(n * c)]
        return lax.ppermute(value, "sparse", pairs)

    def over_pair(self, value):
        return lax.ppermute(value, "sparse", [(i, i ^ 1) for i in range(self.shards)])

    def replica_peer(self, step):
        return self.peer(self.r, self.replicas, step)

    def line_peer(self, step):
        return self.peer(self.z, self.line, step)


def fetch(keys, chunks, bases, before):
    count, many = len(keys), len(chunks)
    tokens = keys[0].shape[1]
    rows, cols = chunks[0].shape[0] // 2, chunks[0].shape[1]

    def body(base_ref, *refs):
        key_refs, chunk_refs = refs[:count], refs[count : count + many]
        before_refs, out_refs = refs[count + many : -count], refs[-count:]
        lane = lax.broadcasted_iota(I32, (tokens, LANES), 1)
        for k in range(count):
            total = before_refs[k][...].astype(F32) if before_refs else None
            for m in range(many):
                hot = []
                for table in range(2):
                    place = key_refs[k][table] - base_ref[m]
                    for start in range(0, rows, LANES):
                        hot.append(jnp.where(place == lane + start, 1.0, 0.0).astype(BF16))
                found = dot(jnp.concatenate(hot, axis=1), chunk_refs[m][...])
                total = found if total is None else total + found
            out_refs[k][...] = total.astype(BF16)

    return run(
        "fetch",
        body,
        [((tokens, cols), BF16)] * count,
        [bases, *keys, *chunks, *before],
        smem=1,
        flops=2 * count * many * tokens * 2 * rows * cols,
    )


def gather_grad(keys, pieces, bases, rows):
    count, many = len(keys), bases.shape[0]
    tokens, cols = pieces[0].shape

    def body(base_ref, *refs):
        key_refs, piece_refs, out_refs = refs[:count], refs[count : 2 * count], refs[2 * count :]
        piece = jnp.concatenate([ref[...] for ref in piece_refs], axis=0)
        row = lax.broadcasted_iota(I32, (rows, tokens), 0)
        for m in range(many):
            for table in range(2):
                hot = []
                for k in range(count):
                    place = key_refs[k][table : table + 1, :] - base_ref[m]
                    hot.append(jnp.where(place == row, 1.0, 0.0).astype(BF16))
                sums = dot(jnp.concatenate(hot, axis=1), piece)
                out_refs[m][table * rows : (table + 1) * rows, :] = sums.astype(BF16)

    return run(
        "gather_grad",
        body,
        [((2 * rows, cols), BF16)] * many,
        [bases, *keys, *pieces],
        smem=1,
        flops=2 * count * many * tokens * 2 * rows * cols,
    )


def sequence(blocks, pieces, cotangent, gain, w_proj, w_out):
    count = len(pieces)
    length, width = cotangent.shape
    cols = width // count
    head_dim = width // HEADS
    factor = head_dim ** (-0.5)
    tile = min(256, length)
    step = min(256, 4 * width)

    def body(block_ref, *refs):
        piece_refs = refs[:count]
        cot_ref, gain_ref, wp_ref, wo_ref = refs[count : count + 4]
        out_ref, *grad_refs = refs[count + 4 : 2 * count + 5]
        normed_ref, dproj_ref, gated_ref = refs[2 * count + 5 : 2 * count + 8]
        emb, act, slope, att, attn, dscale, dkey, dval, tok = refs[2 * count + 8 :]

        def start_of(k):
            return pl.multiple_of(block_ref[k] * cols, cols)

        for k in range(count):
            emb[:, pl.ds(start_of(k), cols)] = piece_refs[k][...]

        def norm_of(value):
            centred = value - jnp.mean(value, axis=-1, keepdims=True)
            scale = lax.rsqrt(jnp.mean(centred * centred, axis=-1, keepdims=True) + EPS)
            return centred * scale, scale

        def norm_back(upper, hat, scale):
            return scale * (
                upper
                - jnp.mean(upper, axis=-1, keepdims=True)
                - hat * jnp.mean(upper * hat, axis=-1, keepdims=True)
            )

        for at in range(0, length, tile):
            span = slice(at, at + tile)
            hat, _ = norm_of(emb[span, :].astype(F32))
            normed_ref[span, :] = (hat * gain_ref[...]).astype(BF16)

        normed = normed_ref[...]

        @pl.loop(0, 4 * width // step)
        def _(j):
            span = pl.ds(pl.multiple_of(j * step, step), step)
            proj = dot(normed, wp_ref[:, span])
            sig = sigmoid(proj)
            act[:, span] = (proj * sig).astype(BF16)
            slope[:, span] = sig * (1.0 + proj * (1.0 - sig))

        dkey[...] = jnp.zeros_like(dkey)
        dval[...] = jnp.zeros_like(dval)

        for at in range(0, length, tile):
            span = slice(at, at + tile)
            seen = at + tile
            past = slice(0, seen)
            keep = lax.broadcasted_iota(I32, (tile, seen), 1) <= at + lax.broadcasted_iota(
                I32, (tile, seen), 0
            )
            for h in range(HEADS):
                head = [slice(p * width + h * head_dim, p * width + (h + 1) * head_dim) for p in range(4)]
                scores = dot(act[span, head[2]], act[past, head[3]], NT) * factor
                sig = sigmoid(scores)
                soft = jnp.where(keep, scores * sig * (1.0 / length), 0.0).astype(BF16)
                attn[h, :, :seen] = soft
                grad = sig * (1.0 + scores * (1.0 - sig)) * (factor / length)
                dscale[h, :, :seen] = jnp.where(keep, grad, 0.0)
                att[:, head[0]] = dot(soft, act[past, head[1]])
            hat, scale = norm_of(att[...])
            gate = act[span, :width].astype(F32)
            gated = (hat * gate).astype(BF16)
            gated_ref[span, :] = gated
            out_ref[span, :] = (emb[span, :].astype(F32) + dot(gated, wo_ref[...])).astype(BF16)
            dgated = dot(cot_ref[span, :], wo_ref[...], NT)
            dproj_ref[span, :width] = (dgated * hat * slope[span, :width]).astype(BF16)
            datt = norm_back(dgated * gate, hat, scale).astype(BF16)
            for h in range(HEADS):
                head = [slice(p * width + h * head_dim, p * width + (h + 1) * head_dim) for p in range(4)]
                dhead = datt[:, head[0]]
                dattn = dot(dhead, act[past, head[1]], NT)
                dscores = (dattn * dscale[h, :, :seen]).astype(BF16)
                dquery = dot(dscores, act[past, head[3]])
                dproj_ref[span, head[2]] = (dquery * slope[span, head[2]]).astype(BF16)
                dkey[past, head[0]] += dot(dscores, act[span, head[2]], TN)
                dval[past, head[0]] += dot(attn[h, :, :seen], dhead, TN)

        dproj_ref[:, width : 2 * width] = (dval[...] * slope[:, width : 2 * width]).astype(BF16)
        dproj_ref[:, 3 * width :] = (dkey[...] * slope[:, 3 * width :]).astype(BF16)

        for at in range(0, length, tile):
            span = slice(at, at + tile)
            hat, scale = norm_of(emb[span, :].astype(F32))
            upper = dot(dproj_ref[span, :], wp_ref[...], NT) * gain_ref[...]
            grad = cot_ref[span, :].astype(F32) + norm_back(upper, hat, scale)
            tok[span, :] = grad.astype(BF16)

        for k in range(count):
            grad_refs[k][...] = tok[:, pl.ds(start_of(k), cols)]

    return run(
        "sequence",
        body,
        [((length, width), BF16)]
        + [((length, cols), BF16)] * count
        + [((length, width), BF16), ((length, 4 * width), BF16), ((length, width), BF16)],
        [blocks, *pieces, cotangent, gain, w_proj, w_out],
        smem=1,
        scratch=[
            pltpu.VMEM((length, width), BF16),
            pltpu.VMEM((length, 4 * width), BF16),
            pltpu.VMEM((length, 4 * width), F32),
            pltpu.VMEM((tile, width), F32),
            pltpu.VMEM((HEADS, tile, length), BF16),
            pltpu.VMEM((HEADS, tile, length), F32),
            pltpu.VMEM((length, width), F32),
            pltpu.VMEM((length, width), F32),
            pltpu.VMEM((length, width), BF16),
        ],
        flops=28 * length * width * width,
    )


def weight_grad(core, normed, dproj, gated, cotangent, cores, line):
    length, width = normed.shape
    rows = width // (cores * line)
    half = width // cores
    total = dproj.shape[1] + cotangent.shape[1]

    def body(core_ref, n_ref, d_ref, g_ref, c_ref, *out_refs):
        feature = lax.broadcasted_iota(I32, (width, half), 0)
        column = lax.broadcasted_iota(I32, (width, half), 1)
        for m, out_ref in enumerate(out_refs):
            parity = (core_ref[0] + cores - 1 - m) % cores
            wanted = (column // rows * cores + parity) * rows + column % rows
            pick = jnp.where(feature == wanted, 1.0, 0.0).astype(BF16)
            n_part = dot(n_ref[...], pick).astype(BF16)
            g_part = dot(g_ref[...], pick).astype(BF16)
            edge = d_ref.shape[1]
            for at in range(0, edge, width):
                out_ref[:, at : at + width] = dot(n_part, d_ref[:, at : at + width], TN).astype(BF16)
            out_ref[:, edge:] = dot(g_part, c_ref[...], TN).astype(BF16)

    return run(
        "weight_grad",
        body,
        [((half, total), BF16)] * cores,
        [core, normed, dproj, gated, cotangent],
        smem=1,
        flops=2 * length * width * (total + 2 * width),
    )


def add_and_split(blocks, parts, along, out_first=F32):
    count = blocks.shape[0]
    shape = list(parts[0].shape)
    whole = tuple(shape)
    shape[along] //= count
    size = shape[along]

    def body(block_ref, *refs):
        part_refs, out_refs, held = refs[: len(parts)], refs[len(parts) : -1], refs[-1]
        total = part_refs[0][...].astype(F32)
        for ref in part_refs[1:]:
            total = total + ref[...].astype(F32)
        held[...] = total
        for k in range(count):
            span = pl.ds(pl.multiple_of(block_ref[k] * size, size), size)
            piece = held[:, span] if along == 1 else held[span, :]
            out_refs[k][...] = piece.astype(out_refs[k].dtype)

    dtypes = [out_first] + [BF16] * (count - 1)
    return run(
        "add_and_split",
        body,
        [(tuple(shape), dtype) for dtype in dtypes],
        [blocks, *parts],
        smem=1,
        scratch=[pltpu.VMEM(whole, F32)],
    )


def assemble(blocks, parts, edge):
    rows, cols = parts[0].shape
    total = cols * len(parts)

    def body(block_ref, *refs):
        part_refs, (left_ref, right_ref, held) = refs[: len(parts)], refs[len(parts) :]
        for k, ref in enumerate(part_refs):
            held[:, pl.ds(pl.multiple_of(block_ref[k] * cols, cols), cols)] = ref[...].astype(F32)
        left_ref[...] = held[:, :edge]
        right_ref[...] = held[:, edge:]

    return run(
        "assemble",
        body,
        [((rows, edge), F32), ((rows, total - edge), F32)],
        [blocks, *parts],
        smem=1,
        scratch=[pltpu.VMEM((rows, total), F32)],
    )


def local(
    item_table,
    action_table,
    item_owner,
    item_row,
    action_owner,
    action_row,
    input_norm_gain,
    w_proj,
    w_out,
    cotangent,
):
    grid = Grid()
    rows, width = item_table.shape
    replicas, line, cores = grid.replicas, grid.line, grid.cores
    length = item_row.shape[0]
    cols = width // replicas
    blocks = jnp.stack([grid.replica_peer(k) for k in range(replicas)]).astype(I32)
    planes = jnp.stack([grid.line_peer(k) for k in range(line)]).astype(I32)

    def bases_of(k):
        first = grid.line_peer(k) * cores
        return jnp.stack([(first + (grid.c + m) % cores) * rows for m in range(cores)]).astype(I32)

    own = jnp.concatenate(
        [
            lax.dynamic_slice_in_dim(item_table, grid.r * cols, cols, 1),
            lax.dynamic_slice_in_dim(action_table, grid.r * cols, cols, 1),
        ],
        axis=0,
    )
    keys = jnp.stack(
        [item_owner[:, 0] * rows + item_row, action_owner[:, 0] * rows + action_row]
    ).astype(I32)

    held = [own] + [grid.over_line(own, k) for k in range(1, line)]
    key_rows = [keys] + [grid.over_replica(keys, k) for k in range(1, replicas)]
    key_cols = [jnp.broadcast_to(k[:, :, None], (2, length, LANES)) for k in key_rows]

    found = []
    for k in range(line):
        chunks = [held[k]] + ([grid.over_pair(held[k])] if cores == 2 else [])
        found = fetch(key_cols, chunks, bases_of(k), found)
    pieces = found[:1] + [grid.over_replica(found[k], k) for k in range(1, replicas)]

    layer_out, *rest = sequence(
        blocks, pieces, cotangent, input_norm_gain.reshape(1, width), w_proj, w_out
    )
    tokens, (normed, dproj, gated) = rest[:replicas], rest[replicas:]
    tokens = tokens[:1] + [grid.over_replica(tokens[k], k) for k in range(1, replicas)]

    order = list(range(1, line)) + [0]
    sums = {}
    for k in order:
        mine, *other = gather_grad(key_rows, tokens, bases_of(k), rows)
        total = mine.astype(F32)
        for part in other:
            total = total + grid.over_pair(part).astype(F32)
        sums[k] = grid.over_line(total.astype(BF16), k) if k else total
    table_grad = sums[0]
    for k in range(1, line):
        table_grad = table_grad + sums[k].astype(F32)

    parts = weight_grad(grid.c.reshape(1), normed, dproj, gated, cotangent, cores, line)
    mine, other = parts[-1], parts[:-1]
    split = add_and_split(blocks, [mine] + [grid.over_pair(o) for o in other], 1)
    parts = split[:1] + [grid.over_replica(split[k], k) for k in range(1, replicas)]
    split = add_and_split(planes, parts, 0)
    parts = split[:1] + [grid.over_line(split[k], k) for k in range(1, line)]
    total = parts[0]
    for part in parts[1:]:
        total = total + part.astype(F32)
    total = total.astype(BF16)
    parts = [total] + [grid.over_replica(total, k) for k in range(1, replicas)]
    grad_proj, grad_out = assemble(blocks, parts, 4 * width)

    return layer_out, table_grad[:rows], table_grad[rows:], grad_proj, grad_out


def solution(mesh):
    tokens = ("replica", "sparse")
    in_specs = (
        P("sparse", None),
        P("sparse", None),
        P(tokens, None),
        P(tokens),
        P(tokens, None),
        P(tokens),
        P(),
        P(),
        P(),
        P(tokens, None),
    )
    out_specs = (
        P(tokens, None),
        P("sparse", "replica"),
        P("sparse", "replica"),
        P("sparse", None),
        P("sparse", None),
    )
    return jax.shard_map(local, mesh=mesh, in_specs=in_specs, out_specs=out_specs, check_vma=False)
```

```python
import jax
import jax.numpy as jnp
from jax import lax
from jax.experimental import pallas as pl
from jax.experimental.pallas import tpu as pltpu
from jax.sharding import PartitionSpec as P

HEADS = 4
EPS = 1e-05
LANES = 128
F32 = jnp.float32
BF16 = jnp.bfloat16
I32 = jnp.int32
VMEM_BYTES = 32 * 1024 * 1024

NN = ((1,), (0,))
NT = ((1,), (1,))
TN = ((0,), (0,))


def dot(left, right, dims=NN):
    return lax.dot_general(left, right, (dims, ((), ())), preferred_element_type=F32)


def sigmoid(value):
    return 0.5 * jnp.tanh(0.5 * value) + 0.5


def run(name, body, outs, args, smem=0, scratch=()):
    outs = [jax.ShapeDtypeStruct(shape, dtype) for shape, dtype in outs]
    in_smem = pl.BlockSpec(memory_space=pltpu.SMEM)
    in_vmem = pl.BlockSpec(memory_space=pltpu.VMEM)
    results = pl.pallas_call(
        body,
        out_shape=outs,
        in_specs=[in_smem] * smem + [in_vmem] * (len(args) - smem),
        out_specs=[in_vmem] * len(outs),
        scratch_shapes=list(scratch),
        compiler_params=pltpu.CompilerParams(vmem_limit_bytes=VMEM_BYTES),
        cost_estimate=pl.CostEstimate(flops=0, bytes_accessed=0, transcendentals=0),
        name=name,
    )(*args)
    return list(results)


class Grid:
    def __init__(self):
        self.replicas = lax.axis_size("replica")
        self.shards = lax.axis_size("sparse")
        self.cores = 2 if self.shards % 2 == 0 else 1
        self.line = self.shards // self.cores
        self.r = lax.axis_index("replica")
        self.s = lax.axis_index("sparse")
        self.z = self.s // self.cores
        self.c = self.s % self.cores

    def peer(self, index, size, step):
        if size & (size - 1) == 0:
            return index ^ step
        return (step - index) % size

    def over_replica(self, value, step):
        n = self.replicas
        return lax.ppermute(value, "replica", [(i, self.peer(i, n, step)) for i in range(n)])

    def swap_replica(self, value):
        return lax.all_to_all(value, "replica", split_axis=0, concat_axis=0, tiled=True)

    def swap_line(self, value):
        groups = [list(range(c, self.shards, self.cores)) for c in range(self.cores)]
        return lax.all_to_all(
            value, "sparse", split_axis=0, concat_axis=0, axis_index_groups=groups, tiled=True
        )

    def over_line(self, value, step):
        n, c = self.line, self.cores
        pairs = [(i, self.peer(i // c, n, step) * c + i % c) for i in range(n * c)]
        return lax.ppermute(value, "sparse", pairs)

    def over_pair(self, value):
        return lax.ppermute(value, "sparse", [(i, i ^ 1) for i in range(self.shards)])

    def replica_peer(self, step):
        return self.peer(self.r, self.replicas, step)

    def line_peer(self, step):
        return self.peer(self.z, self.line, step)


def make_keys(rows, item_owner, item_row, action_owner, action_row, copies):
    length = item_row.shape[0]

    def body(*refs):
        *in_refs, out_ref = refs
        for table in range(2):
            owner, row = in_refs[2 * table : 2 * table + 2]
            number = owner[...] * rows + row[...]
            for k in range(copies):
                out_ref[k, table : table + 1, :] = number

    args = [a.reshape(1, length) for a in (item_owner, item_row, action_owner, action_row)]
    return run("make_keys", body, [((copies, 2, length), I32)], args)[0]


def fetch(cohorts, chunk, base, before=()):
    many = len(cohorts)
    count, _, tokens, _ = cohorts[0].shape
    rows, cols = chunk.shape[0] // 2, chunk.shape[1]

    def body(base_ref, chunk_ref, *refs):
        key_refs, before_refs, out_refs = refs[:many], refs[many:-many], refs[-many:]
        lane = lax.broadcasted_iota(I32, (tokens, LANES), 1)
        for m in range(many):
            for k in range(count):
                hot = []
                for table in range(2):
                    place = key_refs[m][k, table] - base_ref[0]
                    for start in range(0, rows, LANES):
                        hot.append(jnp.where(place == lane + start, 1.0, 0.0).astype(BF16))
                found = dot(jnp.concatenate(hot, axis=1), chunk_ref[...])
                if before_refs:
                    found = found + before_refs[m][k].astype(F32)
                out_refs[m][k] = found.astype(BF16)

    return run(
        "fetch",
        body,
        [((count, tokens, cols), BF16)] * many,
        [base.reshape(1), chunk, *cohorts, *before],
        smem=1,
    )


def gather_grad(keys, pieces, base, rows, before=(), out=BF16):
    count, _, tokens = keys.shape
    cols = pieces.shape[-1]

    def body(base_ref, key_ref, piece_ref, *refs):
        *before_refs, out_ref = refs
        piece = piece_ref[...].reshape(count * tokens, cols)
        row = lax.broadcasted_iota(I32, (rows, tokens), 0)
        for table in range(2):
            span = slice(table * rows, (table + 1) * rows)
            hot = []
            for k in range(count):
                place = key_ref[k, table : table + 1, :] - base_ref[0]
                hot.append(jnp.where(place == row, 1.0, 0.0).astype(BF16))
            sums = dot(jnp.concatenate(hot, axis=1), piece)
            for ref in before_refs:
                sums = sums + ref[span, :].astype(F32)
            out_ref[span, :] = sums.astype(out)

    return run(
        "gather_grad",
        body,
        [((2 * rows, cols), out)],
        [base.reshape(1), keys, pieces, *before],
        smem=1,
    )[0]


def sequence(pieces, cotangent, gain, w_proj, w_out):
    count = pieces.shape[0]
    length, width = cotangent.shape
    cols = width // count
    head_dim = width // HEADS
    factor = head_dim ** (-0.5)
    tile = min(256, length)
    step = min(256, 4 * width)

    def body(piece_ref, cot_ref, gain_ref, wp_ref, wo_ref, *refs):
        out_ref, grad_ref, normed_ref, dproj_ref, gated_ref = refs[:5]
        emb, act, slope, att, attn, dscale, dkey, dval = refs[5:]

        for k in range(count):
            emb[:, k * cols : (k + 1) * cols] = piece_ref[k]

        def norm_of(value):
            centred = value - jnp.mean(value, axis=-1, keepdims=True)
            scale = lax.rsqrt(jnp.mean(centred * centred, axis=-1, keepdims=True) + EPS)
            return centred * scale, scale

        def norm_back(upper, hat, scale):
            return scale * (
                upper
                - jnp.mean(upper, axis=-1, keepdims=True)
                - hat * jnp.mean(upper * hat, axis=-1, keepdims=True)
            )

        for at in range(0, length, tile):
            span = slice(at, at + tile)
            hat, _ = norm_of(emb[span, :].astype(F32))
            normed_ref[span, :] = (hat * gain_ref[...]).astype(BF16)

        normed = normed_ref[...]

        @pl.loop(0, 4 * width // step)
        def _(j):
            span = pl.ds(pl.multiple_of(j * step, step), step)
            proj = dot(normed, wp_ref[:, span])
            sig = sigmoid(proj)
            act[:, span] = (proj * sig).astype(BF16)
            slope[:, span] = sig * (1.0 + proj * (1.0 - sig))

        dkey[...] = jnp.zeros_like(dkey)
        dval[...] = jnp.zeros_like(dval)

        for at in range(0, length, tile):
            span = slice(at, at + tile)
            seen = at + tile
            past = slice(0, seen)
            keep = lax.broadcasted_iota(I32, (tile, seen), 1) <= at + lax.broadcasted_iota(
                I32, (tile, seen), 0
            )
            for h in range(HEADS):
                head = [slice(p * width + h * head_dim, p * width + (h + 1) * head_dim) for p in range(4)]
                scores = dot(act[span, head[2]], act[past, head[3]], NT) * factor
                sig = sigmoid(scores)
                soft = jnp.where(keep, scores * sig * (1.0 / length), 0.0).astype(BF16)
                attn[h, :, :seen] = soft
                grad = sig * (1.0 + scores * (1.0 - sig)) * (factor / length)
                dscale[h, :, :seen] = jnp.where(keep, grad, 0.0)
                att[:, head[0]] = dot(soft, act[past, head[1]])
            hat, scale = norm_of(att[...])
            gate = act[span, :width].astype(F32)
            gated = (hat * gate).astype(BF16)
            gated_ref[span, :] = gated
            out_ref[span, :] = (emb[span, :].astype(F32) + dot(gated, wo_ref[...])).astype(BF16)
            dgated = dot(cot_ref[span, :], wo_ref[...], NT)
            dproj_ref[span, :width] = (dgated * hat * slope[span, :width]).astype(BF16)
            datt = norm_back(dgated * gate, hat, scale).astype(BF16)
            for h in range(HEADS):
                head = [slice(p * width + h * head_dim, p * width + (h + 1) * head_dim) for p in range(4)]
                dhead = datt[:, head[0]]
                dattn = dot(dhead, act[past, head[1]], NT)
                dscores = (dattn * dscale[h, :, :seen]).astype(BF16)
                dquery = dot(dscores, act[past, head[3]])
                dproj_ref[span, head[2]] = (dquery * slope[span, head[2]]).astype(BF16)
                dkey[past, head[0]] += dot(dscores, act[span, head[2]], TN)
                dval[past, head[0]] += dot(attn[h, :, :seen], dhead, TN)

        dproj_ref[:, width : 2 * width] = (dval[...] * slope[:, width : 2 * width]).astype(BF16)
        dproj_ref[:, 3 * width :] = (dkey[...] * slope[:, 3 * width :]).astype(BF16)

        for at in range(0, length, tile):
            span = slice(at, at + tile)
            hat, scale = norm_of(emb[span, :].astype(F32))
            upper = dot(dproj_ref[span, :], wp_ref[...], NT) * gain_ref[...]
            grad = cot_ref[span, :].astype(F32) + norm_back(upper, hat, scale)
            for k in range(count):
                grad_ref[k, span, :] = grad[:, k * cols : (k + 1) * cols].astype(BF16)

    return run(
        "sequence",
        body,
        [
            ((length, width), BF16),
            ((count, length, cols), BF16),
            ((length, width), BF16),
            ((length, 4 * width), BF16),
            ((length, width), BF16),
        ],
        [pieces, cotangent, gain, w_proj, w_out],
        scratch=[
            pltpu.VMEM((length, width), BF16),
            pltpu.VMEM((length, 4 * width), BF16),
            pltpu.VMEM((length, 4 * width), F32),
            pltpu.VMEM((tile, width), F32),
            pltpu.VMEM((HEADS, tile, length), BF16),
            pltpu.VMEM((HEADS, tile, length), F32),
            pltpu.VMEM((length, width), F32),
            pltpu.VMEM((length, width), F32),
        ],
    )


def weight_grad(parity, normed, dproj, gated, cotangent, cores, line, blocks, before=()):
    length, width = normed.shape
    rows = width // (cores * line)
    half = width // cores
    edge = dproj.shape[1]
    total = edge + cotangent.shape[1]
    cols = total // blocks

    def body(parity_ref, n_ref, d_ref, g_ref, c_ref, *refs):
        *before_refs, out_ref = refs
        feature = lax.broadcasted_iota(I32, (width, half), 0)
        column = lax.broadcasted_iota(I32, (width, half), 1)
        wanted = (column // rows * cores + parity_ref[0]) * rows + column % rows
        pick = jnp.where(feature == wanted, 1.0, 0.0).astype(BF16)
        n_part = dot(n_ref[...], pick).astype(BF16)
        g_part = dot(g_ref[...], pick).astype(BF16)
        for k in range(blocks):
            first, last = k * cols, (k + 1) * cols
            parts = []
            if first < edge:
                parts.append(dot(n_part, d_ref[:, first : min(last, edge)], TN))
            if last > edge:
                parts.append(dot(g_part, c_ref[:, max(first, edge) - edge : last - edge], TN))
            sums = parts[0] if len(parts) == 1 else jnp.concatenate(parts, axis=1)
            for ref in before_refs:
                sums = sums + ref[k].astype(F32)
            out_ref[k] = sums.astype(BF16)

    return run(
        "weight_grad",
        body,
        [((blocks, half, cols), BF16)],
        [parity.reshape(1), normed, dproj, gated, cotangent, *before],
        smem=1,
    )[0]


def add_up(parts, copies):
    count, *shape = parts.shape

    def body(part_ref, out_ref):
        total = part_ref[0].astype(F32)
        for k in range(1, count):
            total = total + part_ref[k].astype(F32)
        for k in range(copies):
            out_ref[k] = total.astype(BF16)

    return run("add_up", body, [((copies, *shape), BF16)], [parts])[0]


def assemble(parts, edge):
    count, rows, cols = parts.shape
    total = cols * count

    def body(part_ref, left_ref, right_ref):
        for k in range(count):
            first, last = k * cols, (k + 1) * cols
            part = part_ref[k].astype(F32)
            cut = min(max(edge - first, 0), cols)
            if cut > 0:
                left_ref[:, first : first + cut] = part[:, :cut]
            if cut < cols:
                right_ref[:, first + cut - edge : last - edge] = part[:, cut:]

    return run("assemble", body, [((rows, edge), F32), ((rows, total - edge), F32)], [parts])


def local(
    item_table,
    action_table,
    item_owner,
    item_row,
    action_owner,
    action_row,
    input_norm_gain,
    w_proj,
    w_out,
    cotangent,
):
    grid = Grid()
    rows, width = item_table.shape
    replicas, line, cores = grid.replicas, grid.line, grid.cores
    cols = width // replicas

    def base_of(k):
        return ((grid.line_peer(k) * cores + grid.c) * rows).astype(I32)

    own = jnp.concatenate(
        [
            lax.dynamic_slice_in_dim(item_table, grid.r * cols, cols, 1),
            lax.dynamic_slice_in_dim(action_table, grid.r * cols, cols, 1),
        ],
        axis=0,
    )
    keys = make_keys(rows, item_owner, item_row, action_owner, action_row, replicas)

    held = [own] + [grid.over_line(own, k) for k in range(1, line)]
    bases = [base_of(k) for k in range(line)]
    cohorts = [grid.swap_replica(keys)]
    if cores == 2:
        cohorts.append(grid.over_pair(cohorts[0]))
    key_cols = [jnp.broadcast_to(k[..., None], (*k.shape, LANES)) for k in cohorts]

    found = ()
    for k in range(line - 1):
        found = fetch(key_cols, held[k], bases[k], found)
    found = [
        fetch(key_cols[m : m + 1], held[-1], bases[-1], found[m : m + 1])[0] for m in range(cores)
    ]
    pieces = found[0]
    for part in found[1:]:
        pieces = (pieces.astype(F32) + grid.over_pair(part).astype(F32)).astype(BF16)
    pieces = grid.swap_replica(pieces)

    layer_out, tokens, normed, dproj, gated = sequence(
        pieces, cotangent, input_norm_gain.reshape(1, width), w_proj, w_out
    )
    tokens = grid.swap_replica(tokens)

    def weights_of(m, before=()):
        parity = ((grid.c + m) % cores).astype(I32)
        return weight_grad(
            parity, normed, dproj, gated, cotangent, cores, line, replicas, before
        )

    parts = weights_of(0, [grid.over_pair(weights_of(m)) for m in range(1, cores)])
    parts = grid.swap_replica(parts)
    parts = add_up(parts, 1).reshape(line, width // grid.shards, parts.shape[-1])
    parts = grid.swap_line(parts)
    parts = grid.swap_replica(add_up(parts, replicas))
    grad_proj, grad_out = assemble(parts, 4 * width)

    tokens = [tokens] + [grid.over_pair(tokens)] * (cores - 1)
    table_grad = None
    for k in range(line - 1, -1, -1):
        total = ()
        for key, token in zip(cohorts, tokens):
            total = [gather_grad(key, token, bases[k], rows, total)]
        total = (grid.over_line(total[0], k) if k else total[0]).astype(F32)
        table_grad = total if table_grad is None else table_grad + total

    return layer_out, table_grad[:rows], table_grad[rows:], grad_proj, grad_out


def solution(mesh):
    tokens = ("replica", "sparse")
    in_specs = (
        P("sparse", None),
        P("sparse", None),
        P(tokens, None),
        P(tokens),
        P(tokens, None),
        P(tokens),
        P(),
        P(),
        P(),
        P(tokens, None),
    )
    out_specs = (
        P(tokens, None),
        P("sparse", "replica"),
        P("sparse", "replica"),
        P("sparse", None),
        P("sparse", None),
    )
    return jax.shard_map(local, mesh=mesh, in_specs=in_specs, out_specs=out_specs, check_vma=False)
```

```python
import jax
import jax.numpy as jnp
from jax import lax
from jax.experimental import pallas as pl
from jax.experimental.pallas import tpu as pltpu
from jax.sharding import PartitionSpec as P

HEADS = 4
EPS = 1e-05
LANES = 128
F32 = jnp.float32
BF16 = jnp.bfloat16
I32 = jnp.int32
VMEM_BYTES = 32 * 1024 * 1024

NN = ((1,), (0,))
NT = ((1,), (1,))
TN = ((0,), (0,))


def dot(left, right, dims=NN):
    return lax.dot_general(left, right, (dims, ((), ())), preferred_element_type=F32)


def sigmoid(value):
    return 0.5 * jnp.tanh(0.5 * value) + 0.5


def run(name, body, outs, args, smem=0, hbm=0, scratch=()):
    outs = [jax.ShapeDtypeStruct(shape, dtype) for shape, dtype in outs]
    in_smem = pl.BlockSpec(memory_space=pltpu.SMEM)
    in_hbm = pl.BlockSpec(memory_space=pltpu.HBM)
    in_vmem = pl.BlockSpec(memory_space=pltpu.VMEM)
    places = [in_smem] * smem + [in_hbm] * hbm + [in_vmem] * (len(args) - smem - hbm)
    results = pl.pallas_call(
        body,
        out_shape=outs,
        in_specs=places,
        out_specs=[in_vmem] * len(outs),
        scratch_shapes=list(scratch),
        compiler_params=pltpu.CompilerParams(vmem_limit_bytes=VMEM_BYTES),
        cost_estimate=pl.CostEstimate(flops=0, bytes_accessed=0, transcendentals=0),
        name=name,
    )(*args)
    return list(results)


class Grid:
    def __init__(self):
        self.replicas = lax.axis_size("replica")
        self.shards = lax.axis_size("sparse")
        self.cores = 2 if self.shards % 2 == 0 else 1
        self.line = self.shards // self.cores
        self.r = lax.axis_index("replica")
        self.s = lax.axis_index("sparse")
        self.z = self.s // self.cores
        self.c = self.s % self.cores

    def peer(self, index, size, step):
        if size & (size - 1) == 0:
            return index ^ step
        return (step - index) % size

    def over_replica(self, value, step):
        n = self.replicas
        return lax.ppermute(value, "replica", [(i, self.peer(i, n, step)) for i in range(n)])

    def swap_replica(self, value):
        return lax.all_to_all(value, "replica", split_axis=0, concat_axis=0, tiled=True)

    def swap_line(self, value):
        groups = [list(range(c, self.shards, self.cores)) for c in range(self.cores)]
        return lax.all_to_all(
            value, "sparse", split_axis=0, concat_axis=0, axis_index_groups=groups, tiled=True
        )

    def over_line(self, value, step):
        n, c = self.line, self.cores
        pairs = [(i, self.peer(i // c, n, step) * c + i % c) for i in range(n * c)]
        return lax.ppermute(value, "sparse", pairs)

    def over_pair(self, value):
        return lax.ppermute(value, "sparse", [(i, i ^ 1) for i in range(self.shards)])

    def replica_peer(self, step):
        return self.peer(self.r, self.replicas, step)

    def line_peer(self, step):
        return self.peer(self.z, self.line, step)


def make_keys(rows, item_owner, item_row, action_owner, action_row, copies):
    length = item_row.shape[0]

    def body(*refs):
        in_refs, out_ref, held, sems = refs[:4], refs[4], refs[5:9], refs[9]
        moves = [pltpu.make_async_copy(in_refs[i], held[i], sems.at[i]) for i in range(4)]
        for move in moves:
            move.start()
        for move in moves:
            move.wait()
        for table in range(2):
            number = held[2 * table][...] * rows + held[2 * table + 1][...]
            for k in range(copies):
                out_ref[k, table : table + 1, :] = number

    args = [a.reshape(1, length) for a in (item_owner, item_row, action_owner, action_row)]
    scratch = [pltpu.VMEM((1, length), I32)] * 4 + [pltpu.SemaphoreType.DMA((4,))]
    return run("make_keys", body, [((copies, 2, length), I32)], args, hbm=4, scratch=scratch)[0]


def fetch(cohorts, chunk, base, blocks, before=()):
    many = len(cohorts)
    count, _, tokens, _ = cohorts[0].shape
    rows, cols = chunk.shape[0] // 2, chunk.shape[1]

    def body(base_ref, block_ref, chunk_ref, *refs):
        key_refs, before_refs, out_refs = refs[:many], refs[many:-many], refs[-many:]
        lane = lax.broadcasted_iota(I32, (tokens, LANES), 1)
        for m in range(many):
            for k in range(count):
                hot = []
                for table in range(2):
                    place = key_refs[m][block_ref[k], table] - base_ref[0]
                    for start in range(0, rows, LANES):
                        hot.append(jnp.where(place == lane + start, 1.0, 0.0).astype(BF16))
                found = dot(jnp.concatenate(hot, axis=1), chunk_ref[...])
                if before_refs:
                    found = found + before_refs[m][k].astype(F32)
                out_refs[m][k] = found.astype(BF16)

    return run(
        "fetch",
        body,
        [((count, tokens, cols), BF16)] * many,
        [base.reshape(1), blocks, chunk, *cohorts, *before],
        smem=2,
    )


def combine(parts):
    count, *shape = parts[0].shape

    def body(left_ref, right_ref, *out_refs):
        for k in range(count):
            total = left_ref[k].astype(F32) + right_ref[k].astype(F32)
            out_refs[k][...] = total.astype(BF16)

    return run("combine", body, [(tuple(shape), BF16)] * count, parts)


def gather_grad(cohorts, tokens, base, blocks, rows, before=(), out=BF16):
    many = len(cohorts)
    count, _, length = cohorts[0].shape
    cols = tokens[0].shape[-1]

    def body(base_ref, block_ref, *refs):
        key_refs, piece_refs = refs[:many], refs[many : 2 * many]
        *before_refs, out_ref = refs[2 * many :]
        row = lax.broadcasted_iota(I32, (rows, length), 0)
        for table in range(2):
            span = slice(table * rows, (table + 1) * rows)
            sums = None
            for m in range(many):
                hot = []
                for k in range(count):
                    place = key_refs[m][block_ref[k], table : table + 1, :] - base_ref[0]
                    hot.append(jnp.where(place == row, 1.0, 0.0).astype(BF16))
                piece = piece_refs[m][...].reshape(count * length, cols)
                part = dot(jnp.concatenate(hot, axis=1), piece)
                sums = part if sums is None else sums + part
            for ref in before_refs:
                sums = sums + ref[span, :].astype(F32)
            out_ref[span, :] = sums.astype(out)

    return run(
        "gather_grad",
        body,
        [((2 * rows, cols), out)],
        [base.reshape(1), blocks, *cohorts, *tokens, *before],
        smem=2,
    )[0]


def sequence(blocks, pieces, cotangent, gain, w_proj, w_out):
    count = len(pieces)
    length, width = cotangent.shape
    cols = width // count
    head_dim = width // HEADS
    factor = head_dim ** (-0.5)
    tile = min(256, length)
    step = min(256, 4 * width)

    def body(block_ref, cot_in, wo_in, wp_in, gain_ref, *refs):
        piece_refs, refs = refs[:count], refs[count:]
        out_ref, *grad_refs = refs[: count + 1]
        normed_ref, dproj_ref, gated_ref = refs[count + 1 : count + 4]
        emb, act, slope, att, attn, dscale, dkey, dval, tok = refs[count + 4 : count + 13]
        cot_ref, wo_ref, wp_ref, sems = refs[count + 13 :]
        pairs = ((wp_in, wp_ref), (wo_in, wo_ref), (cot_in, cot_ref))
        moves = [pltpu.make_async_copy(*pair, sems.at[i]) for i, pair in enumerate(pairs)]
        for move in moves:
            move.start()

        def block(k):
            return pl.ds(pl.multiple_of(block_ref[k] * cols, cols), cols)

        for k in range(count):
            emb[:, block(k)] = piece_refs[k][...]

        def norm_of(value):
            centred = value - jnp.mean(value, axis=-1, keepdims=True)
            scale = lax.rsqrt(jnp.mean(centred * centred, axis=-1, keepdims=True) + EPS)
            return centred * scale, scale

        def norm_back(upper, hat, scale):
            return scale * (
                upper
                - jnp.mean(upper, axis=-1, keepdims=True)
                - hat * jnp.mean(upper * hat, axis=-1, keepdims=True)
            )

        for at in range(0, length, tile):
            span = slice(at, at + tile)
            hat, _ = norm_of(emb[span, :].astype(F32))
            normed_ref[span, :] = (hat * gain_ref[...]).astype(BF16)

        normed = normed_ref[...]
        for move in moves:
            move.wait()

        @pl.loop(0, 4 * width // step)
        def _(j):
            span = pl.ds(pl.multiple_of(j * step, step), step)
            proj = dot(normed, wp_ref[:, span])
            sig = sigmoid(proj)
            act[:, span] = (proj * sig).astype(BF16)
            slope[:, span] = sig * (1.0 + proj * (1.0 - sig))

        dkey[...] = jnp.zeros_like(dkey)
        dval[...] = jnp.zeros_like(dval)

        for at in range(0, length, tile):
            span = slice(at, at + tile)
            seen = at + tile
            past = slice(0, seen)
            keep = lax.broadcasted_iota(I32, (tile, seen), 1) <= at + lax.broadcasted_iota(
                I32, (tile, seen), 0
            )
            for h in range(HEADS):
                head = [slice(p * width + h * head_dim, p * width + (h + 1) * head_dim) for p in range(4)]
                scores = dot(act[span, head[2]], act[past, head[3]], NT) * factor
                sig = sigmoid(scores)
                soft = jnp.where(keep, scores * sig * (1.0 / length), 0.0).astype(BF16)
                attn[h, :, :seen] = soft
                grad = sig * (1.0 + scores * (1.0 - sig)) * (factor / length)
                dscale[h, :, :seen] = jnp.where(keep, grad, 0.0)
                att[:, head[0]] = dot(soft, act[past, head[1]])
            hat, scale = norm_of(att[...])
            gate = act[span, :width].astype(F32)
            gated = (hat * gate).astype(BF16)
            gated_ref[span, :] = gated
            out_ref[span, :] = (emb[span, :].astype(F32) + dot(gated, wo_ref[...])).astype(BF16)
            dgated = dot(cot_ref[span, :], wo_ref[...], NT)
            dproj_ref[span, :width] = (dgated * hat * slope[span, :width]).astype(BF16)
            datt = norm_back(dgated * gate, hat, scale).astype(BF16)
            for h in range(HEADS):
                head = [slice(p * width + h * head_dim, p * width + (h + 1) * head_dim) for p in range(4)]
                dhead = datt[:, head[0]]
                dattn = dot(dhead, act[past, head[1]], NT)
                dscores = (dattn * dscale[h, :, :seen]).astype(BF16)
                dquery = dot(dscores, act[past, head[3]])
                dproj_ref[span, head[2]] = (dquery * slope[span, head[2]]).astype(BF16)
                dkey[past, head[0]] += dot(dscores, act[span, head[2]], TN)
                dval[past, head[0]] += dot(attn[h, :, :seen], dhead, TN)

        dproj_ref[:, width : 2 * width] = (dval[...] * slope[:, width : 2 * width]).astype(BF16)
        dproj_ref[:, 3 * width :] = (dkey[...] * slope[:, 3 * width :]).astype(BF16)

        for at in range(0, length, tile):
            span = slice(at, at + tile)
            hat, scale = norm_of(emb[span, :].astype(F32))
            upper = dot(dproj_ref[span, :], wp_ref[...], NT) * gain_ref[...]
            grad = cot_ref[span, :].astype(F32) + norm_back(upper, hat, scale)
            tok[span, :] = grad.astype(BF16)

        for k in range(count):
            grad_refs[k][...] = tok[:, block(k)]

    return run(
        "sequence",
        body,
        [
            ((length, width), BF16),
            *[((length, cols), BF16)] * count,
            ((length, width), BF16),
            ((length, 4 * width), BF16),
            ((length, width), BF16),
        ],
        [blocks, cotangent, w_out, w_proj, gain, *pieces],
        smem=1,
        hbm=3,
        scratch=[
            pltpu.VMEM((length, width), BF16),
            pltpu.VMEM((length, 4 * width), BF16),
            pltpu.VMEM((length, 4 * width), F32),
            pltpu.VMEM((tile, width), F32),
            pltpu.VMEM((HEADS, tile, length), BF16),
            pltpu.VMEM((HEADS, tile, length), F32),
            pltpu.VMEM((length, width), F32),
            pltpu.VMEM((length, width), F32),
            pltpu.VMEM((length, width), BF16),
            pltpu.VMEM((length, width), BF16),
            pltpu.VMEM((width, width), BF16),
            pltpu.VMEM((width, 4 * width), BF16),
            pltpu.SemaphoreType.DMA((3,)),
        ],
    )


def weight_grad(place, normed, dproj, gated, cotangent, cores, line, blocks, before=()):
    length, width = normed.shape
    rows = width // (cores * line)
    half = width // cores
    edge = dproj.shape[1]
    total = edge + cotangent.shape[1]
    cols = total // blocks
    bits = blocks.bit_length() - 1
    tall = half // bits

    def body(place_ref, n_ref, d_ref, g_ref, c_ref, *refs):
        before_refs, out_refs, scratch = refs[: len(before)], refs[len(before) : -1], refs[-1]
        feature = lax.broadcasted_iota(I32, (width, half), 0)
        column = lax.broadcasted_iota(I32, (width, half), 1)
        wanted = (column // rows * cores + place_ref[0]) * rows + column % rows
        pick = jnp.where(feature == wanted, 1.0, 0.0).astype(BF16)
        n_part = dot(n_ref[...], pick).astype(BF16)
        g_part = dot(g_ref[...], pick).astype(BF16)
        for k in range(blocks):
            first, last = k * cols, (k + 1) * cols
            parts = []
            if first < edge:
                parts.append(dot(n_part, d_ref[:, first : min(last, edge)], TN))
            if last > edge:
                parts.append(dot(g_part, c_ref[:, max(first, edge) - edge : last - edge], TN))
            sums = parts[0] if len(parts) == 1 else jnp.concatenate(parts, axis=1)
            if not before:
                out_refs[0][k] = sums.astype(BF16)
                continue
            sums = sums + before_refs[0][k].astype(F32)
            for p in range(bits):
                at = sum((k >> (p + i) % bits & 1) << bits - 1 - i for i in range(bits))
                scratch[p, at] = sums[p * tall : (p + 1) * tall]
        if before:
            for p in range(bits):
                split_halves(scratch.at[p], place_ref[1 + p], out_refs[2 * p : 2 * p + 2])

    outs = [((blocks, half, cols), BF16)]
    if before:
        kept = (blocks // 2, tall, cols)
        outs = [(kept, F32), (kept, BF16)] * bits
    return run(
        "weight_grad",
        body,
        outs,
        [place, normed, dproj, gated, cotangent, *before],
        smem=1,
        scratch=[pltpu.VMEM((bits, blocks, tall, cols), F32)],
    )


def split_halves(ref, bit, out_refs):
    count = ref.shape[0] // 2
    for i, out_ref in enumerate(out_refs):
        start = (bit ^ i) * count
        for k in range(count):
            out_ref[k] = ref[start + k].astype(out_ref.dtype)


def fold(bits, kept, came):
    count, tall, cols = kept[0].shape
    many = len(kept)

    def body(bit_ref, *refs):
        kept_refs, came_refs, out_refs = refs[:many], refs[many : 2 * many], refs[2 * many : -1]
        scratch = refs[-1]
        for p in range(many):
            for k in range(count):
                scratch[p, k] = kept_refs[p][k] + came_refs[p][k].astype(F32)
            split_halves(scratch.at[p], bit_ref[p], out_refs[2 * p : 2 * p + 2])

    half = (count // 2, tall, cols)
    return run(
        "fold",
        body,
        [(half, F32), (half, BF16)] * many,
        [bits, *kept, *came],
        smem=1,
        scratch=[pltpu.VMEM((many, count, tall, cols), F32)],
    )


def cut_line(planes, kept, came):
    _, tall, cols = kept[0].shape
    many, line = len(kept), planes.shape[0]
    rows = many * tall // line

    def body(plane_ref, *refs):
        kept_refs, came_refs, out_refs = refs[:many], refs[many : 2 * many], refs[2 * many : -1]
        scratch = refs[-1]
        for p in range(many):
            scratch[p * tall : (p + 1) * tall] = kept_refs[p][0] + came_refs[p][0].astype(F32)
        for k in range(line):
            span = pl.ds(pl.multiple_of(plane_ref[k] * rows, rows), rows)
            out_refs[k][...] = scratch[span].astype(out_refs[k].dtype)

    return run(
        "cut_line",
        body,
        [((rows, cols), F32)] + [((rows, cols), BF16)] * (line - 1),
        [planes, *kept, *came],
        smem=1,
        scratch=[pltpu.VMEM((many * tall, cols), F32)],
    )


def add_up(parts):
    def body(*refs):
        total = refs[0][...].astype(F32)
        for ref in refs[1:-1]:
            total = total + ref[...].astype(F32)
        refs[-1][...] = total.astype(BF16)

    return run("add_up", body, [(parts[0].shape, BF16)], parts)[0]


def assemble(blocks, parts, edge):
    rows, cols = parts[0].shape
    total = cols * len(parts)

    def body(block_ref, *refs):
        part_refs, (left_ref, right_ref, held) = refs[: len(parts)], refs[len(parts) :]
        for k, ref in enumerate(part_refs):
            held[:, pl.ds(pl.multiple_of(block_ref[k] * cols, cols), cols)] = ref[...].astype(F32)
        left_ref[...] = held[:, :edge]
        right_ref[...] = held[:, edge:]

    return run(
        "assemble",
        body,
        [((rows, edge), F32), ((rows, total - edge), F32)],
        [blocks, *parts],
        smem=1,
        scratch=[pltpu.VMEM((rows, total), F32)],
    )


def local(
    item_table,
    action_table,
    item_owner,
    item_row,
    action_owner,
    action_row,
    input_norm_gain,
    w_proj,
    w_out,
    cotangent,
):
    grid = Grid()
    rows, width = item_table.shape
    replicas, line, cores = grid.replicas, grid.line, grid.cores
    cols = width // replicas

    def base_of(k):
        return ((grid.line_peer(k) * cores + grid.c) * rows).astype(I32)

    own = jnp.concatenate(
        [
            lax.dynamic_slice_in_dim(item_table, grid.r * cols, cols, 1),
            lax.dynamic_slice_in_dim(action_table, grid.r * cols, cols, 1),
        ],
        axis=0,
    )
    keys = make_keys(rows, item_owner, item_row, action_owner, action_row, replicas)

    held = [own] + [grid.over_line(own, k) for k in range(1, line)]
    bases = [base_of(k) for k in range(line)]
    cohorts = [grid.swap_replica(keys)]
    if cores == 2:
        cohorts.append(grid.over_pair(cohorts[0]))
    key_cols = [jnp.broadcast_to(k[..., None], (*k.shape, LANES)) for k in cohorts]

    blocks = jnp.stack([grid.replica_peer(k) for k in range(replicas)]).astype(I32)
    planes = jnp.stack([grid.line_peer(k) for k in range(line)]).astype(I32)
    bits = replicas.bit_length() - 1
    swaps = [3, 1, 2] if replicas == 4 else list(range(1, replicas))

    found = ()
    for k in range(line - 1):
        found = fetch(key_cols, held[k], bases[k], blocks, found)
    found = [
        fetch(key_cols[m : m + 1], held[-1], bases[-1], blocks, found[m : m + 1])[0]
        for m in range(cores)
    ]
    pieces = combine([found[0], grid.over_pair(found[1])])
    for k in swaps:
        pieces[k] = grid.over_replica(pieces[k], k)

    layer_out, *rest = sequence(
        blocks, pieces, cotangent, input_norm_gain.reshape(1, width), w_proj, w_out
    )
    tokens, (normed, dproj, gated) = rest[:replicas], rest[replicas:]
    for k in swaps:
        tokens[k] = grid.over_replica(tokens[k], k)

    def weights_of(m, before=()):
        place = [(grid.c + m) % cores] + [grid.r >> p & 1 for p in range(bits)]
        place = jnp.stack(place).astype(I32)
        args = (place, normed, dproj, gated, cotangent, cores, line, replicas, before)
        return weight_grad(*args)

    weights = weights_of(0, [grid.over_pair(weights_of(1)[0])])
    tokens, weights = lax.optimization_barrier((tokens, weights))
    tokens = jnp.stack(tokens)
    there = grid.over_pair(tokens)
    first = gather_grad(cohorts[:1], [tokens], bases[-1], blocks, rows)

    sums = {line - 1: gather_grad(cohorts[1:], [there], bases[-1], blocks, rows, [first])}
    for k in range(line - 2, -1, -1):
        out = BF16 if k else F32
        sums[k] = gather_grad(cohorts, [tokens, there], bases[k], blocks, rows, out=out)
    table_grad = sums[0]
    for k in range(line - 1, 0, -1):
        table_grad = table_grad + grid.over_line(sums[k], k).astype(F32)

    for step in range(bits):
        kept, sent = weights[0::2], weights[1::2]
        came = [grid.over_replica(sent[p], 1 << (p + step) % bits) for p in range(bits)]
        if step < bits - 1:
            turn = jnp.stack([grid.r >> (p + step + 1) % bits & 1 for p in range(bits)])
            weights = fold(turn.astype(I32), kept, came)
    parts = cut_line(planes, kept, came)
    parts = [parts[0]] + [grid.over_line(parts[k], k) for k in range(1, line)]
    total = add_up(parts)
    parts = [total] + [grid.over_replica(total, k) for k in range(1, replicas)]
    grad_proj, grad_out = assemble(blocks, parts, 4 * width)

    return layer_out, table_grad[:rows], table_grad[rows:], grad_proj, grad_out


def solution(mesh):
    tokens = ("replica", "sparse")
    in_specs = (
        P("sparse", None),
        P("sparse", None),
        P(tokens, None),
        P(tokens),
        P(tokens, None),
        P(tokens),
        P(),
        P(),
        P(),
        P(tokens, None),
    )
    out_specs = (
        P(tokens, None),
        P("sparse", "replica"),
        P("sparse", "replica"),
        P("sparse", None),
        P("sparse", None),
    )
    return jax.shard_map(local, mesh=mesh, in_specs=in_specs, out_specs=out_specs, check_vma=False)
```

```python
import jax
import jax.numpy as jnp
from jax import lax
from jax.experimental import pallas as pl
from jax.experimental.pallas import tpu as pltpu
from jax.sharding import PartitionSpec as P

HEADS = 4
EPS = 1e-05
LANES = 128
F32 = jnp.float32
BF16 = jnp.bfloat16
I32 = jnp.int32
MIB = 1024 * 1024

NN = ((1,), (0,))
NT = ((1,), (1,))
TN = ((0,), (0,))


def dot(left, right, dims=NN):
    return lax.dot_general(left, right, (dims, ((), ())), preferred_element_type=F32)


def sigmoid(value):
    return 0.5 * jnp.tanh(0.5 * value) + 0.5


def run(name, body, outs, args, smem=0, scratch=(), vmem=16):
    outs = [jax.ShapeDtypeStruct(shape, dtype) for shape, dtype in outs]
    in_smem = pl.BlockSpec(memory_space=pltpu.SMEM)
    in_vmem = pl.BlockSpec(memory_space=pltpu.VMEM)
    places = [in_smem] * smem + [in_vmem] * (len(args) - smem)
    results = pl.pallas_call(
        body,
        out_shape=outs,
        in_specs=places,
        out_specs=[in_vmem] * len(outs),
        scratch_shapes=list(scratch),
        compiler_params=pltpu.CompilerParams(vmem_limit_bytes=vmem * MIB),
        cost_estimate=pl.CostEstimate(flops=0, bytes_accessed=0, transcendentals=0),
        name=name,
    )(*args)
    return list(results)


class Grid:
    def __init__(self):
        self.replicas = lax.axis_size("replica")
        self.shards = lax.axis_size("sparse")
        self.cores = 2 if self.shards % 2 == 0 else 1
        self.line = self.shards // self.cores
        self.r = lax.axis_index("replica")
        self.s = lax.axis_index("sparse")
        self.z = self.s // self.cores
        self.c = self.s % self.cores

    def over_replica(self, value, step):
        n = self.replicas
        return lax.ppermute(value, "replica", [(i, i ^ step) for i in range(n)])

    def over_line(self, value, step):
        pairs = [(i, i ^ step * self.cores) for i in range(self.shards)]
        return lax.ppermute(value, "sparse", pairs)

    def over_pair(self, value):
        return lax.ppermute(value, "sparse", [(i, i ^ 1) for i in range(self.shards)])


def fetch(keys, cohorts, chunk, base, before=()):
    many = len(cohorts)
    count, _, _, tokens, _ = keys.shape
    rows, cols = chunk.shape[0] // 2, chunk.shape[1]

    def body(base_ref, chunk_ref, key_ref, *refs):
        before_refs, out_refs = refs[:-many], refs[-many:]
        lane = lax.broadcasted_iota(I32, (tokens, LANES), 1)
        for i, m in enumerate(cohorts):
            for k in range(count):
                hot = []
                for table in range(2):
                    place = key_ref[k, m, table] - base_ref[0]
                    for start in range(0, rows, LANES):
                        hot.append(jnp.where(place == lane + start, 1.0, 0.0).astype(BF16))
                found = dot(jnp.concatenate(hot, axis=1), chunk_ref[...])
                if before_refs:
                    found = found + before_refs[i][k].astype(F32)
                out_refs[i][k] = found.astype(BF16)

    return run(
        "fetch",
        body,
        [((count, tokens, cols), BF16)] * many,
        [base.reshape(1), chunk, keys, *before],
        smem=1,
    )


def combine(parts):
    count, *shape = parts[0].shape

    def body(left_ref, right_ref, *out_refs):
        for k in range(count):
            total = left_ref[k].astype(F32) + right_ref[k].astype(F32)
            out_refs[k][...] = total.astype(BF16)

    return run("combine", body, [(tuple(shape), BF16)] * count, parts)


def gather_grad(keys, cohorts, tokens, base, rows, before=(), out=BF16):
    many = len(cohorts)
    count, _, _, length = keys.shape
    cols = tokens[0].shape[-1]

    def body(base_ref, key_ref, *refs):
        piece_refs, before_refs, out_ref = refs[:many], refs[many:-1], refs[-1]
        row = lax.broadcasted_iota(I32, (rows, length), 0)
        for table in range(2):
            span = slice(table * rows, (table + 1) * rows)
            sums = None
            for i, m in enumerate(cohorts):
                hot = []
                for k in range(count):
                    place = key_ref[k, m, table : table + 1, :] - base_ref[0]
                    hot.append(jnp.where(place == row, 1.0, 0.0).astype(BF16))
                piece = piece_refs[i][...].reshape(count * length, cols)
                part = dot(jnp.concatenate(hot, axis=1), piece)
                sums = part if sums is None else sums + part
            for ref in before_refs:
                sums = sums + ref[span, :].astype(F32)
            out_ref[span, :] = sums.astype(out)

    return run(
        "gather_grad",
        body,
        [((2 * rows, cols), out)],
        [base.reshape(1), keys, *tokens, *before],
        smem=1,
    )[0]


def sequence(blocks, pieces, cotangent, gain, w_proj, w_out):
    count = len(pieces)
    length, width = cotangent.shape
    cols = width // count
    head_dim = width // HEADS
    factor = head_dim ** (-0.5)
    tile = min(256, length)
    step = min(256, 4 * width)

    def body(block_ref, cot_ref, wo_ref, wp_ref, gain_ref, *refs):
        piece_refs, refs = refs[:count], refs[count:]
        out_ref, *grad_refs = refs[: count + 1]
        normed_ref, dproj_ref, gated_ref = refs[count + 1 : count + 4]
        emb, act, slope, att, attn, dscale, dkey, dval, tok = refs[count + 4 :]

        def block(k):
            return pl.ds(pl.multiple_of(block_ref[k] * cols, cols), cols)

        for k in range(count):
            emb[:, block(k)] = piece_refs[k][...]

        def norm_of(value):
            centred = value - jnp.mean(value, axis=-1, keepdims=True)
            scale = lax.rsqrt(jnp.mean(centred * centred, axis=-1, keepdims=True) + EPS)
            return centred * scale, scale

        def norm_back(upper, hat, scale):
            return scale * (
                upper
                - jnp.mean(upper, axis=-1, keepdims=True)
                - hat * jnp.mean(upper * hat, axis=-1, keepdims=True)
            )

        for at in range(0, length, tile):
            span = slice(at, at + tile)
            hat, _ = norm_of(emb[span, :].astype(F32))
            normed_ref[span, :] = (hat * gain_ref[...]).astype(BF16)

        normed = normed_ref[...]

        @pl.loop(0, 4 * width // step)
        def _(j):
            span = pl.ds(pl.multiple_of(j * step, step), step)
            proj = dot(normed, wp_ref[:, span])
            sig = sigmoid(proj)
            act[:, span] = (proj * sig).astype(BF16)
            slope[:, span] = sig * (1.0 + proj * (1.0 - sig))

        dkey[...] = jnp.zeros_like(dkey)
        dval[...] = jnp.zeros_like(dval)

        for at in range(0, length, tile):
            span = slice(at, at + tile)
            seen = at + tile
            past = slice(0, seen)
            keep = lax.broadcasted_iota(I32, (tile, seen), 1) <= at + lax.broadcasted_iota(
                I32, (tile, seen), 0
            )
            for h in range(HEADS):
                head = [slice(p * width + h * head_dim, p * width + (h + 1) * head_dim) for p in range(4)]
                scores = dot(act[span, head[2]], act[past, head[3]], NT) * factor
                sig = sigmoid(scores)
                soft = jnp.where(keep, scores * sig * (1.0 / length), 0.0).astype(BF16)
                attn[h, :, :seen] = soft
                grad = sig * (1.0 + scores * (1.0 - sig)) * (factor / length)
                dscale[h, :, :seen] = jnp.where(keep, grad, 0.0)
                att[:, head[0]] = dot(soft, act[past, head[1]])
            hat, scale = norm_of(att[...])
            gate = act[span, :width].astype(F32)
            gated = (hat * gate).astype(BF16)
            gated_ref[span, :] = gated
            out_ref[span, :] = (emb[span, :].astype(F32) + dot(gated, wo_ref[...])).astype(BF16)
            dgated = dot(cot_ref[span, :], wo_ref[...], NT)
            dproj_ref[span, :width] = (dgated * hat * slope[span, :width]).astype(BF16)
            datt = norm_back(dgated * gate, hat, scale).astype(BF16)
            for h in range(HEADS):
                head = [slice(p * width + h * head_dim, p * width + (h + 1) * head_dim) for p in range(4)]
                dhead = datt[:, head[0]]
                dattn = dot(dhead, act[past, head[1]], NT)
                dscores = (dattn * dscale[h, :, :seen]).astype(BF16)
                dquery = dot(dscores, act[past, head[3]])
                dproj_ref[span, head[2]] = (dquery * slope[span, head[2]]).astype(BF16)
                dkey[past, head[0]] += dot(dscores, act[span, head[2]], TN)
                dval[past, head[0]] += dot(attn[h, :, :seen], dhead, TN)

        dproj_ref[:, width : 2 * width] = (dval[...] * slope[:, width : 2 * width]).astype(BF16)
        dproj_ref[:, 3 * width :] = (dkey[...] * slope[:, 3 * width :]).astype(BF16)

        for at in range(0, length, tile):
            span = slice(at, at + tile)
            hat, scale = norm_of(emb[span, :].astype(F32))
            upper = dot(dproj_ref[span, :], wp_ref[...], NT) * gain_ref[...]
            grad = cot_ref[span, :].astype(F32) + norm_back(upper, hat, scale)
            tok[span, :] = grad.astype(BF16)

        for k in range(count):
            grad_refs[k][...] = tok[:, block(k)]

    return run(
        "sequence",
        body,
        [
            ((length, width), BF16),
            *[((length, cols), BF16)] * count,
            ((length, width), BF16),
            ((length, 4 * width), BF16),
            ((length, width), BF16),
        ],
        [blocks, cotangent, w_out, w_proj, gain, *pieces],
        smem=1,
        vmem=24,
        scratch=[
            pltpu.VMEM((length, width), BF16),
            pltpu.VMEM((length, 4 * width), BF16),
            pltpu.VMEM((length, 4 * width), F32),
            pltpu.VMEM((tile, width), F32),
            pltpu.VMEM((HEADS, tile, length), BF16),
            pltpu.VMEM((HEADS, tile, length), F32),
            pltpu.VMEM((length, width), F32),
            pltpu.VMEM((length, width), F32),
            pltpu.VMEM((length, width), BF16),
        ],
    )


def weight_grad(place, normed, dproj, gated, cotangent, cores, line, blocks, before=()):
    length, width = normed.shape
    rows = width // (cores * line)
    half = width // cores
    edge = dproj.shape[1]
    total = edge + cotangent.shape[1]
    cols = total // blocks
    bits = blocks.bit_length() - 1
    tall = half // bits

    def body(place_ref, n_ref, d_ref, g_ref, c_ref, *refs):
        before_refs, out_refs, scratch = refs[: len(before)], refs[len(before) : -1], refs[-1]
        feature = lax.broadcasted_iota(I32, (width, half), 0)
        column = lax.broadcasted_iota(I32, (width, half), 1)
        wanted = (column // rows * cores + place_ref[0]) * rows + column % rows
        pick = jnp.where(feature == wanted, 1.0, 0.0).astype(BF16)
        n_part = dot(n_ref[...], pick).astype(BF16)
        g_part = dot(g_ref[...], pick).astype(BF16)
        for k in range(blocks):
            first, last = k * cols, (k + 1) * cols
            parts = []
            if first < edge:
                parts.append(dot(n_part, d_ref[:, first : min(last, edge)], TN))
            if last > edge:
                parts.append(dot(g_part, c_ref[:, max(first, edge) - edge : last - edge], TN))
            sums = parts[0] if len(parts) == 1 else jnp.concatenate(parts, axis=1)
            if not before:
                out_refs[0][k] = sums.astype(BF16)
                continue
            sums = sums + before_refs[0][k].astype(F32)
            for p in range(bits):
                at = sum((k >> (p + i) % bits & 1) << bits - 1 - i for i in range(bits))
                scratch[p, at] = sums[p * tall : (p + 1) * tall]
        if before:
            for p in range(bits):
                split_halves(scratch.at[p], place_ref[1 + p], out_refs[2 * p : 2 * p + 2])

    outs = [((blocks, half, cols), BF16)]
    if before:
        kept = (blocks // 2, tall, cols)
        outs = [(kept, F32), (kept, BF16)] * bits
    return run(
        "weight_grad",
        body,
        outs,
        [place, normed, dproj, gated, cotangent, *before],
        smem=1,
        scratch=[pltpu.VMEM((bits, blocks, tall, cols), F32)],
    )


def split_halves(ref, bit, out_refs):
    count = ref.shape[0] // 2
    for i, out_ref in enumerate(out_refs):
        start = (bit ^ i) * count
        for k in range(count):
            out_ref[k] = ref[start + k].astype(out_ref.dtype)


def fold(bits, kept, came):
    count, tall, cols = kept[0].shape
    many = len(kept)

    def body(bit_ref, *refs):
        kept_refs, came_refs, out_refs = refs[:many], refs[many : 2 * many], refs[2 * many : -1]
        scratch = refs[-1]
        for p in range(many):
            for k in range(count):
                scratch[p, k] = kept_refs[p][k] + came_refs[p][k].astype(F32)
            split_halves(scratch.at[p], bit_ref[p], out_refs[2 * p : 2 * p + 2])

    half = (count // 2, tall, cols)
    return run(
        "fold",
        body,
        [(half, F32), (half, BF16)] * many,
        [bits, *kept, *came],
        smem=1,
        scratch=[pltpu.VMEM((many, count, tall, cols), F32)],
    )


def cut_line(planes, kept, came):
    _, tall, cols = kept[0].shape
    many, line = len(kept), planes.shape[0]
    rows = many * tall // line

    def body(plane_ref, *refs):
        kept_refs, came_refs, out_refs = refs[:many], refs[many : 2 * many], refs[2 * many : -1]
        scratch = refs[-1]
        for p in range(many):
            scratch[p * tall : (p + 1) * tall] = kept_refs[p][0] + came_refs[p][0].astype(F32)
        for k in range(line):
            span = pl.ds(pl.multiple_of(plane_ref[k] * rows, rows), rows)
            out_refs[k][...] = scratch[span].astype(out_refs[k].dtype)

    return run(
        "cut_line",
        body,
        [((rows, cols), F32)] + [((rows, cols), BF16)] * (line - 1),
        [planes, *kept, *came],
        smem=1,
        scratch=[pltpu.VMEM((many * tall, cols), F32)],
    )


def add_up(parts):
    def body(*refs):
        total = refs[0][...].astype(F32)
        for ref in refs[1:-1]:
            total = total + ref[...].astype(F32)
        refs[-1][...] = total.astype(BF16)

    return run("add_up", body, [(parts[0].shape, BF16)], parts)[0]


def assemble(blocks, parts, edge):
    rows, cols = parts[0].shape
    total = cols * len(parts)

    def body(block_ref, *refs):
        part_refs, (left_ref, right_ref, held) = refs[: len(parts)], refs[len(parts) :]
        for k, ref in enumerate(part_refs):
            held[:, pl.ds(pl.multiple_of(block_ref[k] * cols, cols), cols)] = ref[...].astype(F32)
        left_ref[...] = held[:, :edge]
        right_ref[...] = held[:, edge:]

    return run(
        "assemble",
        body,
        [((rows, edge), F32), ((rows, total - edge), F32)],
        [blocks, *parts],
        smem=1,
        scratch=[pltpu.VMEM((rows, total), F32)],
    )


def local(
    item_table,
    action_table,
    item_owner,
    item_row,
    action_owner,
    action_row,
    input_norm_gain,
    w_proj,
    w_out,
    cotangent,
):
    grid = Grid()
    rows, width = item_table.shape
    replicas, line, cores = grid.replicas, grid.line, grid.cores
    cols = width // replicas

    bits = replicas.bit_length() - 1
    swaps = [3, 1, 2] if replicas == 4 else list(range(1, replicas))
    blocks = jnp.stack([grid.r ^ k for k in range(replicas)]).astype(I32)
    planes = jnp.stack([grid.z ^ k for k in range(line)]).astype(I32)
    bases = [(((grid.z ^ k) * cores + grid.c) * rows).astype(I32) for k in range(line)]

    own = jnp.concatenate(
        [
            lax.dynamic_slice_in_dim(item_table, grid.r * cols, cols, 1),
            lax.dynamic_slice_in_dim(action_table, grid.r * cols, cols, 1),
        ],
        axis=0,
    )
    keys = jnp.stack(
        [
            (item_owner * rows + item_row[:, None])[:, 0],
            (action_owner * rows + action_row[:, None])[:, 0],
        ]
    ).astype(I32)

    held = {0: own}
    for low in reversed([1 << i for i in range(line.bit_length() - 1)]):
        for k in range(low, line, 2 * low):
            held[k] = grid.over_line(held[k ^ low], low)
    order = sorted(held, key=lambda k: (bin(k).count("1"), k))

    keys = jnp.stack([keys, grid.over_pair(keys)])
    keys = jnp.stack([keys] + [grid.over_replica(keys, k) for k in range(1, replicas)])
    key_cols = jnp.broadcast_to(keys[..., None], (*keys.shape, LANES))
    both = list(range(cores))

    found = ()
    for k in order[:-1]:
        found = fetch(key_cols, both, held[k], bases[k], found)
    last = order[-1]
    there = fetch(key_cols, both[1:], held[last], bases[last], found[1:])
    here = fetch(key_cols, both[:1], held[last], bases[last], found[:1])
    pieces = combine([here[0], grid.over_pair(there[0])])
    for k in swaps:
        pieces[k] = grid.over_replica(pieces[k], k)

    layer_out, *rest = sequence(
        blocks, pieces, cotangent, input_norm_gain.reshape(1, width), w_proj, w_out
    )
    tokens, (normed, dproj, gated) = rest[:replicas], rest[replicas:]
    for k in swaps:
        tokens[k] = grid.over_replica(tokens[k], k)

    def weights_of(m, before=()):
        place = [(grid.c + m) % cores] + [grid.r >> p & 1 for p in range(bits)]
        place = jnp.stack(place).astype(I32)
        args = (place, normed, dproj, gated, cotangent, cores, line, replicas, before)
        return weight_grad(*args)

    weights = weights_of(0, [grid.over_pair(weights_of(1)[0])])
    tokens = lax.optimization_barrier((tokens, weights))[0]
    tokens = jnp.stack(tokens)
    there = grid.over_pair(tokens)

    sums = {}
    for k in reversed(order):
        if k == last:
            first = gather_grad(keys, both[:1], [tokens], bases[k], rows)
            sums[k] = gather_grad(keys, both[1:], [there], bases[k], rows, [first])
            continue
        low = (k & -k) or line
        steps = [1 << i for i in range(low.bit_length() - 1)]
        out = F32 if steps else BF16
        total = gather_grad(keys, both, [tokens, there], bases[k], rows, out=out)
        for step in steps:
            total = total + grid.over_line(sums[k ^ step], step).astype(F32)
        sums[k] = total.astype(BF16) if k else total
    table_grad = sums[0]

    for step in range(bits):
        kept, sent = weights[0::2], weights[1::2]
        came = [grid.over_replica(sent[p], 1 << (p + step) % bits) for p in range(bits)]
        after = sums[last] if step < bits - 1 else sums[line // 2]
        came = lax.optimization_barrier((came, after))[0]
        if step < bits - 1:
            turn = jnp.stack([grid.r >> (p + step + 1) % bits & 1 for p in range(bits)])
            weights = fold(turn.astype(I32), kept, came)
    parts = cut_line(planes, kept, came)
    parts = [parts[0]] + [grid.over_line(parts[k], k) for k in range(1, line)]
    parts = lax.optimization_barrier((parts, table_grad))[0]
    total = add_up(parts)
    parts = [total] + [grid.over_replica(total, k) for k in range(1, replicas)]
    grad_proj, grad_out = assemble(blocks, parts, 4 * width)

    return layer_out, table_grad[:rows], table_grad[rows:], grad_proj, grad_out


def solution(mesh):
    tokens = ("replica", "sparse")
    in_specs = (
        P("sparse", None),
        P("sparse", None),
        P(tokens, None),
        P(tokens),
        P(tokens, None),
        P(tokens),
        P(),
        P(),
        P(),
        P(tokens, None),
    )
    out_specs = (
        P(tokens, None),
        P("sparse", "replica"),
        P("sparse", "replica"),
        P("sparse", None),
        P("sparse", None),
    )
    return jax.shard_map(local, mesh=mesh, in_specs=in_specs, out_specs=out_specs, check_vma=False)
```

```python
import jax
import jax.numpy as jnp
from jax import lax
from jax.experimental import pallas as pl
from jax.experimental.pallas import tpu as pltpu
from jax.sharding import PartitionSpec as P

HEADS = 4
EPS = 1e-05
LANES = 128
F32 = jnp.float32
BF16 = jnp.bfloat16
I32 = jnp.int32
MIB = 1024 * 1024

NN = ((1,), (0,))
NT = ((1,), (1,))
TN = ((0,), (0,))


def dot(left, right, dims=NN):
    return lax.dot_general(left, right, (dims, ((), ())), preferred_element_type=F32)


def sigmoid(value):
    return 0.5 * jnp.tanh(0.5 * value) + 0.5


def run(name, body, outs, args, smem=0, scratch=(), vmem=16, flops=0):
    outs = [jax.ShapeDtypeStruct(shape, dtype) for shape, dtype in outs]
    size = sum(a.size * a.dtype.itemsize for a in [*args, *outs])
    in_smem = pl.BlockSpec(memory_space=pltpu.SMEM)
    in_vmem = pl.BlockSpec(memory_space=pltpu.VMEM)
    places = [in_smem] * smem + [in_vmem] * (len(args) - smem)
    results = pl.pallas_call(
        body,
        out_shape=outs,
        in_specs=places,
        out_specs=[in_vmem] * len(outs),
        scratch_shapes=list(scratch),
        compiler_params=pltpu.CompilerParams(vmem_limit_bytes=vmem * MIB),
        cost_estimate=pl.CostEstimate(flops=flops, bytes_accessed=size, transcendentals=0),
        name=name,
    )(*args)
    return list(results)


class Grid:
    def __init__(self):
        self.replicas = lax.axis_size("replica")
        self.shards = lax.axis_size("sparse")
        self.cores = 2 if self.shards % 2 == 0 else 1
        self.line = self.shards // self.cores
        self.r = lax.axis_index("replica")
        self.s = lax.axis_index("sparse")
        self.z = self.s // self.cores
        self.c = self.s % self.cores

    def over_replica(self, value, step):
        n = self.replicas
        return lax.ppermute(value, "replica", [(i, i ^ step) for i in range(n)])

    def over_line(self, value, step):
        pairs = [(i, i ^ step * self.cores) for i in range(self.shards)]
        return lax.ppermute(value, "sparse", pairs)

    def over_pair(self, value):
        return lax.ppermute(value, "sparse", [(i, i ^ 1) for i in range(self.shards)])


def fetch(keys, cohorts, chunk, base, before=()):
    many = len(cohorts)
    count, _, _, tokens, _ = keys.shape
    rows, cols = chunk.shape[0] // 2, chunk.shape[1]

    def body(base_ref, chunk_ref, key_ref, *refs):
        before_refs, out_refs = refs[:-many], refs[-many:]
        lane = lax.broadcasted_iota(I32, (tokens, LANES), 1)
        for i, m in enumerate(cohorts):
            for k in range(count):
                hot = []
                for table in range(2):
                    place = key_ref[k, m, table] - base_ref[0]
                    for start in range(0, rows, LANES):
                        hot.append(jnp.where(place == lane + start, 1.0, 0.0).astype(BF16))
                found = dot(jnp.concatenate(hot, axis=1), chunk_ref[...])
                if before_refs:
                    found = found + before_refs[i][k].astype(F32)
                out_refs[i][k] = found.astype(BF16)

    return run(
        "fetch",
        body,
        [((count, tokens, cols), BF16)] * many,
        [base.reshape(1), chunk, keys, *before],
        smem=1,
        flops=2 * many * count * tokens * rows * cols,
    )


def combine(parts):
    count, *shape = parts[0].shape

    def body(left_ref, right_ref, *out_refs):
        for k in range(count):
            total = left_ref[k].astype(F32) + right_ref[k].astype(F32)
            out_refs[k][...] = total.astype(BF16)

    return run("combine", body, [(tuple(shape), BF16)] * count, parts)


def gather_grad(keys, cohorts, tokens, base, rows, before=(), out=BF16):
    many = len(cohorts)
    count, _, _, length = keys.shape
    cols = tokens[0].shape[-1]

    def body(base_ref, key_ref, *refs):
        piece_refs, before_refs, out_ref = refs[:many], refs[many:-1], refs[-1]
        row = lax.broadcasted_iota(I32, (rows, length), 0)
        for table in range(2):
            span = slice(table * rows, (table + 1) * rows)
            sums = None
            for i, m in enumerate(cohorts):
                hot = []
                for k in range(count):
                    place = key_ref[k, m, table : table + 1, :] - base_ref[0]
                    hot.append(jnp.where(place == row, 1.0, 0.0).astype(BF16))
                piece = piece_refs[i][...].reshape(count * length, cols)
                part = dot(jnp.concatenate(hot, axis=1), piece)
                sums = part if sums is None else sums + part
            for ref in before_refs:
                sums = sums + ref[span, :].astype(F32)
            out_ref[span, :] = sums.astype(out)

    return run(
        "gather_grad",
        body,
        [((2 * rows, cols), out)],
        [base.reshape(1), keys, *tokens, *before],
        smem=1,
        flops=4 * many * count * length * 2 * rows * cols,
    )[0]


def sequence(blocks, other, pieces, cotangent, gain, w_proj, w_out, cores, line):
    count = len(pieces)
    length, width = cotangent.shape
    cols = width // count
    head_dim = width // HEADS
    factor = head_dim ** (-0.5)
    tile = min(256, length)
    step = min(256, 4 * width)

    def body(block_ref, other_ref, cot_ref, wo_ref, wp_ref, gain_ref, *refs):
        piece_refs, refs = refs[:count], refs[count:]
        out_ref, *grad_refs = refs[: count + 1]
        normed_ref, dproj_ref, gated_ref, weight_ref = refs[count + 1 : count + 5]
        emb, act, slope, att, attn, dscale, dkey, dval, tok = refs[count + 5 :]

        for k in range(count):
            emb[block_ref[k]] = piece_refs[k][...]

        def embedded(span):
            return jnp.concatenate([emb[k, span] for k in range(count)], axis=1).astype(F32)

        def norm_of(value):
            centred = value - jnp.mean(value, axis=-1, keepdims=True)
            scale = lax.rsqrt(jnp.mean(centred * centred, axis=-1, keepdims=True) + EPS)
            return centred * scale, scale

        def norm_back(upper, hat, scale):
            return scale * (
                upper
                - jnp.mean(upper, axis=-1, keepdims=True)
                - hat * jnp.mean(upper * hat, axis=-1, keepdims=True)
            )

        for at in range(0, length, tile):
            span = slice(at, at + tile)
            hat, _ = norm_of(embedded(span))
            normed_ref[span, :] = (hat * gain_ref[...]).astype(BF16)

        normed = normed_ref[...]

        @pl.loop(0, 4 * width // step)
        def _(j):
            span = pl.ds(pl.multiple_of(j * step, step), step)
            proj = dot(normed, wp_ref[:, span])
            sig = sigmoid(proj)
            act[:, span] = (proj * sig).astype(BF16)
            slope[:, span] = sig * (1.0 + proj * (1.0 - sig))

        dkey[...] = jnp.zeros_like(dkey)
        dval[...] = jnp.zeros_like(dval)

        for at in range(0, length, tile):
            span = slice(at, at + tile)
            seen = at + tile
            past = slice(0, seen)
            keep = lax.broadcasted_iota(I32, (tile, seen), 1) <= at + lax.broadcasted_iota(
                I32, (tile, seen), 0
            )
            for h in range(HEADS):
                head = [slice(p * width + h * head_dim, p * width + (h + 1) * head_dim) for p in range(4)]
                scores = dot(act[span, head[2]], act[past, head[3]], NT) * factor
                sig = sigmoid(scores)
                soft = jnp.where(keep, scores * sig * (1.0 / length), 0.0).astype(BF16)
                attn[h, :, :seen] = soft
                grad = sig * (1.0 + scores * (1.0 - sig)) * (factor / length)
                dscale[h, :, :seen] = jnp.where(keep, grad, 0.0)
                att[:, head[0]] = dot(soft, act[past, head[1]])
            hat, scale = norm_of(att[...])
            gate = act[span, :width].astype(F32)
            gated = (hat * gate).astype(BF16)
            gated_ref[span, :] = gated
            out_ref[span, :] = (embedded(span) + dot(gated, wo_ref[...])).astype(BF16)
            dgated = dot(cot_ref[span, :], wo_ref[...], NT)
            dproj_ref[span, :width] = (dgated * hat * slope[span, :width]).astype(BF16)
            datt = norm_back(dgated * gate, hat, scale).astype(BF16)
            for h in range(HEADS):
                head = [slice(p * width + h * head_dim, p * width + (h + 1) * head_dim) for p in range(4)]
                dhead = datt[:, head[0]]
                dattn = dot(dhead, act[past, head[1]], NT)
                dscores = (dattn * dscale[h, :, :seen]).astype(BF16)
                dquery = dot(dscores, act[past, head[3]])
                dproj_ref[span, head[2]] = (dquery * slope[span, head[2]]).astype(BF16)
                dkey[past, head[0]] += dot(dscores, act[span, head[2]], TN)
                dval[past, head[0]] += dot(attn[h, :, :seen], dhead, TN)

        dproj_ref[:, width : 2 * width] = (dval[...] * slope[:, width : 2 * width]).astype(BF16)
        dproj_ref[:, 3 * width :] = (dkey[...] * slope[:, 3 * width :]).astype(BF16)

        for at in range(0, length, tile):
            span = slice(at, at + tile)
            hat, scale = norm_of(embedded(span))
            upper = dot(dproj_ref[span, :], wp_ref[...], NT) * gain_ref[...]
            grad = cot_ref[span, :].astype(F32) + norm_back(upper, hat, scale)
            for k in range(count):
                tok[k, span] = grad[:, k * cols : (k + 1) * cols].astype(BF16)

        for k in range(count):
            grad_refs[k][...] = tok[block_ref[k]]

        sums = weight_sums(other_ref[0], normed_ref, dproj_ref, gated_ref, cot_ref, cores, line, count)
        for k in range(count):
            weight_ref[k] = next(sums).astype(BF16)

    return run(
        "sequence",
        body,
        [
            ((length, width), BF16),
            *[((length, cols), BF16)] * count,
            ((length, width), BF16),
            ((length, 4 * width), BF16),
            ((length, width), BF16),
            ((count, width // cores, 5 * width // count), BF16),
        ],
        [blocks, other, cotangent, w_out, w_proj, gain, *pieces],
        smem=2,
        vmem=24,
        flops=32 * length * width * width,
        scratch=[
            pltpu.VMEM((count, length, cols), BF16),
            pltpu.VMEM((length, 4 * width), BF16),
            pltpu.VMEM((length, 4 * width), F32),
            pltpu.VMEM((tile, width), F32),
            pltpu.VMEM((HEADS, tile, length), BF16),
            pltpu.VMEM((HEADS, tile, length), F32),
            pltpu.VMEM((length, width), F32),
            pltpu.VMEM((length, width), F32),
            pltpu.VMEM((count, length, cols), BF16),
        ],
    )


def weight_sums(core, n_ref, d_ref, g_ref, c_ref, cores, line, blocks):
    length, width = n_ref.shape
    rows = width // (cores * line)
    half = width // cores
    edge = d_ref.shape[1]
    cols = (edge + c_ref.shape[1]) // blocks
    feature = lax.broadcasted_iota(I32, (width, half), 0)
    column = lax.broadcasted_iota(I32, (width, half), 1)
    wanted = (column // rows * cores + core) * rows + column % rows
    pick = jnp.where(feature == wanted, 1.0, 0.0).astype(BF16)
    n_part = dot(n_ref[...], pick).astype(BF16)
    g_part = dot(g_ref[...], pick).astype(BF16)
    for k in range(blocks):
        first, last = k * cols, (k + 1) * cols
        parts = []
        if first < edge:
            parts.append(dot(n_part, d_ref[:, first : min(last, edge)], TN))
        if last > edge:
            parts.append(dot(g_part, c_ref[:, max(first, edge) - edge : last - edge], TN))
        yield parts[0] if len(parts) == 1 else jnp.concatenate(parts, axis=1)


def weight_grad(place, normed, dproj, gated, cotangent, before, line):
    blocks, half, cols = before.shape
    length, width = normed.shape
    cores = width // half
    bits = blocks.bit_length() - 1
    tall = half // bits

    def body(place_ref, n_ref, d_ref, g_ref, c_ref, before_ref, *refs):
        out_refs, scratch = refs[:-1], refs[-1]
        sums = weight_sums(place_ref[0], n_ref, d_ref, g_ref, c_ref, cores, line, blocks)
        for k in range(blocks):
            total = next(sums) + before_ref[k].astype(F32)
            for p in range(bits):
                at = sum((k >> (p + i) % bits & 1) << bits - 1 - i for i in range(bits))
                scratch[p, at] = total[p * tall : (p + 1) * tall]
        for p in range(bits):
            split_halves(scratch.at[p], place_ref[1 + p], out_refs[2 * p : 2 * p + 2])

    kept = (blocks // 2, tall, cols)
    return run(
        "weight_grad",
        body,
        [(kept, F32), (kept, BF16)] * bits,
        [place, normed, dproj, gated, cotangent, before],
        smem=1,
        scratch=[pltpu.VMEM((bits, blocks, tall, cols), F32)],
        flops=2 * length * half * (blocks * cols + 2 * width),
    )


def split_halves(ref, bit, out_refs):
    count = ref.shape[0] // 2
    for i, out_ref in enumerate(out_refs):
        start = (bit ^ i) * count
        for k in range(count):
            out_ref[k] = ref[start + k].astype(out_ref.dtype)


def fold(bits, kept, came):
    count, tall, cols = kept[0].shape
    many = len(kept)

    def body(bit_ref, *refs):
        kept_refs, came_refs, out_refs = refs[:many], refs[many : 2 * many], refs[2 * many : -1]
        scratch = refs[-1]
        for p in range(many):
            for k in range(count):
                scratch[p, k] = kept_refs[p][k] + came_refs[p][k].astype(F32)
            split_halves(scratch.at[p], bit_ref[p], out_refs[2 * p : 2 * p + 2])

    half = (count // 2, tall, cols)
    return run(
        "fold",
        body,
        [(half, F32), (half, BF16)] * many,
        [bits, *kept, *came],
        smem=1,
        scratch=[pltpu.VMEM((many, count, tall, cols), F32)],
    )


def cut_line(planes, kept, came):
    _, tall, cols = kept[0].shape
    many, line = len(kept), planes.shape[0]
    rows = many * tall // line

    def body(plane_ref, *refs):
        kept_refs, came_refs, out_refs = refs[:many], refs[many : 2 * many], refs[2 * many : -1]
        scratch = refs[-1]
        for p in range(many):
            scratch[p * tall : (p + 1) * tall] = kept_refs[p][0] + came_refs[p][0].astype(F32)
        for k in range(line):
            span = pl.ds(pl.multiple_of(plane_ref[k] * rows, rows), rows)
            out_refs[k][...] = scratch[span].astype(out_refs[k].dtype)

    return run(
        "cut_line",
        body,
        [((rows, cols), F32)] + [((rows, cols), BF16)] * (line - 1),
        [planes, *kept, *came],
        smem=1,
        scratch=[pltpu.VMEM((many * tall, cols), F32)],
    )


def add_up(parts):
    def body(*refs):
        total = refs[0][...].astype(F32)
        for ref in refs[1:-1]:
            total = total + ref[...].astype(F32)
        refs[-1][...] = total.astype(BF16)

    return run("add_up", body, [(parts[0].shape, BF16)], parts)[0]


def assemble(blocks, parts, edge):
    rows, cols = parts[0].shape
    total = cols * len(parts)

    def body(block_ref, *refs):
        part_refs, (left_ref, right_ref, held) = refs[: len(parts)], refs[len(parts) :]
        for k, ref in enumerate(part_refs):
            held[block_ref[k]] = ref[...].astype(F32)
        for k in range(len(parts)):
            first, last = k * cols, (k + 1) * cols
            cut = min(max(edge - first, 0), cols)
            if cut > 0:
                left_ref[:, first : first + cut] = held[k, :, :cut]
            if cut < cols:
                right_ref[:, first + cut - edge : last - edge] = held[k, :, cut:]

    return run(
        "assemble",
        body,
        [((rows, edge), F32), ((rows, total - edge), F32)],
        [blocks, *parts],
        smem=1,
        scratch=[pltpu.VMEM((len(parts), rows, cols), F32)],
    )


def local(
    item_table,
    action_table,
    item_owner,
    item_row,
    action_owner,
    action_row,
    input_norm_gain,
    w_proj,
    w_out,
    cotangent,
):
    grid = Grid()
    rows, width = item_table.shape
    replicas, line, cores = grid.replicas, grid.line, grid.cores
    cols = width // replicas

    bits = replicas.bit_length() - 1
    swaps = [3, 1, 2] if replicas == 4 else list(range(1, replicas))
    blocks = jnp.stack([grid.r ^ k for k in range(replicas)]).astype(I32)
    planes = jnp.stack([grid.z ^ k for k in range(line)]).astype(I32)
    bases = [(((grid.z ^ k) * cores + grid.c) * rows).astype(I32) for k in range(line)]

    own = jnp.concatenate(
        [
            lax.dynamic_slice_in_dim(item_table, grid.r * cols, cols, 1),
            lax.dynamic_slice_in_dim(action_table, grid.r * cols, cols, 1),
        ],
        axis=0,
    )
    keys = jnp.stack(
        [
            (item_owner * rows + item_row[:, None])[:, 0],
            (action_owner * rows + action_row[:, None])[:, 0],
        ]
    ).astype(I32)

    keys = jnp.stack([keys, grid.over_pair(keys)])
    keys = jnp.stack([keys] + [grid.over_replica(keys, k) for k in range(1, replicas)])

    held = {0: own}
    for low in reversed([1 << i for i in range(line.bit_length() - 1)]):
        for k in range(low, line, 2 * low):
            held[k] = grid.over_line(held[k ^ low], low)
    order = sorted(held, key=lambda k: (bin(k).count("1"), k))

    key_cols = jnp.broadcast_to(keys[..., None], (*keys.shape, LANES))
    both = list(range(cores))

    found = ()
    for k in order[:-1]:
        found = fetch(key_cols, both, held[k], bases[k], found)
    last = order[-1]
    there = fetch(key_cols, both[1:], held[last], bases[last], found[1:])
    here = fetch(key_cols, both[:1], held[last], bases[last], found[:1])
    pieces = combine([here[0], grid.over_pair(there[0])])
    for k in swaps:
        pieces[k] = grid.over_replica(pieces[k], k)

    layer_out, *rest = sequence(
        blocks,
        ((grid.c + 1) % cores).astype(I32).reshape(1),
        pieces,
        cotangent,
        input_norm_gain.reshape(1, width),
        w_proj,
        w_out,
        cores,
        line,
    )
    tokens, (normed, dproj, gated, weights) = rest[:replicas], rest[replicas:]
    for k in swaps:
        tokens[k] = grid.over_replica(tokens[k], k)

    place = jnp.stack([grid.c] + [grid.r >> p & 1 for p in range(bits)]).astype(I32)
    weights = grid.over_pair(weights)
    weights = weight_grad(place, normed, dproj, gated, cotangent, weights, line)
    tokens = lax.optimization_barrier((tokens, weights))[0]
    tokens = jnp.stack(tokens)
    there = grid.over_pair(tokens)

    def swap_weights(weights, step):
        kept, sent = weights[0::2], weights[1::2]
        return kept, [grid.over_replica(sent[p], 1 << (p + step) % bits) for p in range(bits)]

    kept, came = swap_weights(weights, 0)
    first = {k: gather_grad(keys, both[:1], [tokens], bases[k], rows) for k in order[-2:]}
    there = lax.optimization_barrier((there, came, first))[0]

    sums = {}
    for k in reversed(order):
        low = (k & -k) or line
        steps = [1 << i for i in range(low.bit_length() - 1)]
        out = F32 if steps else BF16
        if k in first:
            total = gather_grad(keys, both[1:], [there], bases[k], rows, [first[k]], out)
        else:
            total = gather_grad(keys, both, [tokens, there], bases[k], rows, out=out)
        for step in steps:
            total = total + grid.over_line(sums[k ^ step], step).astype(F32)
        sums[k] = total.astype(BF16) if k else total
    table_grad = sums[0]

    for step in range(1, bits + 1):
        after = sums[last] if step < bits else sums[line // 2]
        came = lax.optimization_barrier((came, after))[0]
        if step < bits:
            turn = jnp.stack([grid.r >> (p + step) % bits & 1 for p in range(bits)])
            kept, came = swap_weights(fold(turn.astype(I32), kept, came), step)
    parts = cut_line(planes, kept, came)
    parts = [parts[0]] + [grid.over_line(parts[k], k) for k in range(1, line)]
    parts = lax.optimization_barrier((parts, table_grad))[0]
    total = add_up(parts)
    parts = [total] + [grid.over_replica(total, k) for k in range(1, replicas)]
    grad_proj, grad_out = assemble(blocks, parts, 4 * width)

    return layer_out, table_grad[:rows], table_grad[rows:], grad_proj, grad_out


def solution(mesh):
    tokens = ("replica", "sparse")
    in_specs = (
        P("sparse", None),
        P("sparse", None),
        P(tokens, None),
        P(tokens),
        P(tokens, None),
        P(tokens),
        P(),
        P(),
        P(),
        P(tokens, None),
    )
    out_specs = (
        P(tokens, None),
        P("sparse", "replica"),
        P("sparse", "replica"),
        P("sparse", None),
        P("sparse", None),
    )
    return jax.shard_map(local, mesh=mesh, in_specs=in_specs, out_specs=out_specs, check_vma=False)
```

```python
import jax
import jax.numpy as jnp
from jax import lax
from jax.experimental import pallas as pl
from jax.experimental.pallas import tpu as pltpu
from jax.sharding import PartitionSpec as P

HEADS = 4
EPS = 1e-05
LANES = 128
F32 = jnp.float32
BF16 = jnp.bfloat16
I32 = jnp.int32
MIB = 1024 * 1024

NN = ((1,), (0,))
NT = ((1,), (1,))
TN = ((0,), (0,))


def dot(left, right, dims=NN):
    return lax.dot_general(left, right, (dims, ((), ())), preferred_element_type=F32)


def sigmoid(value):
    return 0.5 * jnp.tanh(0.5 * value) + 0.5


def run(name, body, outs, args, smem=0, scratch=(), vmem=16, flops=0):
    outs = [jax.ShapeDtypeStruct(shape, dtype) for shape, dtype in outs]
    size = sum(a.size * a.dtype.itemsize for a in [*args, *outs])
    in_smem = pl.BlockSpec(memory_space=pltpu.SMEM)
    in_vmem = pl.BlockSpec(memory_space=pltpu.VMEM)
    places = [in_smem] * smem + [in_vmem] * (len(args) - smem)
    results = pl.pallas_call(
        body,
        out_shape=outs,
        in_specs=places,
        out_specs=[in_vmem] * len(outs),
        scratch_shapes=list(scratch),
        compiler_params=pltpu.CompilerParams(vmem_limit_bytes=vmem * MIB),
        cost_estimate=pl.CostEstimate(flops=flops, bytes_accessed=size, transcendentals=0),
        name=name,
    )(*args)
    return list(results)


class Grid:
    def __init__(self):
        self.replicas = lax.axis_size("replica")
        self.shards = lax.axis_size("sparse")
        self.cores = 2 if self.shards % 2 == 0 else 1
        self.line = self.shards // self.cores
        self.r = lax.axis_index("replica")
        self.s = lax.axis_index("sparse")
        self.z = self.s // self.cores
        self.c = self.s % self.cores

    def over_replica(self, value, step):
        n = self.replicas
        return lax.ppermute(value, "replica", [(i, i ^ step) for i in range(n)])

    def over_line(self, value, step):
        pairs = [(i, i ^ step * self.cores) for i in range(self.shards)]
        return lax.ppermute(value, "sparse", pairs)

    def over_pair(self, value):
        return lax.ppermute(value, "sparse", [(i, i ^ 1) for i in range(self.shards)])


R, Z, C = range(3)


def first_row(ids, step, cores, rows):
    return ((ids[Z] ^ step) * cores + ids[C]) * rows


def fetch(ids, keys, cohorts, chunk, step, before=()):
    many = len(cohorts)
    count, cores, _, tokens, _ = keys.shape
    rows, cols = chunk.shape[0] // 2, chunk.shape[1]

    def body(ids, chunk_ref, key_ref, *refs):
        before_refs, out_refs = refs[:-many], refs[-many:]
        base = first_row(ids, step, cores, rows)
        lane = lax.broadcasted_iota(I32, (tokens, LANES), 1)
        for i, m in enumerate(cohorts):
            for k in range(count):
                hot = []
                for table in range(2):
                    place = key_ref[k, m, table] - base
                    for start in range(0, rows, LANES):
                        hot.append(jnp.where(place == lane + start, 1.0, 0.0).astype(BF16))
                found = dot(jnp.concatenate(hot, axis=1), chunk_ref[...])
                if before_refs:
                    found = found + before_refs[i][k].astype(F32)
                out_refs[i][k] = found.astype(BF16)

    return run(
        "fetch",
        body,
        [((count, tokens, cols), BF16)] * many,
        [ids, chunk, keys, *before],
        smem=1,
        flops=2 * many * count * tokens * rows * cols,
    )


def combine(parts):
    count, *shape = parts[0].shape

    def body(left_ref, right_ref, *out_refs):
        for k in range(count):
            total = left_ref[k].astype(F32) + right_ref[k].astype(F32)
            out_refs[k][...] = total.astype(BF16)

    return run("combine", body, [(tuple(shape), BF16)] * count, parts)


def pack(parts):
    def body(*refs):
        for k, ref in enumerate(refs[:-1]):
            refs[-1][k] = ref[...]

    shape, dtype = parts[0].shape, parts[0].dtype
    return run("pack", body, [((len(parts), *shape), dtype)], parts)[0]


def add_up(parts, cuts=1, out=BF16):
    rows, cols = parts[0].shape
    tall = rows // cuts

    def body(*refs):
        part_refs, out_refs = refs[: len(parts)], refs[len(parts) :]
        for i in range(cuts):
            span = slice(i * tall, (i + 1) * tall)
            total = part_refs[0][span, :].astype(F32)
            for ref in part_refs[1:]:
                total = total + ref[span, :].astype(F32)
            out_refs[i][...] = total.astype(out)

    return run("add_up", body, [((tall, cols), out)] * cuts, parts)


def gather_grad(ids, keys, cohorts, tokens, step, rows, before=(), out=BF16):
    many = len(cohorts)
    count, cores, _, length = keys.shape
    cols = tokens[0].shape[-1]

    def body(ids, key_ref, *refs):
        base = first_row(ids, step, cores, rows)
        piece_refs, before_refs, out_ref = refs[:many], refs[many:-1], refs[-1]
        row = lax.broadcasted_iota(I32, (rows, length), 0)
        for table in range(2):
            span = slice(table * rows, (table + 1) * rows)
            sums = None
            for i, m in enumerate(cohorts):
                hot = []
                for k in range(count):
                    place = key_ref[k, m, table : table + 1, :] - base
                    hot.append(jnp.where(place == row, 1.0, 0.0).astype(BF16))
                piece = piece_refs[i][...].reshape(count * length, cols)
                part = dot(jnp.concatenate(hot, axis=1), piece)
                sums = part if sums is None else sums + part
            for ref in before_refs:
                sums = sums + ref[span, :].astype(F32)
            out_ref[span, :] = sums.astype(out)

    return run(
        "gather_grad",
        body,
        [((2 * rows, cols), out)],
        [ids, keys, *tokens, *before],
        smem=1,
        flops=4 * many * count * length * 2 * rows * cols,
    )[0]


def sequence(ids, pieces, cotangent, gain, w_proj, w_out, cores, line):
    count = len(pieces)
    length, width = cotangent.shape
    cols = width // count
    head_dim = width // HEADS
    factor = head_dim ** (-0.5)
    tile = min(256, length)
    step = min(256, 4 * width)

    def body(ids, cot_ref, wo_ref, wp_ref, gain_ref, *refs):
        piece_refs, refs = refs[:count], refs[count:]
        out_ref, *grad_refs = refs[: count + 1]
        normed_ref, dproj_ref, gated_ref, weight_ref = refs[count + 1 : count + 5]
        emb, act, slope, att, attn, dscale, dkey, dval, tok = refs[count + 5 :]

        for k in range(count):
            emb[ids[R] ^ k] = piece_refs[k][...]

        def embedded(span):
            return jnp.concatenate([emb[k, span] for k in range(count)], axis=1).astype(F32)

        def norm_of(value):
            centred = value - jnp.mean(value, axis=-1, keepdims=True)
            scale = lax.rsqrt(jnp.mean(centred * centred, axis=-1, keepdims=True) + EPS)
            return centred * scale, scale

        def norm_back(upper, hat, scale):
            return scale * (
                upper
                - jnp.mean(upper, axis=-1, keepdims=True)
                - hat * jnp.mean(upper * hat, axis=-1, keepdims=True)
            )

        for at in range(0, length, tile):
            span = slice(at, at + tile)
            hat, _ = norm_of(embedded(span))
            normed_ref[span, :] = (hat * gain_ref[...]).astype(BF16)

        normed = normed_ref[...]

        @pl.loop(0, 4 * width // step)
        def _(j):
            span = pl.ds(pl.multiple_of(j * step, step), step)
            proj = dot(normed, wp_ref[:, span])
            sig = sigmoid(proj)
            act[:, span] = (proj * sig).astype(BF16)
            slope[:, span] = sig * (1.0 + proj * (1.0 - sig))

        dkey[...] = jnp.zeros_like(dkey)
        dval[...] = jnp.zeros_like(dval)

        for at in range(0, length, tile):
            span = slice(at, at + tile)
            seen = at + tile
            past = slice(0, seen)
            keep = lax.broadcasted_iota(I32, (tile, seen), 1) <= at + lax.broadcasted_iota(
                I32, (tile, seen), 0
            )
            for h in range(HEADS):
                head = [slice(p * width + h * head_dim, p * width + (h + 1) * head_dim) for p in range(4)]
                scores = dot(act[span, head[2]], act[past, head[3]], NT) * factor
                sig = sigmoid(scores)
                soft = jnp.where(keep, scores * sig * (1.0 / length), 0.0).astype(BF16)
                attn[h, :, :seen] = soft
                grad = sig * (1.0 + scores * (1.0 - sig)) * (factor / length)
                dscale[h, :, :seen] = jnp.where(keep, grad, 0.0)
                att[:, head[0]] = dot(soft, act[past, head[1]])
            hat, scale = norm_of(att[...])
            gate = act[span, :width].astype(F32)
            gated = (hat * gate).astype(BF16)
            gated_ref[span, :] = gated
            out_ref[span, :] = (embedded(span) + dot(gated, wo_ref[...])).astype(BF16)
            dgated = dot(cot_ref[span, :], wo_ref[...], NT)
            dproj_ref[span, :width] = (dgated * hat * slope[span, :width]).astype(BF16)
            datt = norm_back(dgated * gate, hat, scale).astype(BF16)
            for h in range(HEADS):
                head = [slice(p * width + h * head_dim, p * width + (h + 1) * head_dim) for p in range(4)]
                dhead = datt[:, head[0]]
                dattn = dot(dhead, act[past, head[1]], NT)
                dscores = (dattn * dscale[h, :, :seen]).astype(BF16)
                dquery = dot(dscores, act[past, head[3]])
                dproj_ref[span, head[2]] = (dquery * slope[span, head[2]]).astype(BF16)
                dkey[past, head[0]] += dot(dscores, act[span, head[2]], TN)
                dval[past, head[0]] += dot(attn[h, :, :seen], dhead, TN)

        dproj_ref[:, width : 2 * width] = (dval[...] * slope[:, width : 2 * width]).astype(BF16)
        dproj_ref[:, 3 * width :] = (dkey[...] * slope[:, 3 * width :]).astype(BF16)

        for at in range(0, length, tile):
            span = slice(at, at + tile)
            hat, scale = norm_of(embedded(span))
            upper = dot(dproj_ref[span, :], wp_ref[...], NT) * gain_ref[...]
            grad = cot_ref[span, :].astype(F32) + norm_back(upper, hat, scale)
            for k in range(count):
                tok[k, span] = grad[:, k * cols : (k + 1) * cols].astype(BF16)

        for k in range(count):
            grad_refs[k][...] = tok[ids[R] ^ k]

        other = (ids[C] + 1) % cores
        sums = weight_sums(other, normed_ref, dproj_ref, gated_ref, cot_ref, cores, line, count)
        for k in range(count):
            weight_ref[k] = next(sums).astype(BF16)

    return run(
        "sequence",
        body,
        [
            ((length, width), BF16),
            *[((length, cols), BF16)] * count,
            ((length, width), BF16),
            ((length, 4 * width), BF16),
            ((length, width), BF16),
            ((count, width // cores, 5 * width // count), BF16),
        ],
        [ids, cotangent, w_out, w_proj, gain, *pieces],
        smem=1,
        vmem=24,
        flops=32 * length * width * width,
        scratch=[
            pltpu.VMEM((count, length, cols), BF16),
            pltpu.VMEM((length, 4 * width), BF16),
            pltpu.VMEM((length, 4 * width), F32),
            pltpu.VMEM((tile, width), F32),
            pltpu.VMEM((HEADS, tile, length), BF16),
            pltpu.VMEM((HEADS, tile, length), F32),
            pltpu.VMEM((length, width), F32),
            pltpu.VMEM((length, width), F32),
            pltpu.VMEM((count, length, cols), BF16),
        ],
    )


def weight_sums(core, n_ref, d_ref, g_ref, c_ref, cores, line, blocks):
    length, width = n_ref.shape
    rows = width // (cores * line)
    half = width // cores
    edge = d_ref.shape[1]
    cols = (edge + c_ref.shape[1]) // blocks
    feature = lax.broadcasted_iota(I32, (width, half), 0)
    column = lax.broadcasted_iota(I32, (width, half), 1)
    wanted = (column // rows * cores + core) * rows + column % rows
    pick = jnp.where(feature == wanted, 1.0, 0.0).astype(BF16)
    n_part = dot(n_ref[...], pick).astype(BF16)
    g_part = dot(g_ref[...], pick).astype(BF16)
    for k in range(blocks):
        first, last = k * cols, (k + 1) * cols
        parts = []
        if first < edge:
            parts.append(dot(n_part, d_ref[:, first : min(last, edge)], TN))
        if last > edge:
            parts.append(dot(g_part, c_ref[:, max(first, edge) - edge : last - edge], TN))
        yield parts[0] if len(parts) == 1 else jnp.concatenate(parts, axis=1)


def weight_grad(ids, normed, dproj, gated, cotangent, before, line):
    blocks, half, cols = before.shape
    length, width = normed.shape
    cores = width // half
    bits = blocks.bit_length() - 1
    tall = half // bits

    def body(ids, n_ref, d_ref, g_ref, c_ref, before_ref, *refs):
        out_refs, scratch = refs[:-1], refs[-1]
        sums = weight_sums(ids[C], n_ref, d_ref, g_ref, c_ref, cores, line, blocks)
        for k in range(blocks):
            total = next(sums) + before_ref[k].astype(F32)
            for p in range(bits):
                at = sum((k >> (p + i) % bits & 1) << bits - 1 - i for i in range(bits))
                scratch[p, at] = total[p * tall : (p + 1) * tall]
        for p in range(bits):
            split_halves(scratch.at[p], ids[R] >> p & 1, out_refs[2 * p : 2 * p + 2])

    kept = (blocks // 2, tall, cols)
    return run(
        "weight_grad",
        body,
        [(kept, F32), (kept, BF16)] * bits,
        [ids, normed, dproj, gated, cotangent, before],
        smem=1,
        scratch=[pltpu.VMEM((bits, blocks, tall, cols), F32)],
        flops=2 * length * half * (blocks * cols + 2 * width),
    )


def split_halves(ref, bit, out_refs):
    count = ref.shape[0] // 2
    for i, out_ref in enumerate(out_refs):
        start = (bit ^ i) * count
        for k in range(count):
            out_ref[k] = ref[start + k].astype(out_ref.dtype)


def fold(ids, kept, came, step):
    count, tall, cols = kept[0].shape
    many = len(kept)

    def body(ids, *refs):
        kept_refs, came_refs, out_refs = refs[:many], refs[many : 2 * many], refs[2 * many : -1]
        scratch = refs[-1]
        for p in range(many):
            for k in range(count):
                scratch[p, k] = kept_refs[p][k] + came_refs[p][k].astype(F32)
            split_halves(scratch.at[p], ids[R] >> (p + step) % many & 1, out_refs[2 * p : 2 * p + 2])

    half = (count // 2, tall, cols)
    return run(
        "fold",
        body,
        [(half, F32), (half, BF16)] * many,
        [ids, *kept, *came],
        smem=1,
        scratch=[pltpu.VMEM((many, count, tall, cols), F32)],
    )


def cut_line(ids, kept, came, line):
    _, tall, cols = kept[0].shape
    many = len(kept)
    rows = many * tall // line

    def body(ids, *refs):
        kept_refs, came_refs, out_refs = refs[:many], refs[many : 2 * many], refs[2 * many : -1]
        scratch = refs[-1]
        for p in range(many):
            scratch[p * tall : (p + 1) * tall] = kept_refs[p][0] + came_refs[p][0].astype(F32)
        for k in range(line):
            span = pl.ds(pl.multiple_of((ids[Z] ^ k) * rows, rows), rows)
            out_refs[k][...] = scratch[span].astype(out_refs[k].dtype)

    return run(
        "cut_line",
        body,
        [((rows, cols), F32)] + [((rows, cols), BF16)] * (line - 1),
        [ids, *kept, *came],
        smem=1,
        scratch=[pltpu.VMEM((many * tall, cols), F32)],
    )


def assemble(ids, parts, edge):
    rows, cols = parts[0].shape
    total = cols * len(parts)

    def body(ids, *refs):
        part_refs, (left_ref, right_ref, held) = refs[: len(parts)], refs[len(parts) :]
        for k, ref in enumerate(part_refs):
            held[ids[R] ^ k] = ref[...].astype(F32)
        for k in range(len(parts)):
            first, last = k * cols, (k + 1) * cols
            cut = min(max(edge - first, 0), cols)
            if cut > 0:
                left_ref[:, first : first + cut] = held[k, :, :cut]
            if cut < cols:
                right_ref[:, first + cut - edge : last - edge] = held[k, :, cut:]

    return run(
        "assemble",
        body,
        [((rows, edge), F32), ((rows, total - edge), F32)],
        [ids, *parts],
        smem=1,
        scratch=[pltpu.VMEM((len(parts), rows, cols), F32)],
    )


def local(
    item_table,
    action_table,
    item_owner,
    item_row,
    action_owner,
    action_row,
    input_norm_gain,
    w_proj,
    w_out,
    cotangent,
):
    grid = Grid()
    rows, width = item_table.shape
    replicas, line, cores = grid.replicas, grid.line, grid.cores
    cols = width // replicas

    bits = replicas.bit_length() - 1
    swaps = [3, 1, 2] if replicas == 4 else list(range(1, replicas))
    ids = jnp.stack([grid.r, grid.z, grid.c]).astype(I32)

    own = jnp.concatenate(
        [
            lax.dynamic_slice_in_dim(item_table, grid.r * cols, cols, 1),
            lax.dynamic_slice_in_dim(action_table, grid.r * cols, cols, 1),
        ],
        axis=0,
    )
    keys = jnp.stack(
        [
            (item_owner * rows + item_row[:, None])[:, 0],
            (action_owner * rows + action_row[:, None])[:, 0],
        ]
    ).astype(I32)

    keys = jnp.stack([keys, grid.over_pair(keys)])
    keys = jnp.stack([keys] + [grid.over_replica(keys, k) for k in range(1, replicas)])

    held = {0: own}
    for low in reversed([1 << i for i in range(line.bit_length() - 1)]):
        for k in range(low, line, 2 * low):
            held[k] = grid.over_line(held[k ^ low], low)
    order = sorted(held, key=lambda k: (bin(k).count("1"), k))

    key_cols = jnp.broadcast_to(keys[..., None], (*keys.shape, LANES))
    both = list(range(cores))

    found = ()
    for k in order[:-1]:
        found = fetch(ids, key_cols, both, held[k], k, found)
    last = order[-1]
    there = fetch(ids, key_cols, both[1:], held[last], last, found[1:])
    here = fetch(ids, key_cols, both[:1], held[last], last, found[:1])
    pieces = combine([here[0], grid.over_pair(there[0])])
    for k in swaps:
        pieces[k] = grid.over_replica(pieces[k], k)

    gain = input_norm_gain.reshape(1, width)
    layer_out, *rest = sequence(ids, pieces, cotangent, gain, w_proj, w_out, cores, line)
    tokens, (normed, dproj, gated, weights) = rest[:replicas], rest[replicas:]
    for k in swaps:
        tokens[k] = grid.over_replica(tokens[k], k)

    weights = grid.over_pair(weights)
    weights = weight_grad(ids, normed, dproj, gated, cotangent, weights, line)
    tokens = lax.optimization_barrier((tokens, weights))[0]
    tokens = pack(tokens)
    there = grid.over_pair(tokens)

    def swap_weights(weights, step):
        kept, sent = weights[0::2], weights[1::2]
        return kept, [grid.over_replica(sent[p], 1 << (p + step) % bits) for p in range(bits)]

    kept, came = swap_weights(weights, 0)
    first = {k: gather_grad(ids, keys, both[:1], [tokens], k, rows) for k in order[-2:]}

    sums = {}
    for k in reversed(order):
        low = (k & -k) or line
        steps = [1 << i for i in range(low.bit_length() - 1)]
        out = F32 if steps else BF16
        if k in first:
            sums[k] = gather_grad(ids, keys, both[1:], [there], k, rows, [first[k]], out)
        else:
            if k == 1:
                there = lax.optimization_barrier((there, came))[0]
            sums[k] = gather_grad(ids, keys, both, [tokens, there], k, rows, out=out)
        if steps:
            parts = [sums[k]] + [grid.over_line(sums[k ^ step], step) for step in steps]
            sums[k] = add_up(parts, 1, BF16)[0] if k else add_up(parts, 2, F32)
    item_grad, action_grad = sums[0]

    for step in range(1, bits + 1):
        after = sums[last] if step < bits else sums[line // 2]
        came = lax.optimization_barrier((came, after))[0]
        if step < bits:
            kept, came = swap_weights(fold(ids, kept, came, step), step)
    parts = cut_line(ids, kept, came, line)
    parts = [parts[0]] + [grid.over_line(parts[k], k) for k in range(1, line)]
    parts = lax.optimization_barrier((parts, item_grad))[0]
    total = add_up(parts)[0]
    parts = [total] + [grid.over_replica(total, k) for k in range(1, replicas)]
    grad_proj, grad_out = assemble(ids, parts, 4 * width)

    return layer_out, item_grad, action_grad, grad_proj, grad_out


def solution(mesh):
    tokens = ("replica", "sparse")
    in_specs = (
        P("sparse", None),
        P("sparse", None),
        P(tokens, None),
        P(tokens),
        P(tokens, None),
        P(tokens),
        P(),
        P(),
        P(),
        P(tokens, None),
    )
    out_specs = (
        P(tokens, None),
        P("sparse", "replica"),
        P("sparse", "replica"),
        P("sparse", None),
        P("sparse", None),
    )
    return jax.shard_map(local, mesh=mesh, in_specs=in_specs, out_specs=out_specs, check_vma=False)
```

```python
import jax
import jax.numpy as jnp
from jax import lax
from jax.experimental import pallas as pl
from jax.experimental.pallas import tpu as pltpu
from jax.sharding import PartitionSpec as P

HEADS = 4
EPS = 1e-05
LANES = 128
F32 = jnp.float32
BF16 = jnp.bfloat16
I32 = jnp.int32
MIB = 1024 * 1024

NN = ((1,), (0,))
NT = ((1,), (1,))
TN = ((0,), (0,))


def dot(left, right, dims=NN):
    return lax.dot_general(left, right, (dims, ((), ())), preferred_element_type=F32)


def sigmoid(value):
    return 0.5 * jnp.tanh(0.5 * value) + 0.5


def run(name, body, outs, args, smem=0, scratch=(), vmem=16, flops=0):
    outs = [jax.ShapeDtypeStruct(shape, dtype) for shape, dtype in outs]
    size = sum(a.size * a.dtype.itemsize for a in [*args, *outs])
    in_smem = pl.BlockSpec(memory_space=pltpu.SMEM)
    in_vmem = pl.BlockSpec(memory_space=pltpu.VMEM)
    places = [in_smem] * smem + [in_vmem] * (len(args) - smem)
    results = pl.pallas_call(
        body,
        out_shape=outs,
        in_specs=places,
        out_specs=[in_vmem] * len(outs),
        scratch_shapes=list(scratch),
        compiler_params=pltpu.CompilerParams(vmem_limit_bytes=vmem * MIB),
        cost_estimate=pl.CostEstimate(flops=flops, bytes_accessed=size, transcendentals=0),
        name=name,
    )(*args)
    return list(results)


class Grid:
    def __init__(self):
        self.replicas = lax.axis_size("replica")
        self.shards = lax.axis_size("sparse")
        self.cores = 2 if self.shards % 2 == 0 else 1
        self.line = self.shards // self.cores
        self.r = lax.axis_index("replica")
        self.s = lax.axis_index("sparse")
        self.z = self.s // self.cores
        self.c = self.s % self.cores

    def over_replica(self, value, step):
        n = self.replicas
        return lax.ppermute(value, "replica", [(i, i ^ step) for i in range(n)])

    def over_line(self, value, step):
        pairs = [(i, i ^ step * self.cores) for i in range(self.shards)]
        return lax.ppermute(value, "sparse", pairs)

    def over_pair(self, value):
        return lax.ppermute(value, "sparse", [(i, i ^ 1) for i in range(self.shards)])


def fetch(base, keys, cohorts, chunk, before=()):
    many = len(cohorts)
    count, _, _, tokens, _ = keys.shape
    rows, cols = chunk.shape[0] // 2, chunk.shape[1]

    def body(base_ref, chunk_ref, key_ref, *refs):
        before_refs, out_refs = refs[:-many], refs[-many:]
        lane = lax.broadcasted_iota(I32, (tokens, LANES), 1)
        for i, m in enumerate(cohorts):
            for k in range(count):
                hot = []
                for table in range(2):
                    place = key_ref[k, m, table] - base_ref[0]
                    for start in range(0, rows, LANES):
                        hot.append(jnp.where(place == lane + start, 1.0, 0.0).astype(BF16))
                found = dot(jnp.concatenate(hot, axis=1), chunk_ref[...])
                if before_refs:
                    found = found + before_refs[i][k].astype(F32)
                out_refs[i][k] = found.astype(BF16)

    return run(
        "fetch",
        body,
        [((count, tokens, cols), BF16)] * many,
        [base, chunk, keys, *before],
        smem=1,
        flops=2 * many * count * tokens * rows * cols,
    )


def combine(parts):
    count, *shape = parts[0].shape

    def body(left_ref, right_ref, *out_refs):
        for k in range(count):
            total = left_ref[k].astype(F32) + right_ref[k].astype(F32)
            out_refs[k][...] = total.astype(BF16)

    return run("combine", body, [(tuple(shape), BF16)] * count, parts)


def pack(parts):
    def body(*refs):
        for k, ref in enumerate(refs[:-1]):
            refs[-1][k] = ref[...]

    shape, dtype = parts[0].shape, parts[0].dtype
    return run("pack", body, [((len(parts), *shape), dtype)], parts)[0]


def add_up(parts):
    def body(*refs):
        total = refs[0][...].astype(F32)
        for ref in refs[1:-1]:
            total = total + ref[...].astype(F32)
        refs[-1][...] = total.astype(BF16)

    return run("add_up", body, [(parts[0].shape, BF16)], parts)[0]


def table_sums(here, whole, halves):
    rows, cols = here.shape[0] // 2, here.shape[1]

    def body(here_ref, *refs):
        whole_refs, half_refs, out_refs = refs[: len(whole)], refs[len(whole) : -2], refs[-2:]
        for i in range(2):
            span = slice(i * rows, (i + 1) * rows)
            total = here_ref[span, :]
            for ref in whole_refs:
                total = total + ref[span, :].astype(F32)
            for ref in half_refs[i::2]:
                total = total + ref[...].astype(F32)
            out_refs[i][...] = total

    return run("table_sums", body, [((rows, cols), F32)] * 2, [here, *whole, *halves])


def gather_grad(base, keys, cohorts, tokens, rows, before=(), out=BF16, apart=False):
    many = len(cohorts)
    count, _, _, length = keys.shape
    cols = tokens[0].shape[-1]

    def body(base_ref, key_ref, *refs):
        piece_refs, before_refs = refs[:many], refs[many : many + len(before)]
        out_refs = refs[many + len(before) :]
        row = lax.broadcasted_iota(I32, (rows, length), 0)
        for table in range(2):
            span = slice(table * rows, (table + 1) * rows)
            sums = None
            for i, m in enumerate(cohorts):
                hot = []
                for k in range(count):
                    place = key_ref[k, m, table : table + 1, :] - base_ref[0]
                    hot.append(jnp.where(place == row, 1.0, 0.0).astype(BF16))
                piece = piece_refs[i][...].reshape(count * length, cols)
                part = dot(jnp.concatenate(hot, axis=1), piece)
                sums = part if sums is None else sums + part
            for ref in before_refs:
                sums = sums + ref[span, :].astype(F32)
            if apart:
                out_refs[table][...] = sums.astype(out)
            else:
                out_refs[0][span, :] = sums.astype(out)

    return run(
        "gather_grad",
        body,
        [((rows, cols), out)] * 2 if apart else [((2 * rows, cols), out)],
        [base, keys, *tokens, *before],
        smem=1,
        flops=4 * many * count * length * 2 * rows * cols,
    )


def sequence(replica, core, pieces, cotangent, gain, w_proj, w_out, cores, line):
    count = len(pieces)
    length, width = cotangent.shape
    cols = width // count
    head_dim = width // HEADS
    factor = head_dim ** (-0.5)
    tile = min(256, length)
    step = min(256, 4 * width)

    def body(r_ref, core_ref, cot_ref, wo_ref, wp_ref, gain_ref, *refs):
        piece_refs, refs = refs[:count], refs[count:]
        out_ref, *grad_refs = refs[: count + 1]
        normed_ref, dproj_ref, gated_ref, weight_ref = refs[count + 1 : count + 5]
        emb, act, slope, att, attn, dscale, dkey, dval, tok = refs[count + 5 :]

        for k in range(count):
            emb[r_ref[0] ^ k] = piece_refs[k][...]

        def embedded(span):
            return jnp.concatenate([emb[k, span] for k in range(count)], axis=1).astype(F32)

        def norm_of(value):
            centred = value - jnp.mean(value, axis=-1, keepdims=True)
            scale = lax.rsqrt(jnp.mean(centred * centred, axis=-1, keepdims=True) + EPS)
            return centred * scale, scale

        def norm_back(upper, hat, scale):
            return scale * (
                upper
                - jnp.mean(upper, axis=-1, keepdims=True)
                - hat * jnp.mean(upper * hat, axis=-1, keepdims=True)
            )

        for at in range(0, length, tile):
            span = slice(at, at + tile)
            hat, _ = norm_of(embedded(span))
            normed_ref[span, :] = (hat * gain_ref[...]).astype(BF16)

        normed = normed_ref[...]

        @pl.loop(0, 4 * width // step)
        def _(j):
            span = pl.ds(pl.multiple_of(j * step, step), step)
            proj = dot(normed, wp_ref[:, span])
            sig = sigmoid(proj)
            act[:, span] = (proj * sig).astype(BF16)
            slope[:, span] = sig * (1.0 + proj * (1.0 - sig))

        dkey[...] = jnp.zeros_like(dkey)
        dval[...] = jnp.zeros_like(dval)

        for at in range(0, length, tile):
            span = slice(at, at + tile)
            seen = at + tile
            past = slice(0, seen)
            keep = lax.broadcasted_iota(I32, (tile, seen), 1) <= at + lax.broadcasted_iota(
                I32, (tile, seen), 0
            )
            for h in range(HEADS):
                head = [slice(p * width + h * head_dim, p * width + (h + 1) * head_dim) for p in range(4)]
                scores = dot(act[span, head[2]], act[past, head[3]], NT) * factor
                sig = sigmoid(scores)
                soft = jnp.where(keep, scores * sig * (1.0 / length), 0.0).astype(BF16)
                attn[h, :, :seen] = soft
                grad = sig * (1.0 + scores * (1.0 - sig)) * (factor / length)
                dscale[h, :, :seen] = jnp.where(keep, grad, 0.0)
                att[:, head[0]] = dot(soft, act[past, head[1]])
            hat, scale = norm_of(att[...])
            gate = act[span, :width].astype(F32)
            gated = (hat * gate).astype(BF16)
            gated_ref[span, :] = gated
            out_ref[span, :] = (embedded(span) + dot(gated, wo_ref[...])).astype(BF16)
            dgated = dot(cot_ref[span, :], wo_ref[...], NT)
            dproj_ref[span, :width] = (dgated * hat * slope[span, :width]).astype(BF16)
            datt = norm_back(dgated * gate, hat, scale).astype(BF16)
            for h in range(HEADS):
                head = [slice(p * width + h * head_dim, p * width + (h + 1) * head_dim) for p in range(4)]
                dhead = datt[:, head[0]]
                dattn = dot(dhead, act[past, head[1]], NT)
                dscores = (dattn * dscale[h, :, :seen]).astype(BF16)
                dquery = dot(dscores, act[past, head[3]])
                dproj_ref[span, head[2]] = (dquery * slope[span, head[2]]).astype(BF16)
                dkey[past, head[0]] += dot(dscores, act[span, head[2]], TN)
                dval[past, head[0]] += dot(attn[h, :, :seen], dhead, TN)

        dproj_ref[:, width : 2 * width] = (dval[...] * slope[:, width : 2 * width]).astype(BF16)
        dproj_ref[:, 3 * width :] = (dkey[...] * slope[:, 3 * width :]).astype(BF16)

        for at in range(0, length, tile):
            span = slice(at, at + tile)
            hat, scale = norm_of(embedded(span))
            upper = dot(dproj_ref[span, :], wp_ref[...], NT) * gain_ref[...]
            grad = cot_ref[span, :].astype(F32) + norm_back(upper, hat, scale)
            for k in range(count):
                tok[k, span] = grad[:, k * cols : (k + 1) * cols].astype(BF16)

        for k in range(count):
            grad_refs[k][...] = tok[r_ref[0] ^ k]

        other = (core_ref[0] + 1) % cores
        sums = weight_sums(other, normed_ref, dproj_ref, gated_ref, cot_ref, cores, line, count)
        for k in range(count):
            weight_ref[k] = next(sums).astype(BF16)

    return run(
        "sequence",
        body,
        [
            ((length, width), BF16),
            *[((length, cols), BF16)] * count,
            ((length, width), BF16),
            ((length, 4 * width), BF16),
            ((length, width), BF16),
            ((count, width // cores, 5 * width // count), BF16),
        ],
        [replica, core, cotangent, w_out, w_proj, gain, *pieces],
        smem=2,
        vmem=24,
        flops=32 * length * width * width,
        scratch=[
            pltpu.VMEM((count, length, cols), BF16),
            pltpu.VMEM((length, 4 * width), BF16),
            pltpu.VMEM((length, 4 * width), F32),
            pltpu.VMEM((tile, width), F32),
            pltpu.VMEM((HEADS, tile, length), BF16),
            pltpu.VMEM((HEADS, tile, length), F32),
            pltpu.VMEM((length, width), F32),
            pltpu.VMEM((length, width), F32),
            pltpu.VMEM((count, length, cols), BF16),
        ],
    )


def weight_sums(core, n_ref, d_ref, g_ref, c_ref, cores, line, blocks):
    length, width = n_ref.shape
    rows = width // (cores * line)
    half = width // cores
    edge = d_ref.shape[1]
    cols = (edge + c_ref.shape[1]) // blocks
    feature = lax.broadcasted_iota(I32, (width, half), 0)
    column = lax.broadcasted_iota(I32, (width, half), 1)
    wanted = (column // rows * cores + core) * rows + column % rows
    pick = jnp.where(feature == wanted, 1.0, 0.0).astype(BF16)
    n_part = dot(n_ref[...], pick).astype(BF16)
    g_part = dot(g_ref[...], pick).astype(BF16)
    for k in range(blocks):
        first, last = k * cols, (k + 1) * cols
        parts = []
        if first < edge:
            parts.append(dot(n_part, d_ref[:, first : min(last, edge)], TN))
        if last > edge:
            parts.append(dot(g_part, c_ref[:, max(first, edge) - edge : last - edge], TN))
        yield parts[0] if len(parts) == 1 else jnp.concatenate(parts, axis=1)


def weight_grad(replica, core, normed, dproj, gated, cotangent, before, line):
    blocks, half, cols = before.shape
    length, width = normed.shape
    cores = width // half
    bits = blocks.bit_length() - 1
    tall = half // bits

    def body(r_ref, core_ref, n_ref, d_ref, g_ref, c_ref, before_ref, *refs):
        out_refs, scratch = refs[:-1], refs[-1]
        sums = weight_sums(core_ref[0], n_ref, d_ref, g_ref, c_ref, cores, line, blocks)
        for k in range(blocks):
            total = next(sums) + before_ref[k].astype(F32)
            for p in range(bits):
                at = sum((k >> (p + i) % bits & 1) << bits - 1 - i for i in range(bits))
                scratch[p, at] = total[p * tall : (p + 1) * tall]
        for p in range(bits):
            split_halves(scratch.at[p], r_ref[0] >> p & 1, out_refs[2 * p : 2 * p + 2])

    kept = (blocks // 2, tall, cols)
    return run(
        "weight_grad",
        body,
        [(kept, F32), (kept, BF16)] * bits,
        [replica, core, normed, dproj, gated, cotangent, before],
        smem=2,
        scratch=[pltpu.VMEM((bits, blocks, tall, cols), F32)],
        flops=2 * length * half * (blocks * cols + 2 * width),
    )


def split_halves(ref, bit, out_refs):
    count = ref.shape[0] // 2
    for i, out_ref in enumerate(out_refs):
        start = (bit ^ i) * count
        for k in range(count):
            out_ref[k] = ref[start + k].astype(out_ref.dtype)


def fold(replica, kept, came, step):
    count, tall, cols = kept[0].shape
    many = len(kept)

    def body(r_ref, *refs):
        kept_refs, came_refs, out_refs = refs[:many], refs[many : 2 * many], refs[2 * many : -1]
        scratch = refs[-1]
        for p in range(many):
            for k in range(count):
                scratch[p, k] = kept_refs[p][k] + came_refs[p][k].astype(F32)
            split_halves(scratch.at[p], r_ref[0] >> (p + step) % many & 1, out_refs[2 * p : 2 * p + 2])

    half = (count // 2, tall, cols)
    return run(
        "fold",
        body,
        [(half, F32), (half, BF16)] * many,
        [replica, *kept, *came],
        smem=1,
        scratch=[pltpu.VMEM((many, count, tall, cols), F32)],
    )


def cut_line(place, kept, came, line):
    _, tall, cols = kept[0].shape
    many = len(kept)
    rows = many * tall // line

    def body(place_ref, *refs):
        kept_refs, came_refs, out_refs = refs[:many], refs[many : 2 * many], refs[2 * many : -1]
        scratch = refs[-1]
        for p in range(many):
            scratch[p * tall : (p + 1) * tall] = kept_refs[p][0] + came_refs[p][0].astype(F32)
        for k in range(line):
            span = pl.ds(pl.multiple_of((place_ref[0] ^ k) * rows, rows), rows)
            out_refs[k][...] = scratch[span].astype(out_refs[k].dtype)

    return run(
        "cut_line",
        body,
        [((rows, cols), F32)] + [((rows, cols), BF16)] * (line - 1),
        [place, *kept, *came],
        smem=1,
        scratch=[pltpu.VMEM((many * tall, cols), F32)],
    )


def assemble(replica, parts, edge):
    rows, cols = parts[0].shape
    total = cols * len(parts)

    def body(r_ref, *refs):
        part_refs, (left_ref, right_ref, held) = refs[: len(parts)], refs[len(parts) :]
        for k, ref in enumerate(part_refs):
            held[r_ref[0] ^ k] = ref[...].astype(F32)
        for k in range(len(parts)):
            first, last = k * cols, (k + 1) * cols
            cut = min(max(edge - first, 0), cols)
            if cut > 0:
                left_ref[:, first : first + cut] = held[k, :, :cut]
            if cut < cols:
                right_ref[:, first + cut - edge : last - edge] = held[k, :, cut:]

    return run(
        "assemble",
        body,
        [((rows, edge), F32), ((rows, total - edge), F32)],
        [replica, *parts],
        smem=1,
        scratch=[pltpu.VMEM((len(parts), rows, cols), F32)],
    )


def local(
    item_table,
    action_table,
    item_owner,
    item_row,
    action_owner,
    action_row,
    input_norm_gain,
    w_proj,
    w_out,
    cotangent,
):
    grid = Grid()
    rows, width = item_table.shape
    replicas, line, cores = grid.replicas, grid.line, grid.cores
    cols = width // replicas

    bits = replicas.bit_length() - 1
    swaps = [3, 1, 2] if replicas == 4 else list(range(1, replicas))
    replica, place, core = (i.astype(I32).reshape(1) for i in (grid.r, grid.z, grid.c))
    bases = [((place ^ k) * cores + core) * rows for k in range(line)]

    own = jnp.concatenate(
        [
            lax.dynamic_slice_in_dim(item_table, grid.r * cols, cols, 1),
            lax.dynamic_slice_in_dim(action_table, grid.r * cols, cols, 1),
        ],
        axis=0,
    )
    keys = jnp.stack(
        [
            (item_owner * rows + item_row[:, None])[:, 0],
            (action_owner * rows + action_row[:, None])[:, 0],
        ]
    ).astype(I32)

    keys = jnp.stack([keys, grid.over_pair(keys)])
    keys = jnp.stack([keys] + [grid.over_replica(keys, k) for k in range(1, replicas)])

    held = {0: own}
    for low in reversed([1 << i for i in range(line.bit_length() - 1)]):
        for k in range(low, line, 2 * low):
            held[k] = grid.over_line(held[k ^ low], low)
    order = sorted(held, key=lambda k: (bin(k).count("1"), k))

    key_cols = jnp.broadcast_to(keys[..., None], (*keys.shape, LANES))
    both = list(range(cores))

    found = ()
    for k in order[:-1]:
        found = fetch(bases[k], key_cols, both, held[k], found)
    last = order[-1]
    there = fetch(bases[last], key_cols, both[1:], held[last], found[1:])
    here = fetch(bases[last], key_cols, both[:1], held[last], found[:1])
    pieces = combine([here[0], grid.over_pair(there[0])])
    for k in swaps:
        pieces[k] = grid.over_replica(pieces[k], k)

    gain = input_norm_gain.reshape(1, width)
    layer_out, *rest = sequence(
        replica, core, pieces, cotangent, gain, w_proj, w_out, cores, line
    )
    tokens, (normed, dproj, gated, weights) = rest[:replicas], rest[replicas:]
    for k in swaps:
        tokens[k] = grid.over_replica(tokens[k], k)

    weights = grid.over_pair(weights)
    weights = weight_grad(replica, core, normed, dproj, gated, cotangent, weights, line)
    tokens = lax.optimization_barrier((tokens, weights))[0]
    tokens = pack(tokens)
    there = grid.over_pair(tokens)

    def swap_weights(weights, step):
        kept, sent = weights[0::2], weights[1::2]
        return kept, [grid.over_replica(sent[p], 1 << (p + step) % bits) for p in range(bits)]

    kept, swapped = swap_weights(weights, 0)

    sums, raw, both_there = {}, {}, [tokens, there]
    for k in reversed(order):
        low = (k & -k) or line
        steps = [1 << i for i in range(low.bit_length() - 1)]
        out = F32 if steps else BF16
        if k == last:
            first = gather_grad(bases[k], keys, both[:1], [tokens], rows)
            raw[k] = gather_grad(bases[k], keys, both[1:], [there], rows, first, out)
        else:
            if k == 1 and line > 2:
                both_there = lax.optimization_barrier((both_there, sums[line // 2]))[0]
            raw[k] = gather_grad(bases[k], keys, both, both_there, rows, out=out)
        came = [[grid.over_line(part, step) for part in sums[k ^ step]] for step in steps]
        if k == 0:
            whole = [parts[0] for parts in came if len(parts) == 1]
            halves = [part for parts in came if len(parts) == 2 for part in parts]
            item_grad, action_grad = table_sums(raw[k][0], whole, halves)
        else:
            sums[k] = [add_up(raw[k] + [parts[0] for parts in came])] if steps else raw[k]

    for step in range(1, bits + 1):
        after = raw[line // 2] if step < bits else sums[line // 2]
        swapped = lax.optimization_barrier((swapped, after))[0]
        if step < bits:
            kept, swapped = swap_weights(fold(replica, kept, swapped, step), step)
    parts = cut_line(place, kept, swapped, line)
    parts = [parts[0]] + [grid.over_line(parts[k], k) for k in range(1, line)]
    parts = lax.optimization_barrier((parts, item_grad))[0]
    total = add_up(parts)
    parts = [total] + [grid.over_replica(total, k) for k in range(1, replicas)]
    grad_proj, grad_out = assemble(replica, parts, 4 * width)

    return layer_out, item_grad, action_grad, grad_proj, grad_out


def solution(mesh):
    tokens = ("replica", "sparse")
    in_specs = (
        P("sparse", None),
        P("sparse", None),
        P(tokens, None),
        P(tokens),
        P(tokens, None),
        P(tokens),
        P(),
        P(),
        P(),
        P(tokens, None),
    )
    out_specs = (
        P(tokens, None),
        P("sparse", "replica"),
        P("sparse", "replica"),
        P("sparse", None),
        P("sparse", None),
    )
    return jax.shard_map(local, mesh=mesh, in_specs=in_specs, out_specs=out_specs, check_vma=False)
```

```python
import jax
import jax.numpy as jnp
from jax import lax
from jax.experimental import pallas as pl
from jax.experimental.pallas import tpu as pltpu
from jax.sharding import PartitionSpec as P

HEADS = 4
EPS = 1e-05
LANES = 128
F32 = jnp.float32
BF16 = jnp.bfloat16
I32 = jnp.int32
MIB = 1024 * 1024
EARLY = 6 * 10**9

NN = ((1,), (0,))
NT = ((1,), (1,))
TN = ((0,), (0,))


def dot(left, right, dims=NN):
    return lax.dot_general(left, right, (dims, ((), ())), preferred_element_type=F32)


def sigmoid(value):
    return 0.5 * jnp.tanh(0.5 * value) + 0.5


def run(name, body, outs, args, smem=0, scratch=(), vmem=16, flops=0):
    outs = [jax.ShapeDtypeStruct(shape, dtype) for shape, dtype in outs]
    size = sum(a.size * a.dtype.itemsize for a in [*args, *outs])
    in_smem = pl.BlockSpec(memory_space=pltpu.SMEM)
    in_vmem = pl.BlockSpec(memory_space=pltpu.VMEM)
    places = [in_smem] * smem + [in_vmem] * (len(args) - smem)
    results = pl.pallas_call(
        body,
        out_shape=outs,
        in_specs=places,
        out_specs=[in_vmem] * len(outs),
        scratch_shapes=list(scratch),
        compiler_params=pltpu.CompilerParams(vmem_limit_bytes=vmem * MIB),
        cost_estimate=pl.CostEstimate(flops=flops, bytes_accessed=size, transcendentals=0),
        name=name,
    )(*args)
    return list(results)


class Grid:
    def __init__(self):
        self.replicas = lax.axis_size("replica")
        self.shards = lax.axis_size("sparse")
        self.cores = 2 if self.shards % 2 == 0 else 1
        self.line = self.shards // self.cores
        self.r = lax.axis_index("replica")
        self.s = lax.axis_index("sparse")
        self.z = self.s // self.cores
        self.c = self.s % self.cores

    def over_replica(self, value, step):
        n = self.replicas
        return lax.ppermute(value, "replica", [(i, i ^ step) for i in range(n)])

    def over_line(self, value, step):
        pairs = [(i, i ^ step * self.cores) for i in range(self.shards)]
        return lax.ppermute(value, "sparse", pairs)

    def over_pair(self, value):
        return lax.ppermute(value, "sparse", [(i, i ^ 1) for i in range(self.shards)])


def fetch(base, keys, cohorts, chunk, before=()):
    many = len(cohorts)
    count, _, _, tokens, _ = keys.shape
    rows, cols = chunk.shape[0] // 2, chunk.shape[1]

    def body(base_ref, chunk_ref, key_ref, *refs):
        before_refs, out_refs = refs[:-many], refs[-many:]
        lane = lax.broadcasted_iota(I32, (tokens, LANES), 1)
        for i, m in enumerate(cohorts):
            for k in range(count):
                hot = []
                for table in range(2):
                    place = key_ref[k, m, table] - base_ref[0]
                    for start in range(0, rows, LANES):
                        hot.append(jnp.where(place == lane + start, 1.0, 0.0).astype(BF16))
                found = dot(jnp.concatenate(hot, axis=1), chunk_ref[...])
                if before_refs:
                    found = found + before_refs[i][k].astype(F32)
                out_refs[i][k] = found.astype(BF16)

    return run(
        "fetch",
        body,
        [((count, tokens, cols), BF16)] * many,
        [base, chunk, keys, *before],
        smem=1,
        flops=2 * many * count * tokens * rows * cols,
    )


def combine(parts):
    count, *shape = parts[0].shape

    def body(left_ref, right_ref, *out_refs):
        for k in range(count):
            total = left_ref[k].astype(F32) + right_ref[k].astype(F32)
            out_refs[k][...] = total.astype(BF16)

    return run("combine", body, [(tuple(shape), BF16)] * count, parts)


def pack(parts):
    def body(*refs):
        for k, ref in enumerate(refs[:-1]):
            refs[-1][k] = ref[...]

    shape, dtype = parts[0].shape, parts[0].dtype
    return run("pack", body, [((len(parts), *shape), dtype)], parts)[0]


def add_up(parts):
    def body(*refs):
        total = refs[0][...].astype(F32)
        for ref in refs[1:-1]:
            total = total + ref[...].astype(F32)
        refs[-1][...] = total.astype(BF16)

    return run("add_up", body, [(parts[0].shape, BF16)], parts)[0]


def table_sums(here, came, out, flops=0):
    rows, cols = here.shape[0] // 2, here.shape[1]
    cuts = 2 if out else 1

    def body(here_ref, *refs):
        came_refs, out_refs = refs[:-cuts], refs[-cuts:]
        for i in range(2):
            span = slice(i * rows, (i + 1) * rows)
            total = here_ref[span, :]
            for ref in came_refs:
                total = total + ref[span, :].astype(F32)
            if out:
                out_refs[i][...] = total
            else:
                out_refs[0][span, :] = total

    outs = [((2 * rows // cuts, cols), F32)] * cuts
    return run("table_sums", body, outs, [here, *came], flops=flops)


def gather_grad(base, keys, cohorts, tokens, rows, before=(), out=BF16):
    many = len(cohorts)
    count, _, _, length = keys.shape
    cols = tokens[0].shape[-1]

    def body(base_ref, key_ref, *refs):
        piece_refs, before_refs = refs[:many], refs[many : many + len(before)]
        out_ref = refs[-1]
        row = lax.broadcasted_iota(I32, (rows, length), 0)
        for table in range(2):
            span = slice(table * rows, (table + 1) * rows)
            sums = None
            for i, m in enumerate(cohorts):
                hot = []
                for k in range(count):
                    place = key_ref[k, m, table : table + 1, :] - base_ref[0]
                    hot.append(jnp.where(place == row, 1.0, 0.0).astype(BF16))
                piece = piece_refs[i][...].reshape(count * length, cols)
                part = dot(jnp.concatenate(hot, axis=1), piece)
                sums = part if sums is None else sums + part
            for ref in before_refs:
                sums = sums + ref[span, :].astype(F32)
            out_ref[span, :] = sums.astype(out)

    return run(
        "gather_grad",
        body,
        [((2 * rows, cols), out)],
        [base, keys, *tokens, *before],
        smem=1,
        flops=4 * many * count * length * 2 * rows * cols,
    )


def sequence(replica, core, pieces, cotangent, gain, w_proj, w_out, cores, line):
    count = len(pieces)
    length, width = cotangent.shape
    cols = width // count
    head_dim = width // HEADS
    factor = head_dim ** (-0.5)
    tile = min(256, length)
    step = min(256, 4 * width)

    def body(r_ref, core_ref, cot_ref, wo_ref, wp_ref, gain_ref, *refs):
        piece_refs, refs = refs[:count], refs[count:]
        out_ref, *grad_refs = refs[: count + 1]
        normed_ref, dproj_ref, gated_ref, weight_ref = refs[count + 1 : count + 5]
        emb, act, slope, att, attn, dscale, dkey, dval, tok = refs[count + 5 :]

        for k in range(count):
            emb[r_ref[0] ^ k] = piece_refs[k][...]

        def embedded(span):
            return jnp.concatenate([emb[k, span] for k in range(count)], axis=1).astype(F32)

        def norm_of(value):
            centred = value - jnp.mean(value, axis=-1, keepdims=True)
            scale = lax.rsqrt(jnp.mean(centred * centred, axis=-1, keepdims=True) + EPS)
            return centred * scale, scale

        def norm_back(upper, hat, scale):
            return scale * (
                upper
                - jnp.mean(upper, axis=-1, keepdims=True)
                - hat * jnp.mean(upper * hat, axis=-1, keepdims=True)
            )

        for at in range(0, length, tile):
            span = slice(at, at + tile)
            hat, _ = norm_of(embedded(span))
            normed_ref[span, :] = (hat * gain_ref[...]).astype(BF16)

        normed = normed_ref[...]

        @pl.loop(0, 4 * width // step)
        def _(j):
            span = pl.ds(pl.multiple_of(j * step, step), step)
            proj = dot(normed, wp_ref[:, span])
            sig = sigmoid(proj)
            act[:, span] = (proj * sig).astype(BF16)
            slope[:, span] = sig * (1.0 + proj * (1.0 - sig))

        dkey[...] = jnp.zeros_like(dkey)
        dval[...] = jnp.zeros_like(dval)

        for at in range(0, length, tile):
            span = slice(at, at + tile)
            seen = at + tile
            past = slice(0, seen)
            keep = lax.broadcasted_iota(I32, (tile, seen), 1) <= at + lax.broadcasted_iota(
                I32, (tile, seen), 0
            )
            for h in range(HEADS):
                head = [slice(p * width + h * head_dim, p * width + (h + 1) * head_dim) for p in range(4)]
                scores = dot(act[span, head[2]], act[past, head[3]], NT) * factor
                sig = sigmoid(scores)
                soft = jnp.where(keep, scores * sig * (1.0 / length), 0.0).astype(BF16)
                attn[h, :, :seen] = soft
                grad = sig * (1.0 + scores * (1.0 - sig)) * (factor / length)
                dscale[h, :, :seen] = jnp.where(keep, grad, 0.0)
                att[:, head[0]] = dot(soft, act[past, head[1]])
            hat, scale = norm_of(att[...])
            gate = act[span, :width].astype(F32)
            gated = (hat * gate).astype(BF16)
            gated_ref[span, :] = gated
            out_ref[span, :] = (embedded(span) + dot(gated, wo_ref[...])).astype(BF16)
            dgated = dot(cot_ref[span, :], wo_ref[...], NT)
            dproj_ref[span, :width] = (dgated * hat * slope[span, :width]).astype(BF16)
            datt = norm_back(dgated * gate, hat, scale).astype(BF16)
            for h in range(HEADS):
                head = [slice(p * width + h * head_dim, p * width + (h + 1) * head_dim) for p in range(4)]
                dhead = datt[:, head[0]]
                dattn = dot(dhead, act[past, head[1]], NT)
                dscores = (dattn * dscale[h, :, :seen]).astype(BF16)
                dquery = dot(dscores, act[past, head[3]])
                dproj_ref[span, head[2]] = (dquery * slope[span, head[2]]).astype(BF16)
                dkey[past, head[0]] += dot(dscores, act[span, head[2]], TN)
                dval[past, head[0]] += dot(attn[h, :, :seen], dhead, TN)

        dproj_ref[:, width : 2 * width] = (dval[...] * slope[:, width : 2 * width]).astype(BF16)
        dproj_ref[:, 3 * width :] = (dkey[...] * slope[:, 3 * width :]).astype(BF16)

        for at in range(0, length, tile):
            span = slice(at, at + tile)
            hat, scale = norm_of(embedded(span))
            upper = dot(dproj_ref[span, :], wp_ref[...], NT) * gain_ref[...]
            grad = cot_ref[span, :].astype(F32) + norm_back(upper, hat, scale)
            for k in range(count):
                tok[k, span] = grad[:, k * cols : (k + 1) * cols].astype(BF16)

        for k in range(count):
            grad_refs[k][...] = tok[r_ref[0] ^ k]

        other = (core_ref[0] + 1) % cores
        sums = weight_sums(other, normed_ref, dproj_ref, gated_ref, cot_ref, cores, line, count)
        for k in range(count):
            weight_ref[k] = next(sums).astype(BF16)

    return run(
        "sequence",
        body,
        [
            ((length, width), BF16),
            *[((length, cols), BF16)] * count,
            ((length, width), BF16),
            ((length, 4 * width), BF16),
            ((length, width), BF16),
            ((count, width // cores, 5 * width // count), BF16),
        ],
        [replica, core, cotangent, w_out, w_proj, gain, *pieces],
        smem=2,
        vmem=24,
        flops=32 * length * width * width,
        scratch=[
            pltpu.VMEM((count, length, cols), BF16),
            pltpu.VMEM((length, 4 * width), BF16),
            pltpu.VMEM((length, 4 * width), F32),
            pltpu.VMEM((tile, width), F32),
            pltpu.VMEM((HEADS, tile, length), BF16),
            pltpu.VMEM((HEADS, tile, length), F32),
            pltpu.VMEM((length, width), F32),
            pltpu.VMEM((length, width), F32),
            pltpu.VMEM((count, length, cols), BF16),
        ],
    )


def weight_sums(core, n_ref, d_ref, g_ref, c_ref, cores, line, blocks):
    length, width = n_ref.shape
    rows = width // (cores * line)
    half = width // cores
    edge = d_ref.shape[1]
    cols = (edge + c_ref.shape[1]) // blocks
    feature = lax.broadcasted_iota(I32, (width, half), 0)
    column = lax.broadcasted_iota(I32, (width, half), 1)
    wanted = (column // rows * cores + core) * rows + column % rows
    pick = jnp.where(feature == wanted, 1.0, 0.0).astype(BF16)
    n_part = dot(n_ref[...], pick).astype(BF16)
    g_part = dot(g_ref[...], pick).astype(BF16)
    for k in range(blocks):
        first, last = k * cols, (k + 1) * cols
        parts = []
        if first < edge:
            parts.append(dot(n_part, d_ref[:, first : min(last, edge)], TN))
        if last > edge:
            parts.append(dot(g_part, c_ref[:, max(first, edge) - edge : last - edge], TN))
        yield parts[0] if len(parts) == 1 else jnp.concatenate(parts, axis=1)


def weight_grad(replica, core, normed, dproj, gated, cotangent, before, line):
    blocks, half, cols = before.shape
    length, width = normed.shape
    cores = width // half
    bits = blocks.bit_length() - 1
    tall = half // bits

    def body(r_ref, core_ref, n_ref, d_ref, g_ref, c_ref, before_ref, *refs):
        out_refs, scratch = refs[:-1], refs[-1]
        sums = weight_sums(core_ref[0], n_ref, d_ref, g_ref, c_ref, cores, line, blocks)
        for k in range(blocks):
            total = next(sums) + before_ref[k].astype(F32)
            for p in range(bits):
                at = sum((k >> (p + i) % bits & 1) << bits - 1 - i for i in range(bits))
                scratch[p, at] = total[p * tall : (p + 1) * tall]
        for p in range(bits):
            split_halves(scratch.at[p], r_ref[0] >> p & 1, out_refs[2 * p : 2 * p + 2])

    kept = (blocks // 2, tall, cols)
    return run(
        "weight_grad",
        body,
        [(kept, F32), (kept, BF16)] * bits,
        [replica, core, normed, dproj, gated, cotangent, before],
        smem=2,
        scratch=[pltpu.VMEM((bits, blocks, tall, cols), F32)],
        flops=2 * length * half * (blocks * cols + 2 * width),
    )


def split_halves(ref, bit, out_refs):
    count = ref.shape[0] // 2
    for i, out_ref in enumerate(out_refs):
        start = (bit ^ i) * count
        for k in range(count):
            out_ref[k] = ref[start + k].astype(out_ref.dtype)


def fold(replica, kept, came, step):
    count, tall, cols = kept[0].shape
    many = len(kept)

    def body(r_ref, *refs):
        kept_refs, came_refs, out_refs = refs[:many], refs[many : 2 * many], refs[2 * many : -1]
        scratch = refs[-1]
        for p in range(many):
            for k in range(count):
                scratch[p, k] = kept_refs[p][k] + came_refs[p][k].astype(F32)
            split_halves(scratch.at[p], r_ref[0] >> (p + step) % many & 1, out_refs[2 * p : 2 * p + 2])

    half = (count // 2, tall, cols)
    return run(
        "fold",
        body,
        [(half, F32), (half, BF16)] * many,
        [replica, *kept, *came],
        smem=1,
        scratch=[pltpu.VMEM((many, count, tall, cols), F32)],
    )


def cut_line(place, kept, came, line):
    _, tall, cols = kept[0].shape
    many = len(kept)
    rows = many * tall // line

    def body(place_ref, *refs):
        kept_refs, came_refs, out_refs = refs[:many], refs[many : 2 * many], refs[2 * many : -1]
        scratch = refs[-1]
        for p in range(many):
            scratch[p * tall : (p + 1) * tall] = kept_refs[p][0] + came_refs[p][0].astype(F32)
        for k in range(line):
            span = pl.ds(pl.multiple_of((place_ref[0] ^ k) * rows, rows), rows)
            out_refs[k % 2][k // 2] = scratch[span].astype(out_refs[k % 2].dtype)

    half = (line // 2, rows, cols)
    return run(
        "cut_line",
        body,
        [(half, F32), (half, BF16)],
        [place, *kept, *came],
        smem=1,
        scratch=[pltpu.VMEM((many * tall, cols), F32)],
    )


def fold_line(kept, came):
    count, rows, cols = kept.shape

    def body(kept_ref, came_ref, *out_refs):
        for k in range(count):
            total = kept_ref[k] + came_ref[k].astype(F32)
            out_refs[k % 2][k // 2] = total.astype(out_refs[k % 2].dtype)

    half = (count // 2, rows, cols)
    return run("fold_line", body, [(half, F32), (half, BF16)], [kept, came])


def assemble(replica, parts, edge):
    rows, cols = parts[0].shape
    total = cols * len(parts)

    def body(r_ref, *refs):
        part_refs, (left_ref, right_ref, held) = refs[: len(parts)], refs[len(parts) :]
        for k, ref in enumerate(part_refs):
            held[r_ref[0] ^ k] = ref[...].astype(F32)
        for k in range(len(parts)):
            first, last = k * cols, (k + 1) * cols
            cut = min(max(edge - first, 0), cols)
            if cut > 0:
                left_ref[:, first : first + cut] = held[k, :, :cut]
            if cut < cols:
                right_ref[:, first + cut - edge : last - edge] = held[k, :, cut:]

    return run(
        "assemble",
        body,
        [((rows, edge), F32), ((rows, total - edge), F32)],
        [replica, *parts],
        smem=1,
        scratch=[pltpu.VMEM((len(parts), rows, cols), F32)],
    )


def local(
    item_table,
    action_table,
    item_owner,
    item_row,
    action_owner,
    action_row,
    input_norm_gain,
    w_proj,
    w_out,
    cotangent,
):
    grid = Grid()
    rows, width = item_table.shape
    replicas, line, cores = grid.replicas, grid.line, grid.cores
    cols = width // replicas

    bits = replicas.bit_length() - 1
    swaps = [3, 1, 2] if replicas == 4 else list(range(1, replicas))
    replica, place, core = (i.astype(I32).reshape(1) for i in (grid.r, grid.z, grid.c))
    bases = [((place ^ k) * cores + core) * rows for k in range(line)]

    own = jnp.concatenate(
        [
            lax.dynamic_slice_in_dim(item_table, grid.r * cols, cols, 1),
            lax.dynamic_slice_in_dim(action_table, grid.r * cols, cols, 1),
        ],
        axis=0,
    )
    keys = jnp.stack(
        [
            (item_owner * rows + item_row[:, None])[:, 0],
            (action_owner * rows + action_row[:, None])[:, 0],
        ]
    ).astype(I32)

    keys = jnp.stack([keys, grid.over_pair(keys)])
    keys = jnp.stack([keys] + [grid.over_replica(keys, k) for k in range(1, replicas)])

    held = {0: own}
    for low in reversed([1 << i for i in range(line.bit_length() - 1)]):
        for k in range(low, line, 2 * low):
            held[k] = grid.over_line(held[k ^ low], low)
    order = sorted(held, key=lambda k: (bin(k).count("1"), k))

    key_cols = jnp.broadcast_to(keys[..., None], (*keys.shape, LANES))
    both = list(range(cores))

    found = ()
    for k in order[:-1]:
        found = fetch(bases[k], key_cols, both, held[k], found)
    last = order[-1]
    there = fetch(bases[last], key_cols, both[1:], held[last], found[1:])
    here = fetch(bases[last], key_cols, both[:1], held[last], found[:1])
    pieces = combine([here[0], grid.over_pair(there[0])])
    for k in swaps:
        pieces[k] = grid.over_replica(pieces[k], k)

    gain = input_norm_gain.reshape(1, width)
    layer_out, *rest = sequence(
        replica, core, pieces, cotangent, gain, w_proj, w_out, cores, line
    )
    tokens, (normed, dproj, gated, weights) = rest[:replicas], rest[replicas:]
    for k in swaps:
        tokens[k] = grid.over_replica(tokens[k], k)

    weights = grid.over_pair(weights)
    weights = weight_grad(replica, core, normed, dproj, gated, cotangent, weights, line)
    tokens = lax.optimization_barrier((tokens, weights))[0]
    tokens = pack(tokens)
    there = grid.over_pair(tokens)

    def swap_weights(weights, step):
        kept, sent = weights[0::2], weights[1::2]
        return kept, [grid.over_replica(sent[p], 1 << (p + step) % bits) for p in range(bits)]

    kept, swapped = swap_weights(weights, 0)

    sums, raw, both_there = {}, {}, [tokens, there]
    for k in reversed(order):
        low = (k & -k) or line
        steps = [1 << i for i in range(low.bit_length() - 1)]
        out = F32 if steps else BF16
        if k == last:
            first = gather_grad(bases[k], keys, both[:1], [tokens], rows)
            raw[k] = gather_grad(bases[k], keys, both[1:], [there], rows, first, out)
        else:
            if k == 1 and line > 2:
                both_there = lax.optimization_barrier((both_there, sums[line // 2]))[0]
            raw[k] = gather_grad(bases[k], keys, both, both_there, rows, out=out)
        came = [grid.over_line(sums[k ^ step], step) for step in steps]
        if k == 0:
            table = raw[k]
            if len(came) > 1:
                table = table_sums(table[0], came[1:], out=False, flops=EARLY)
            item_grad, action_grad = table_sums(table[0], came[:1], out=True)
        else:
            sums[k] = add_up(raw[k] + came) if steps else raw[k][0]

    for step in range(1, bits + 1):
        after = raw[line // 2] if step < bits else sums[line // 2]
        swapped = lax.optimization_barrier((swapped, after))[0]
        if step < bits:
            kept, swapped = swap_weights(fold(replica, kept, swapped, step), step)
    kept, sent = cut_line(place, kept, swapped, line)
    step = 1
    while step < line // 2:
        kept, sent = fold_line(kept, grid.over_line(sent, step))
        step *= 2
    parts = [kept[0], grid.over_line(sent, step)[0]]
    parts = lax.optimization_barrier((parts, item_grad))[0]
    total = add_up(parts)
    parts = [total] + [grid.over_replica(total, k) for k in range(1, replicas)]
    grad_proj, grad_out = assemble(replica, parts, 4 * width)

    return layer_out, item_grad, action_grad, grad_proj, grad_out


def solution(mesh):
    tokens = ("replica", "sparse")
    in_specs = (
        P("sparse", None),
        P("sparse", None),
        P(tokens, None),
        P(tokens),
        P(tokens, None),
        P(tokens),
        P(),
        P(),
        P(),
        P(tokens, None),
    )
    out_specs = (
        P(tokens, None),
        P("sparse", "replica"),
        P("sparse", "replica"),
        P("sparse", None),
        P("sparse", None),
    )
    return jax.shard_map(local, mesh=mesh, in_specs=in_specs, out_specs=out_specs, check_vma=False)
```

```python
import jax
import jax.numpy as jnp
from jax import lax
from jax.experimental import pallas as pl
from jax.experimental.pallas import tpu as pltpu
from jax.sharding import PartitionSpec as P

HEADS = 4
EPS = 1e-05
LANES = 128
F32 = jnp.float32
BF16 = jnp.bfloat16
I32 = jnp.int32
MIB = 1024 * 1024
EARLY = 6 * 10**9

NN = ((1,), (0,))
NT = ((1,), (1,))
TN = ((0,), (0,))


def dot(left, right, dims=NN):
    return lax.dot_general(left, right, (dims, ((), ())), preferred_element_type=F32)


def sigmoid(value):
    return 0.5 * jnp.tanh(0.5 * value) + 0.5


def run(name, body, outs, args, smem=0, scratch=(), vmem=16, flops=0):
    outs = [jax.ShapeDtypeStruct(shape, dtype) for shape, dtype in outs]
    size = sum(a.size * a.dtype.itemsize for a in [*args, *outs])
    in_smem = pl.BlockSpec(memory_space=pltpu.SMEM)
    in_vmem = pl.BlockSpec(memory_space=pltpu.VMEM)
    places = [in_smem] * smem + [in_vmem] * (len(args) - smem)
    results = pl.pallas_call(
        body,
        out_shape=outs,
        in_specs=places,
        out_specs=[in_vmem] * len(outs),
        scratch_shapes=list(scratch),
        compiler_params=pltpu.CompilerParams(vmem_limit_bytes=vmem * MIB),
        cost_estimate=pl.CostEstimate(flops=flops, bytes_accessed=size, transcendentals=0),
        name=name,
    )(*args)
    return list(results)


class Grid:
    def __init__(self):
        self.replicas = lax.axis_size("replica")
        self.shards = lax.axis_size("sparse")
        self.cores = 2 if self.shards % 2 == 0 else 1
        self.line = self.shards // self.cores
        self.r = lax.axis_index("replica")
        self.s = lax.axis_index("sparse")
        self.z = self.s // self.cores
        self.c = self.s % self.cores

    def over_replica(self, value, step):
        n = self.replicas
        return lax.ppermute(value, "replica", [(i, i ^ step) for i in range(n)])

    def swap_replica(self, value):
        return lax.all_to_all(value, "replica", split_axis=0, concat_axis=0, tiled=True)

    def over_line(self, value, step):
        pairs = [(i, i ^ step * self.cores) for i in range(self.shards)]
        return lax.ppermute(value, "sparse", pairs)

    def over_pair(self, value):
        return lax.ppermute(value, "sparse", [(i, i ^ 1) for i in range(self.shards)])


def fetch(base, keys, cohorts, chunk, before=()):
    many = len(cohorts)
    count, _, _, tokens, _ = keys.shape
    rows, cols = chunk.shape[0] // 2, chunk.shape[1]

    def body(base_ref, chunk_ref, key_ref, *refs):
        before_refs, out_refs = refs[:-many], refs[-many:]
        lane = lax.broadcasted_iota(I32, (tokens, LANES), 1)
        for i, m in enumerate(cohorts):
            for k in range(count):
                hot = []
                for table in range(2):
                    place = key_ref[k, m, table] - base_ref[0]
                    for start in range(0, rows, LANES):
                        hot.append(jnp.where(place == lane + start, 1.0, 0.0).astype(BF16))
                found = dot(jnp.concatenate(hot, axis=1), chunk_ref[...])
                if before_refs:
                    found = found + before_refs[i][k].astype(F32)
                out_refs[i][k] = found.astype(BF16)

    return run(
        "fetch",
        body,
        [((count, tokens, cols), BF16)] * many,
        [base, chunk, keys, *before],
        smem=1,
        flops=2 * many * count * tokens * rows * cols,
    )


def combine(parts):
    count, *shape = parts[0].shape

    def body(left_ref, right_ref, *out_refs):
        for k in range(count):
            total = left_ref[k].astype(F32) + right_ref[k].astype(F32)
            out_refs[k][...] = total.astype(BF16)

    return run("combine", body, [(tuple(shape), BF16)] * count, parts)


def pack(parts):
    def body(*refs):
        for k, ref in enumerate(refs[:-1]):
            refs[-1][k] = ref[...]

    shape, dtype = parts[0].shape, parts[0].dtype
    return run("pack", body, [((len(parts), *shape), dtype)], parts)[0]


def add_up(parts):
    def body(*refs):
        total = refs[0][...].astype(F32)
        for ref in refs[1:-1]:
            total = total + ref[...].astype(F32)
        refs[-1][...] = total.astype(BF16)

    return run("add_up", body, [(parts[0].shape, BF16)], parts)[0]


def table_sums(here, came, out, flops=0):
    rows, cols = here.shape[0] // 2, here.shape[1]
    cuts = 2 if out else 1

    def body(here_ref, *refs):
        came_refs, out_refs = refs[:-cuts], refs[-cuts:]
        for i in range(2):
            span = slice(i * rows, (i + 1) * rows)
            total = here_ref[span, :]
            for ref in came_refs:
                total = total + ref[span, :].astype(F32)
            if out:
                out_refs[i][...] = total
            else:
                out_refs[0][span, :] = total

    outs = [((2 * rows // cuts, cols), F32)] * cuts
    return run("table_sums", body, outs, [here, *came], flops=flops)


def gather_grad(base, keys, cohorts, tokens, rows, before=(), out=BF16):
    many = len(cohorts)
    count, _, _, length = keys.shape
    cols = tokens[0].shape[-1]

    def body(base_ref, key_ref, *refs):
        piece_refs, before_refs = refs[:many], refs[many : many + len(before)]
        out_ref = refs[-1]
        row = lax.broadcasted_iota(I32, (rows, length), 0)
        for table in range(2):
            span = slice(table * rows, (table + 1) * rows)
            sums = None
            for i, m in enumerate(cohorts):
                hot = []
                for k in range(count):
                    place = key_ref[k, m, table : table + 1, :] - base_ref[0]
                    hot.append(jnp.where(place == row, 1.0, 0.0).astype(BF16))
                piece = piece_refs[i][...].reshape(count * length, cols)
                part = dot(jnp.concatenate(hot, axis=1), piece)
                sums = part if sums is None else sums + part
            for ref in before_refs:
                sums = sums + ref[span, :].astype(F32)
            out_ref[span, :] = sums.astype(out)

    return run(
        "gather_grad",
        body,
        [((2 * rows, cols), out)],
        [base, keys, *tokens, *before],
        smem=1,
        flops=4 * many * count * length * 2 * rows * cols,
    )


def sequence(replica, core, pieces, cotangent, gain, w_proj, w_out, cores, line):
    count = len(pieces)
    length, width = cotangent.shape
    cols = width // count
    head_dim = width // HEADS
    factor = head_dim ** (-0.5)
    tile = min(256, length)
    step = min(256, 4 * width)

    def body(r_ref, core_ref, cot_ref, wo_ref, wp_ref, gain_ref, *refs):
        piece_refs, refs = refs[:count], refs[count:]
        out_ref, *grad_refs = refs[: count + 1]
        normed_ref, dproj_ref, gated_ref, weight_ref = refs[count + 1 : count + 5]
        emb, act, slope, att, attn, dscale, dkey, dval, tok = refs[count + 5 :]

        for k in range(count):
            emb[r_ref[0] ^ k] = piece_refs[k][...]

        def embedded(span):
            return jnp.concatenate([emb[k, span] for k in range(count)], axis=1).astype(F32)

        def norm_of(value):
            centred = value - jnp.mean(value, axis=-1, keepdims=True)
            scale = lax.rsqrt(jnp.mean(centred * centred, axis=-1, keepdims=True) + EPS)
            return centred * scale, scale

        def norm_back(upper, hat, scale):
            return scale * (
                upper
                - jnp.mean(upper, axis=-1, keepdims=True)
                - hat * jnp.mean(upper * hat, axis=-1, keepdims=True)
            )

        for at in range(0, length, tile):
            span = slice(at, at + tile)
            hat, _ = norm_of(embedded(span))
            normed_ref[span, :] = (hat * gain_ref[...]).astype(BF16)

        normed = normed_ref[...]

        @pl.loop(0, 4 * width // step)
        def _(j):
            span = pl.ds(pl.multiple_of(j * step, step), step)
            proj = dot(normed, wp_ref[:, span])
            sig = sigmoid(proj)
            act[:, span] = (proj * sig).astype(BF16)
            slope[:, span] = sig * (1.0 + proj * (1.0 - sig))

        dkey[...] = jnp.zeros_like(dkey)
        dval[...] = jnp.zeros_like(dval)

        for at in range(0, length, tile):
            span = slice(at, at + tile)
            seen = at + tile
            past = slice(0, seen)
            keep = lax.broadcasted_iota(I32, (tile, seen), 1) <= at + lax.broadcasted_iota(
                I32, (tile, seen), 0
            )
            for h in range(HEADS):
                head = [slice(p * width + h * head_dim, p * width + (h + 1) * head_dim) for p in range(4)]
                scores = dot(act[span, head[2]], act[past, head[3]], NT) * factor
                sig = sigmoid(scores)
                soft = jnp.where(keep, scores * sig * (1.0 / length), 0.0).astype(BF16)
                attn[h, :, :seen] = soft
                grad = sig * (1.0 + scores * (1.0 - sig)) * (factor / length)
                dscale[h, :, :seen] = jnp.where(keep, grad, 0.0)
                att[:, head[0]] = dot(soft, act[past, head[1]])
            hat, scale = norm_of(att[...])
            gate = act[span, :width].astype(F32)
            gated = (hat * gate).astype(BF16)
            gated_ref[span, :] = gated
            out_ref[span, :] = (embedded(span) + dot(gated, wo_ref[...])).astype(BF16)
            dgated = dot(cot_ref[span, :], wo_ref[...], NT)
            dproj_ref[span, :width] = (dgated * hat * slope[span, :width]).astype(BF16)
            datt = norm_back(dgated * gate, hat, scale).astype(BF16)
            for h in range(HEADS):
                head = [slice(p * width + h * head_dim, p * width + (h + 1) * head_dim) for p in range(4)]
                dhead = datt[:, head[0]]
                dattn = dot(dhead, act[past, head[1]], NT)
                dscores = (dattn * dscale[h, :, :seen]).astype(BF16)
                dquery = dot(dscores, act[past, head[3]])
                dproj_ref[span, head[2]] = (dquery * slope[span, head[2]]).astype(BF16)
                dkey[past, head[0]] += dot(dscores, act[span, head[2]], TN)
                dval[past, head[0]] += dot(attn[h, :, :seen], dhead, TN)

        dproj_ref[:, width : 2 * width] = (dval[...] * slope[:, width : 2 * width]).astype(BF16)
        dproj_ref[:, 3 * width :] = (dkey[...] * slope[:, 3 * width :]).astype(BF16)

        for at in range(0, length, tile):
            span = slice(at, at + tile)
            hat, scale = norm_of(embedded(span))
            upper = dot(dproj_ref[span, :], wp_ref[...], NT) * gain_ref[...]
            grad = cot_ref[span, :].astype(F32) + norm_back(upper, hat, scale)
            for k in range(count):
                tok[k, span] = grad[:, k * cols : (k + 1) * cols].astype(BF16)

        for k in range(count):
            grad_refs[k][...] = tok[r_ref[0] ^ k]

        other = (core_ref[0] + 1) % cores
        sums = weight_sums(other, normed_ref, dproj_ref, gated_ref, cot_ref, cores, line, count)
        for k in range(count):
            weight_ref[k] = next(sums).astype(BF16)

    return run(
        "sequence",
        body,
        [
            ((length, width), BF16),
            *[((length, cols), BF16)] * count,
            ((length, width), BF16),
            ((length, 4 * width), BF16),
            ((length, width), BF16),
            ((count, width // cores, 5 * width // count), BF16),
        ],
        [replica, core, cotangent, w_out, w_proj, gain, *pieces],
        smem=2,
        vmem=24,
        flops=32 * length * width * width,
        scratch=[
            pltpu.VMEM((count, length, cols), BF16),
            pltpu.VMEM((length, 4 * width), BF16),
            pltpu.VMEM((length, 4 * width), F32),
            pltpu.VMEM((tile, width), F32),
            pltpu.VMEM((HEADS, tile, length), BF16),
            pltpu.VMEM((HEADS, tile, length), F32),
            pltpu.VMEM((length, width), F32),
            pltpu.VMEM((length, width), F32),
            pltpu.VMEM((count, length, cols), BF16),
        ],
    )


def weight_sums(core, n_ref, d_ref, g_ref, c_ref, cores, line, blocks):
    length, width = n_ref.shape
    rows = width // (cores * line)
    half = width // cores
    edge = d_ref.shape[1]
    cols = (edge + c_ref.shape[1]) // blocks
    feature = lax.broadcasted_iota(I32, (width, half), 0)
    column = lax.broadcasted_iota(I32, (width, half), 1)
    wanted = (column // rows * cores + core) * rows + column % rows
    pick = jnp.where(feature == wanted, 1.0, 0.0).astype(BF16)
    n_part = dot(n_ref[...], pick).astype(BF16)
    g_part = dot(g_ref[...], pick).astype(BF16)
    for k in range(blocks):
        first, last = k * cols, (k + 1) * cols
        parts = []
        if first < edge:
            parts.append(dot(n_part, d_ref[:, first : min(last, edge)], TN))
        if last > edge:
            parts.append(dot(g_part, c_ref[:, max(first, edge) - edge : last - edge], TN))
        yield parts[0] if len(parts) == 1 else jnp.concatenate(parts, axis=1)


def weight_grad(core, normed, dproj, gated, cotangent, before, line):
    blocks, half, cols = before.shape
    length, width = normed.shape
    cores = width // half

    def body(core_ref, n_ref, d_ref, g_ref, c_ref, before_ref, out_ref):
        sums = weight_sums(core_ref[0], n_ref, d_ref, g_ref, c_ref, cores, line, blocks)
        for k in range(blocks):
            out_ref[k] = (next(sums) + before_ref[k].astype(F32)).astype(BF16)

    return run(
        "weight_grad",
        body,
        [(before.shape, BF16)],
        [core, normed, dproj, gated, cotangent, before],
        smem=1,
        flops=2 * length * half * (blocks * cols + 2 * width),
    )[0]


def cut_line(place, parts, line):
    count, tall, cols = parts.shape
    rows = tall // line

    def body(place_ref, part_ref, *refs):
        out_refs, scratch = refs[:2], refs[2]
        total = part_ref[0].astype(F32)
        for k in range(1, count):
            total = total + part_ref[k].astype(F32)
        scratch[...] = total
        for k in range(line):
            span = pl.ds(pl.multiple_of((place_ref[0] ^ k) * rows, rows), rows)
            out_refs[k % 2][k // 2] = scratch[span].astype(out_refs[k % 2].dtype)

    half = (line // 2, rows, cols)
    return run(
        "cut_line",
        body,
        [(half, F32), (half, BF16)],
        [place, parts],
        smem=1,
        scratch=[pltpu.VMEM((tall, cols), F32)],
    )


def fold_line(kept, came):
    count, rows, cols = kept.shape

    def body(kept_ref, came_ref, *out_refs):
        for k in range(count):
            total = kept_ref[k] + came_ref[k].astype(F32)
            out_refs[k % 2][k // 2] = total.astype(out_refs[k % 2].dtype)

    half = (count // 2, rows, cols)
    return run("fold_line", body, [(half, F32), (half, BF16)], [kept, came])


def assemble(replica, parts, edge):
    rows, cols = parts[0].shape
    total = cols * len(parts)

    def body(r_ref, *refs):
        part_refs, (left_ref, right_ref, held) = refs[: len(parts)], refs[len(parts) :]
        for k, ref in enumerate(part_refs):
            held[r_ref[0] ^ k] = ref[...].astype(F32)
        for k in range(len(parts)):
            first, last = k * cols, (k + 1) * cols
            cut = min(max(edge - first, 0), cols)
            if cut > 0:
                left_ref[:, first : first + cut] = held[k, :, :cut]
            if cut < cols:
                right_ref[:, first + cut - edge : last - edge] = held[k, :, cut:]

    return run(
        "assemble",
        body,
        [((rows, edge), F32), ((rows, total - edge), F32)],
        [replica, *parts],
        smem=1,
        scratch=[pltpu.VMEM((len(parts), rows, cols), F32)],
    )


def local(
    item_table,
    action_table,
    item_owner,
    item_row,
    action_owner,
    action_row,
    input_norm_gain,
    w_proj,
    w_out,
    cotangent,
):
    grid = Grid()
    rows, width = item_table.shape
    replicas, line, cores = grid.replicas, grid.line, grid.cores
    cols = width // replicas

    swaps = [3, 1, 2] if replicas == 4 else list(range(1, replicas))
    replica, place, core = (i.astype(I32).reshape(1) for i in (grid.r, grid.z, grid.c))
    bases = [((place ^ k) * cores + core) * rows for k in range(line)]

    own = jnp.concatenate(
        [
            lax.dynamic_slice_in_dim(item_table, grid.r * cols, cols, 1),
            lax.dynamic_slice_in_dim(action_table, grid.r * cols, cols, 1),
        ],
        axis=0,
    )
    keys = jnp.stack(
        [
            (item_owner * rows + item_row[:, None])[:, 0],
            (action_owner * rows + action_row[:, None])[:, 0],
        ]
    ).astype(I32)

    keys = jnp.stack([keys, grid.over_pair(keys)])
    keys = jnp.stack([keys] + [grid.over_replica(keys, k) for k in range(1, replicas)])

    held = {0: own}
    for low in reversed([1 << i for i in range(line.bit_length() - 1)]):
        for k in range(low, line, 2 * low):
            held[k] = grid.over_line(held[k ^ low], low)
    order = sorted(held, key=lambda k: (bin(k).count("1"), k))

    key_cols = jnp.broadcast_to(keys[..., None], (*keys.shape, LANES))
    both = list(range(cores))

    found = ()
    for k in order[:-1]:
        found = fetch(bases[k], key_cols, both, held[k], found)
    last = order[-1]
    there = fetch(bases[last], key_cols, both[1:], held[last], found[1:])
    here = fetch(bases[last], key_cols, both[:1], held[last], found[:1])
    pieces = combine([here[0], grid.over_pair(there[0])])
    for k in swaps:
        pieces[k] = grid.over_replica(pieces[k], k)

    gain = input_norm_gain.reshape(1, width)
    layer_out, *rest = sequence(
        replica, core, pieces, cotangent, gain, w_proj, w_out, cores, line
    )
    tokens, (normed, dproj, gated, weights) = rest[:replicas], rest[replicas:]
    for k in swaps:
        tokens[k] = grid.over_replica(tokens[k], k)

    weights = grid.over_pair(weights)
    weights = weight_grad(core, normed, dproj, gated, cotangent, weights, line)
    tokens = lax.optimization_barrier((tokens, weights))[0]
    tokens = pack(tokens)
    there = grid.over_pair(tokens)

    weights = grid.swap_replica(weights)

    sums, raw, both_there = {}, {}, [tokens, there]
    for k in reversed(order):
        low = (k & -k) or line
        steps = [1 << i for i in range(low.bit_length() - 1)]
        out = F32 if steps else BF16
        if k == last:
            first = gather_grad(bases[k], keys, both[:1], [tokens], rows)
            raw[k] = gather_grad(bases[k], keys, both[1:], [there], rows, first, out)
        else:
            if k == 1 and line > 2:
                both_there = lax.optimization_barrier((both_there, sums[line // 2]))[0]
            raw[k] = gather_grad(bases[k], keys, both, both_there, rows, out=out)
        came = [grid.over_line(sums[k ^ step], step) for step in steps]
        if k == 0:
            table = raw[k]
            if len(came) > 1:
                table = table_sums(table[0], came[1:], out=False, flops=EARLY)
            item_grad, action_grad = table_sums(table[0], came[:1], out=True)
        else:
            sums[k] = add_up(raw[k] + came) if steps else raw[k][0]

    weights = lax.optimization_barrier((weights, sums[line // 2]))[0]
    kept, sent = cut_line(place, weights, line)
    step = 1
    while step < line // 2:
        kept, sent = fold_line(kept, grid.over_line(sent, step))
        step *= 2
    parts = [kept[0], grid.over_line(sent, step)[0]]
    parts = lax.optimization_barrier((parts, item_grad))[0]
    total = add_up(parts)
    parts = [total] + [grid.over_replica(total, k) for k in range(1, replicas)]
    grad_proj, grad_out = assemble(replica, parts, 4 * width)

    return layer_out, item_grad, action_grad, grad_proj, grad_out


def solution(mesh):
    tokens = ("replica", "sparse")
    in_specs = (
        P("sparse", None),
        P("sparse", None),
        P(tokens, None),
        P(tokens),
        P(tokens, None),
        P(tokens),
        P(),
        P(),
        P(),
        P(tokens, None),
    )
    out_specs = (
        P(tokens, None),
        P("sparse", "replica"),
        P("sparse", "replica"),
        P("sparse", None),
        P("sparse", None),
    )
    return jax.shard_map(local, mesh=mesh, in_specs=in_specs, out_specs=out_specs, check_vma=False)
```

```python
import jax
import jax.numpy as jnp
from jax import lax
from jax.experimental import pallas as pl
from jax.experimental.pallas import tpu as pltpu
from jax.sharding import PartitionSpec as P

HEADS = 4
EPS = 1e-05
LANES = 128
F32 = jnp.float32
BF16 = jnp.bfloat16
I32 = jnp.int32
MIB = 1024 * 1024
EARLY = 6 * 10**9

NN = ((1,), (0,))
NT = ((1,), (1,))
TN = ((0,), (0,))


def dot(left, right, dims=NN):
    return lax.dot_general(left, right, (dims, ((), ())), preferred_element_type=F32)


def sigmoid(value):
    return 0.5 * jnp.tanh(0.5 * value) + 0.5


def run(name, body, outs, args, smem=0, scratch=(), vmem=16, flops=0):
    outs = [jax.ShapeDtypeStruct(shape, dtype) for shape, dtype in outs]
    size = sum(a.size * a.dtype.itemsize for a in [*args, *outs])
    in_smem = pl.BlockSpec(memory_space=pltpu.SMEM)
    in_vmem = pl.BlockSpec(memory_space=pltpu.VMEM)
    places = [in_smem] * smem + [in_vmem] * (len(args) - smem)
    results = pl.pallas_call(
        body,
        out_shape=outs,
        in_specs=places,
        out_specs=[in_vmem] * len(outs),
        scratch_shapes=list(scratch),
        compiler_params=pltpu.CompilerParams(vmem_limit_bytes=vmem * MIB),
        cost_estimate=pl.CostEstimate(flops=flops, bytes_accessed=size, transcendentals=0),
        name=name,
    )(*args)
    return list(results)


class Grid:
    def __init__(self):
        self.replicas = lax.axis_size("replica")
        self.shards = lax.axis_size("sparse")
        self.cores = 2 if self.shards % 2 == 0 else 1
        self.line = self.shards // self.cores
        self.r = lax.axis_index("replica")
        self.s = lax.axis_index("sparse")
        self.z = self.s // self.cores
        self.c = self.s % self.cores

    def over_replica(self, value, step):
        n = self.replicas
        return lax.ppermute(value, "replica", [(i, i ^ step) for i in range(n)])

    def over_line(self, value, step):
        pairs = [(i, i ^ step * self.cores) for i in range(self.shards)]
        return lax.ppermute(value, "sparse", pairs)

    def over_pair(self, value):
        return lax.ppermute(value, "sparse", [(i, i ^ 1) for i in range(self.shards)])


def fetch(base, keys, cohorts, chunk, before=()):
    many = len(cohorts)
    count, _, _, tokens, _ = keys.shape
    rows, cols = chunk.shape[0] // 2, chunk.shape[1]

    def body(base_ref, chunk_ref, key_ref, *refs):
        before_refs, out_refs = refs[:-many], refs[-many:]
        lane = lax.broadcasted_iota(I32, (tokens, LANES), 1)
        for i, m in enumerate(cohorts):
            for k in range(count):
                hot = []
                for table in range(2):
                    place = key_ref[k, m, table] - base_ref[0]
                    for start in range(0, rows, LANES):
                        hot.append(jnp.where(place == lane + start, 1.0, 0.0).astype(BF16))
                found = dot(jnp.concatenate(hot, axis=1), chunk_ref[...])
                if before_refs:
                    found = found + before_refs[i][k].astype(F32)
                out_refs[i][k] = found.astype(BF16)

    return run(
        "fetch",
        body,
        [((count, tokens, cols), BF16)] * many,
        [base, chunk, keys, *before],
        smem=1,
        flops=2 * many * count * tokens * rows * cols,
    )


def combine(parts):
    count, *shape = parts[0].shape

    def body(left_ref, right_ref, *out_refs):
        for k in range(count):
            total = left_ref[k].astype(F32) + right_ref[k].astype(F32)
            out_refs[k][...] = total.astype(BF16)

    return run("combine", body, [(tuple(shape), BF16)] * count, parts)


def pack(parts):
    def body(*refs):
        for k, ref in enumerate(refs[:-1]):
            refs[-1][k] = ref[...]

    shape, dtype = parts[0].shape, parts[0].dtype
    return run("pack", body, [((len(parts), *shape), dtype)], parts)[0]


def add_up(parts):
    def body(*refs):
        total = refs[0][...].astype(F32)
        for ref in refs[1:-1]:
            total = total + ref[...].astype(F32)
        refs[-1][...] = total.astype(BF16)

    return run("add_up", body, [(parts[0].shape, BF16)], parts)[0]


def table_sums(here, came, cuts):
    rows, cols = here.shape[0] // cuts, here.shape[1]

    def body(here_ref, came_ref, *out_refs):
        for i in range(cuts):
            span = slice(i * rows, (i + 1) * rows)
            out_refs[i][...] = here_ref[span, :] + came_ref[span, :].astype(F32)

    outs = [((rows, cols), F32)] * cuts
    return run("table_sums", body, outs, [here, came], flops=EARLY)


def gather_grad(base, keys, cohorts, tokens, rows, before=(), out=BF16):
    many = len(cohorts)
    count, _, _, length = keys.shape
    cols = tokens[0].shape[-1]

    def body(base_ref, key_ref, *refs):
        piece_refs, before_refs = refs[:many], refs[many : many + len(before)]
        out_ref = refs[-1]
        row = lax.broadcasted_iota(I32, (rows, length), 0)
        for table in range(2):
            span = slice(table * rows, (table + 1) * rows)
            sums = None
            for i, m in enumerate(cohorts):
                hot = []
                for k in range(count):
                    place = key_ref[k, m, table : table + 1, :] - base_ref[0]
                    hot.append(jnp.where(place == row, 1.0, 0.0).astype(BF16))
                piece = piece_refs[i][...].reshape(count * length, cols)
                part = dot(jnp.concatenate(hot, axis=1), piece)
                sums = part if sums is None else sums + part
            for ref in before_refs:
                sums = sums + ref[span, :].astype(F32)
            out_ref[span, :] = sums.astype(out)

    return run(
        "gather_grad",
        body,
        [((2 * rows, cols), out)],
        [base, keys, *tokens, *before],
        smem=1,
        flops=4 * many * count * length * 2 * rows * cols,
    )


def sequence(replica, core, pieces, cotangent, gain, w_proj, w_out, cores, line):
    count = len(pieces)
    length, width = cotangent.shape
    cols = width // count
    head_dim = width // HEADS
    factor = head_dim ** (-0.5)
    tile = min(256, length)
    step = min(256, 4 * width)

    def body(r_ref, core_ref, cot_ref, wo_ref, wp_ref, gain_ref, *refs):
        piece_refs, refs = refs[:count], refs[count:]
        out_ref, *grad_refs = refs[: count + 1]
        normed_ref, dproj_ref, gated_ref, weight_ref = refs[count + 1 : count + 5]
        emb, act, slope, att, attn, dscale, dkey, dval, tok = refs[count + 5 :]

        for k in range(count):
            emb[r_ref[0] ^ k] = piece_refs[k][...]

        def embedded(span):
            return jnp.concatenate([emb[k, span] for k in range(count)], axis=1).astype(F32)

        def norm_of(value):
            centred = value - jnp.mean(value, axis=-1, keepdims=True)
            scale = lax.rsqrt(jnp.mean(centred * centred, axis=-1, keepdims=True) + EPS)
            return centred * scale, scale

        def norm_back(upper, hat, scale):
            return scale * (
                upper
                - jnp.mean(upper, axis=-1, keepdims=True)
                - hat * jnp.mean(upper * hat, axis=-1, keepdims=True)
            )

        for at in range(0, length, tile):
            span = slice(at, at + tile)
            hat, _ = norm_of(embedded(span))
            normed_ref[span, :] = (hat * gain_ref[...]).astype(BF16)

        normed = normed_ref[...]

        @pl.loop(0, 4 * width // step)
        def _(j):
            span = pl.ds(pl.multiple_of(j * step, step), step)
            proj = dot(normed, wp_ref[:, span])
            sig = sigmoid(proj)
            act[:, span] = (proj * sig).astype(BF16)
            slope[:, span] = sig * (1.0 + proj * (1.0 - sig))

        dkey[...] = jnp.zeros_like(dkey)
        dval[...] = jnp.zeros_like(dval)

        for at in range(0, length, tile):
            span = slice(at, at + tile)
            seen = at + tile
            past = slice(0, seen)
            keep = lax.broadcasted_iota(I32, (tile, seen), 1) <= at + lax.broadcasted_iota(
                I32, (tile, seen), 0
            )
            for h in range(HEADS):
                head = [slice(p * width + h * head_dim, p * width + (h + 1) * head_dim) for p in range(4)]
                scores = dot(act[span, head[2]], act[past, head[3]], NT) * factor
                sig = sigmoid(scores)
                soft = jnp.where(keep, scores * sig * (1.0 / length), 0.0).astype(BF16)
                attn[h, :, :seen] = soft
                grad = sig * (1.0 + scores * (1.0 - sig)) * (factor / length)
                dscale[h, :, :seen] = jnp.where(keep, grad, 0.0)
                att[:, head[0]] = dot(soft, act[past, head[1]])
            hat, scale = norm_of(att[...])
            gate = act[span, :width].astype(F32)
            gated = (hat * gate).astype(BF16)
            gated_ref[span, :] = gated
            out_ref[span, :] = (embedded(span) + dot(gated, wo_ref[...])).astype(BF16)
            dgated = dot(cot_ref[span, :], wo_ref[...], NT)
            dproj_ref[span, :width] = (dgated * hat * slope[span, :width]).astype(BF16)
            datt = norm_back(dgated * gate, hat, scale).astype(BF16)
            for h in range(HEADS):
                head = [slice(p * width + h * head_dim, p * width + (h + 1) * head_dim) for p in range(4)]
                dhead = datt[:, head[0]]
                dattn = dot(dhead, act[past, head[1]], NT)
                dscores = (dattn * dscale[h, :, :seen]).astype(BF16)
                dquery = dot(dscores, act[past, head[3]])
                dproj_ref[span, head[2]] = (dquery * slope[span, head[2]]).astype(BF16)
                dkey[past, head[0]] += dot(dscores, act[span, head[2]], TN)
                dval[past, head[0]] += dot(attn[h, :, :seen], dhead, TN)

        dproj_ref[:, width : 2 * width] = (dval[...] * slope[:, width : 2 * width]).astype(BF16)
        dproj_ref[:, 3 * width :] = (dkey[...] * slope[:, 3 * width :]).astype(BF16)

        for at in range(0, length, tile):
            span = slice(at, at + tile)
            hat, scale = norm_of(embedded(span))
            upper = dot(dproj_ref[span, :], wp_ref[...], NT) * gain_ref[...]
            grad = cot_ref[span, :].astype(F32) + norm_back(upper, hat, scale)
            for k in range(count):
                tok[k, span] = grad[:, k * cols : (k + 1) * cols].astype(BF16)

        for k in range(count):
            grad_refs[k][...] = tok[r_ref[0] ^ k]

        other = (core_ref[0] + 1) % cores
        sums = weight_sums(other, normed_ref, dproj_ref, gated_ref, cot_ref, cores, line, count)
        for k in range(count):
            weight_ref[k] = next(sums).astype(BF16)

    return run(
        "sequence",
        body,
        [
            ((length, width), BF16),
            *[((length, cols), BF16)] * count,
            ((length, width), BF16),
            ((length, 4 * width), BF16),
            ((length, width), BF16),
            ((count, width // cores, 5 * width // count), BF16),
        ],
        [replica, core, cotangent, w_out, w_proj, gain, *pieces],
        smem=2,
        vmem=24,
        flops=32 * length * width * width,
        scratch=[
            pltpu.VMEM((count, length, cols), BF16),
            pltpu.VMEM((length, 4 * width), BF16),
            pltpu.VMEM((length, 4 * width), F32),
            pltpu.VMEM((tile, width), F32),
            pltpu.VMEM((HEADS, tile, length), BF16),
            pltpu.VMEM((HEADS, tile, length), F32),
            pltpu.VMEM((length, width), F32),
            pltpu.VMEM((length, width), F32),
            pltpu.VMEM((count, length, cols), BF16),
        ],
    )


def weight_sums(core, n_ref, d_ref, g_ref, c_ref, cores, line, blocks):
    length, width = n_ref.shape
    rows = width // (cores * line)
    half = width // cores
    edge = d_ref.shape[1]
    cols = (edge + c_ref.shape[1]) // blocks
    feature = lax.broadcasted_iota(I32, (width, half), 0)
    column = lax.broadcasted_iota(I32, (width, half), 1)
    wanted = (column // rows * cores + core) * rows + column % rows
    pick = jnp.where(feature == wanted, 1.0, 0.0).astype(BF16)
    n_part = dot(n_ref[...], pick).astype(BF16)
    g_part = dot(g_ref[...], pick).astype(BF16)
    for k in range(blocks):
        first, last = k * cols, (k + 1) * cols
        parts = []
        if first < edge:
            parts.append(dot(n_part, d_ref[:, first : min(last, edge)], TN))
        if last > edge:
            parts.append(dot(g_part, c_ref[:, max(first, edge) - edge : last - edge], TN))
        yield parts[0] if len(parts) == 1 else jnp.concatenate(parts, axis=1)


def weight_grad(replica, core, normed, dproj, gated, cotangent, before, line):
    blocks, half, cols = before.shape
    length, width = normed.shape
    cores = width // half
    bits = blocks.bit_length() - 1
    tall = half // bits

    def body(r_ref, core_ref, n_ref, d_ref, g_ref, c_ref, before_ref, *refs):
        out_refs, scratch = refs[:-1], refs[-1]
        sums = weight_sums(core_ref[0], n_ref, d_ref, g_ref, c_ref, cores, line, blocks)
        for k in range(blocks):
            total = next(sums) + before_ref[k].astype(F32)
            for p in range(bits):
                at = sum((k >> (p + i) % bits & 1) << bits - 1 - i for i in range(bits))
                scratch[p, at] = total[p * tall : (p + 1) * tall]
        for p in range(bits):
            split_halves(scratch.at[p], r_ref[0] >> p & 1, out_refs[2 * p : 2 * p + 2])

    kept = (blocks // 2, tall, cols)
    return run(
        "weight_grad",
        body,
        [(kept, F32), (kept, BF16)] * bits,
        [replica, core, normed, dproj, gated, cotangent, before],
        smem=2,
        scratch=[pltpu.VMEM((bits, blocks, tall, cols), F32)],
        flops=2 * length * half * (blocks * cols + 2 * width),
    )


def split_halves(ref, bit, out_refs):
    count = ref.shape[0] // 2
    for i, out_ref in enumerate(out_refs):
        start = (bit ^ i) * count
        for k in range(count):
            out_ref[k] = ref[start + k].astype(out_ref.dtype)


def fold(replica, kept, came, step):
    count, tall, cols = kept[0].shape
    many = len(kept)

    def body(r_ref, *refs):
        kept_refs, came_refs, out_refs = refs[:many], refs[many : 2 * many], refs[2 * many : -1]
        scratch = refs[-1]
        for p in range(many):
            for k in range(count):
                scratch[p, k] = kept_refs[p][k] + came_refs[p][k].astype(F32)
            split_halves(scratch.at[p], r_ref[0] >> (p + step) % many & 1, out_refs[2 * p : 2 * p + 2])

    half = (count // 2, tall, cols)
    return run(
        "fold",
        body,
        [(half, F32), (half, BF16)] * many,
        [replica, *kept, *came],
        smem=1,
        scratch=[pltpu.VMEM((many, count, tall, cols), F32)],
    )


def cut_line(place, kept, came, line):
    _, tall, cols = kept[0].shape
    many = len(kept)
    rows = many * tall // line

    def body(place_ref, *refs):
        kept_refs, came_refs, out_refs = refs[:many], refs[many : 2 * many], refs[2 * many : -1]
        scratch = refs[-1]
        for p in range(many):
            scratch[p * tall : (p + 1) * tall] = kept_refs[p][0] + came_refs[p][0].astype(F32)
        for k in range(line):
            span = pl.ds(pl.multiple_of((place_ref[0] ^ k) * rows, rows), rows)
            out_refs[k % 2][k // 2] = scratch[span].astype(out_refs[k % 2].dtype)

    half = (line // 2, rows, cols)
    return run(
        "cut_line",
        body,
        [(half, F32), (half, BF16)],
        [place, *kept, *came],
        smem=1,
        scratch=[pltpu.VMEM((many * tall, cols), F32)],
    )


def fold_line(kept, came):
    count, rows, cols = kept.shape

    def body(kept_ref, came_ref, *out_refs):
        for k in range(count):
            total = kept_ref[k] + came_ref[k].astype(F32)
            out_refs[k % 2][k // 2] = total.astype(out_refs[k % 2].dtype)

    half = (count // 2, rows, cols)
    return run("fold_line", body, [(half, F32), (half, BF16)], [kept, came])


def assemble(replica, parts, edge):
    rows, cols = parts[0].shape
    total = cols * len(parts)

    def body(r_ref, *refs):
        part_refs, (left_ref, right_ref, held) = refs[: len(parts)], refs[len(parts) :]
        for k, ref in enumerate(part_refs):
            held[r_ref[0] ^ k] = ref[...].astype(F32)
        for k in range(len(parts)):
            first, last = k * cols, (k + 1) * cols
            cut = min(max(edge - first, 0), cols)
            if cut > 0:
                left_ref[:, first : first + cut] = held[k, :, :cut]
            if cut < cols:
                right_ref[:, first + cut - edge : last - edge] = held[k, :, cut:]

    return run(
        "assemble",
        body,
        [((rows, edge), F32), ((rows, total - edge), F32)],
        [replica, *parts],
        smem=1,
        scratch=[pltpu.VMEM((len(parts), rows, cols), F32)],
    )


def local(
    item_table,
    action_table,
    item_owner,
    item_row,
    action_owner,
    action_row,
    input_norm_gain,
    w_proj,
    w_out,
    cotangent,
):
    grid = Grid()
    rows, width = item_table.shape
    replicas, line, cores = grid.replicas, grid.line, grid.cores
    cols = width // replicas

    bits = replicas.bit_length() - 1
    swaps = [3, 1, 2] if replicas == 4 else list(range(1, replicas))
    replica, place, core = (i.astype(I32).reshape(1) for i in (grid.r, grid.z, grid.c))
    bases = [((place ^ k) * cores + core) * rows for k in range(line)]

    own = jnp.concatenate(
        [
            lax.dynamic_slice_in_dim(item_table, grid.r * cols, cols, 1),
            lax.dynamic_slice_in_dim(action_table, grid.r * cols, cols, 1),
        ],
        axis=0,
    )
    keys = jnp.stack(
        [
            (item_owner * rows + item_row[:, None])[:, 0],
            (action_owner * rows + action_row[:, None])[:, 0],
        ]
    ).astype(I32)

    keys = jnp.stack([keys, grid.over_pair(keys)])
    keys = jnp.stack([keys] + [grid.over_replica(keys, k) for k in range(1, replicas)])

    held = {0: own}
    for low in reversed([1 << i for i in range(line.bit_length() - 1)]):
        for k in range(low, line, 2 * low):
            held[k] = grid.over_line(held[k ^ low], low)
    order = sorted(held, key=lambda k: (bin(k).count("1"), k))

    key_cols = jnp.broadcast_to(keys[..., None], (*keys.shape, LANES))
    both = list(range(cores))

    found = ()
    for k in order[:-1]:
        found = fetch(bases[k], key_cols, both, held[k], found)
    last = order[-1]
    there = fetch(bases[last], key_cols, both[1:], held[last], found[1:])
    here = fetch(bases[last], key_cols, both[:1], held[last], found[:1])
    pieces = combine([here[0], grid.over_pair(there[0])])
    for k in swaps:
        pieces[k] = grid.over_replica(pieces[k], k)

    gain = input_norm_gain.reshape(1, width)
    layer_out, *rest = sequence(
        replica, core, pieces, cotangent, gain, w_proj, w_out, cores, line
    )
    tokens, (normed, dproj, gated, weights) = rest[:replicas], rest[replicas:]
    for k in swaps:
        tokens[k] = grid.over_replica(tokens[k], k)

    weights = grid.over_pair(weights)
    weights = weight_grad(replica, core, normed, dproj, gated, cotangent, weights, line)
    tokens = lax.optimization_barrier((tokens, weights))[0]
    tokens = pack(tokens)
    there = grid.over_pair(tokens)

    def swap_weights(weights, step):
        kept, sent = weights[0::2], weights[1::2]
        return kept, [grid.over_replica(sent[p], 1 << (p + step) % bits) for p in range(bits)]

    kept, swapped = swap_weights(weights, 0)

    sums, raw, both_there = {}, {}, [tokens, there]
    for k in reversed(order):
        low = (k & -k) or line
        steps = [1 << i for i in range(low.bit_length() - 1)]
        out = F32 if steps else BF16
        if k == last:
            first = gather_grad(bases[k], keys, both[:1], [tokens], rows)
            raw[k] = gather_grad(bases[k], keys, both[1:], [there], rows, first, out)
        else:
            after = {1: raw[last], 0: sums.get(line // 2)}.get(k)
            if after is not None:
                both_there = lax.optimization_barrier((both_there, after))[0]
            raw[k] = gather_grad(bases[k], keys, both, both_there, rows, out=out)
        came = [grid.over_line(sums[k ^ step], step) for step in steps]
        if k == 0:
            near, table = came[0], raw[k][0]
            for part in came[:-1]:
                table = table_sums(table, part, 1)[0]
            item_grad, action_grad = table_sums(table, came[-1], 2)
        else:
            sums[k] = add_up(raw[k] + came) if steps else raw[k][0]

    for step in range(1, bits + 1):
        after = [raw[1], raw[line // 2]] if step < bits else [near, sums[line // 2]]
        swapped = lax.optimization_barrier((swapped, after))[0]
        if step < bits:
            kept, swapped = swap_weights(fold(replica, kept, swapped, step), step)
    kept, sent = cut_line(place, kept, swapped, line)
    step = 1
    while step < line // 2:
        kept, sent = fold_line(kept, grid.over_line(sent, step))
        step *= 2
    parts = [kept[0], grid.over_line(sent, step)[0]]
    parts = lax.optimization_barrier((parts, item_grad))[0]
    total = add_up(parts)
    parts = [total] + [grid.over_replica(total, k) for k in range(1, replicas)]
    grad_proj, grad_out = assemble(replica, parts, 4 * width)

    return layer_out, item_grad, action_grad, grad_proj, grad_out


def solution(mesh):
    tokens = ("replica", "sparse")
    in_specs = (
        P("sparse", None),
        P("sparse", None),
        P(tokens, None),
        P(tokens),
        P(tokens, None),
        P(tokens),
        P(),
        P(),
        P(),
        P(tokens, None),
    )
    out_specs = (
        P(tokens, None),
        P("sparse", "replica"),
        P("sparse", "replica"),
        P("sparse", None),
        P("sparse", None),
    )
    return jax.shard_map(local, mesh=mesh, in_specs=in_specs, out_specs=out_specs, check_vma=False)
```

```python
import jax
import jax.numpy as jnp
from jax import lax
from jax.experimental import pallas as pl
from jax.experimental.pallas import tpu as pltpu
from jax.sharding import PartitionSpec as P

HEADS = 4
EPS = 1e-05
LANES = 128
F32 = jnp.float32
BF16 = jnp.bfloat16
I32 = jnp.int32
MIB = 1024 * 1024
EARLY = 6 * 10**9
LATE = 40 * 10**9

NN = ((1,), (0,))
NT = ((1,), (1,))
TN = ((0,), (0,))


def dot(left, right, dims=NN):
    return lax.dot_general(left, right, (dims, ((), ())), preferred_element_type=F32)


def sigmoid(value):
    return 0.5 * jnp.tanh(0.5 * value) + 0.5


def run(name, body, outs, args, smem=0, scratch=(), vmem=16, flops=0):
    outs = [jax.ShapeDtypeStruct(shape, dtype) for shape, dtype in outs]
    size = sum(a.size * a.dtype.itemsize for a in [*args, *outs])
    in_smem = pl.BlockSpec(memory_space=pltpu.SMEM)
    in_vmem = pl.BlockSpec(memory_space=pltpu.VMEM)
    places = [in_smem] * smem + [in_vmem] * (len(args) - smem)
    results = pl.pallas_call(
        body,
        out_shape=outs,
        in_specs=places,
        out_specs=[in_vmem] * len(outs),
        scratch_shapes=list(scratch),
        compiler_params=pltpu.CompilerParams(vmem_limit_bytes=vmem * MIB),
        cost_estimate=pl.CostEstimate(flops=flops, bytes_accessed=size, transcendentals=0),
        name=name,
    )(*args)
    return list(results)


class Grid:
    def __init__(self):
        self.replicas = lax.axis_size("replica")
        self.shards = lax.axis_size("sparse")
        self.cores = 2 if self.shards % 2 == 0 else 1
        self.line = self.shards // self.cores
        self.r = lax.axis_index("replica")
        self.s = lax.axis_index("sparse")
        self.z = self.s // self.cores
        self.c = self.s % self.cores

    def over_replica(self, value, step):
        n = self.replicas
        return lax.ppermute(value, "replica", [(i, i ^ step) for i in range(n)])

    def over_line(self, value, step):
        pairs = [(i, i ^ step * self.cores) for i in range(self.shards)]
        return lax.ppermute(value, "sparse", pairs)

    def over_pair(self, value):
        return lax.ppermute(value, "sparse", [(i, i ^ 1) for i in range(self.shards)])


def fetch(base, keys, cohorts, chunk, before=()):
    many = len(cohorts)
    count, _, _, tokens, _ = keys.shape
    rows, cols = chunk.shape[0] // 2, chunk.shape[1]

    def body(base_ref, chunk_ref, key_ref, *refs):
        before_refs, out_refs = refs[:-many], refs[-many:]
        lane = lax.broadcasted_iota(I32, (tokens, LANES), 1)
        for i, m in enumerate(cohorts):
            for k in range(count):
                hot = []
                for table in range(2):
                    place = key_ref[k, m, table] - base_ref[0]
                    for start in range(0, rows, LANES):
                        hot.append(jnp.where(place == lane + start, 1.0, 0.0).astype(BF16))
                found = dot(jnp.concatenate(hot, axis=1), chunk_ref[...])
                if before_refs:
                    found = found + before_refs[i][k].astype(F32)
                out_refs[i][k] = found.astype(BF16)

    return run(
        "fetch",
        body,
        [((count, tokens, cols), BF16)] * many,
        [base, chunk, keys, *before],
        smem=1,
        flops=2 * many * count * tokens * rows * cols,
    )


def combine(parts):
    count, *shape = parts[0].shape

    def body(left_ref, right_ref, *out_refs):
        for k in range(count):
            total = left_ref[k].astype(F32) + right_ref[k].astype(F32)
            out_refs[k][...] = total.astype(BF16)

    return run("combine", body, [(tuple(shape), BF16)] * count, parts)


def pack(parts):
    def body(*refs):
        for k, ref in enumerate(refs[:-1]):
            refs[-1][k] = ref[...]

    shape, dtype = parts[0].shape, parts[0].dtype
    return run("pack", body, [((len(parts), *shape), dtype)], parts, flops=LATE)[0]


def add_up(parts):
    def body(*refs):
        total = refs[0][...].astype(F32)
        for ref in refs[1:-1]:
            total = total + ref[...].astype(F32)
        refs[-1][...] = total.astype(BF16)

    return run("add_up", body, [(parts[0].shape, BF16)], parts)[0]


def table_sums(here, came, cuts):
    rows, cols = here.shape[0] // cuts, here.shape[1]

    def body(here_ref, came_ref, *out_refs):
        for i in range(cuts):
            span = slice(i * rows, (i + 1) * rows)
            out_refs[i][...] = here_ref[span, :] + came_ref[span, :].astype(F32)

    outs = [((rows, cols), F32)] * cuts
    return run("table_sums", body, outs, [here, came], flops=EARLY)


def gather_grad(base, keys, cohorts, tokens, rows, before=(), out=BF16):
    many = len(cohorts)
    count, _, _, length = keys.shape
    cols = tokens[0].shape[-1]

    def body(base_ref, key_ref, *refs):
        piece_refs, before_refs = refs[:many], refs[many : many + len(before)]
        out_ref = refs[-1]
        row = lax.broadcasted_iota(I32, (rows, length), 0)
        for table in range(2):
            span = slice(table * rows, (table + 1) * rows)
            sums = None
            for i, m in enumerate(cohorts):
                hot = []
                for k in range(count):
                    place = key_ref[k, m, table : table + 1, :] - base_ref[0]
                    hot.append(jnp.where(place == row, 1.0, 0.0).astype(BF16))
                piece = piece_refs[i][...].reshape(count * length, cols)
                part = dot(jnp.concatenate(hot, axis=1), piece)
                sums = part if sums is None else sums + part
            for ref in before_refs:
                sums = sums + ref[span, :].astype(F32)
            out_ref[span, :] = sums.astype(out)

    return run(
        "gather_grad",
        body,
        [((2 * rows, cols), out)],
        [base, keys, *tokens, *before],
        smem=1,
        flops=4 * many * count * length * 2 * rows * cols,
    )


def sequence(replica, core, pieces, cotangent, gain, w_proj, w_out, cores, line):
    count = len(pieces)
    length, width = cotangent.shape
    cols = width // count
    head_dim = width // HEADS
    factor = head_dim ** (-0.5)
    tile = min(256, length)
    step = min(256, 4 * width)

    def body(r_ref, core_ref, cot_ref, wo_ref, wp_ref, gain_ref, *refs):
        piece_refs, refs = refs[:count], refs[count:]
        out_ref, *grad_refs = refs[: count + 1]
        normed_ref, dproj_ref, gated_ref, weight_ref = refs[count + 1 : count + 5]
        emb, act, slope, att, attn, dscale, dkey, dval, tok = refs[count + 5 :]

        for k in range(count):
            emb[r_ref[0] ^ k] = piece_refs[k][...]

        def embedded(span):
            return jnp.concatenate([emb[k, span] for k in range(count)], axis=1).astype(F32)

        def norm_of(value):
            centred = value - jnp.mean(value, axis=-1, keepdims=True)
            scale = lax.rsqrt(jnp.mean(centred * centred, axis=-1, keepdims=True) + EPS)
            return centred * scale, scale

        def norm_back(upper, hat, scale):
            return scale * (
                upper
                - jnp.mean(upper, axis=-1, keepdims=True)
                - hat * jnp.mean(upper * hat, axis=-1, keepdims=True)
            )

        for at in range(0, length, tile):
            span = slice(at, at + tile)
            hat, _ = norm_of(embedded(span))
            normed_ref[span, :] = (hat * gain_ref[...]).astype(BF16)

        normed = normed_ref[...]

        @pl.loop(0, 4 * width // step)
        def _(j):
            span = pl.ds(pl.multiple_of(j * step, step), step)
            proj = dot(normed, wp_ref[:, span])
            sig = sigmoid(proj)
            act[:, span] = (proj * sig).astype(BF16)
            slope[:, span] = sig * (1.0 + proj * (1.0 - sig))

        dkey[...] = jnp.zeros_like(dkey)
        dval[...] = jnp.zeros_like(dval)

        for at in range(0, length, tile):
            span = slice(at, at + tile)
            seen = at + tile
            past = slice(0, seen)
            keep = lax.broadcasted_iota(I32, (tile, seen), 1) <= at + lax.broadcasted_iota(
                I32, (tile, seen), 0
            )
            for h in range(HEADS):
                head = [slice(p * width + h * head_dim, p * width + (h + 1) * head_dim) for p in range(4)]
                scores = dot(act[span, head[2]], act[past, head[3]], NT) * factor
                sig = sigmoid(scores)
                soft = jnp.where(keep, scores * sig * (1.0 / length), 0.0).astype(BF16)
                attn[h, :, :seen] = soft
                grad = sig * (1.0 + scores * (1.0 - sig)) * (factor / length)
                dscale[h, :, :seen] = jnp.where(keep, grad, 0.0)
                att[:, head[0]] = dot(soft, act[past, head[1]])
            hat, scale = norm_of(att[...])
            gate = act[span, :width].astype(F32)
            gated = (hat * gate).astype(BF16)
            gated_ref[span, :] = gated
            out_ref[span, :] = (embedded(span) + dot(gated, wo_ref[...])).astype(BF16)
            dgated = dot(cot_ref[span, :], wo_ref[...], NT)
            dproj_ref[span, :width] = (dgated * hat * slope[span, :width]).astype(BF16)
            datt = norm_back(dgated * gate, hat, scale).astype(BF16)
            for h in range(HEADS):
                head = [slice(p * width + h * head_dim, p * width + (h + 1) * head_dim) for p in range(4)]
                dhead = datt[:, head[0]]
                dattn = dot(dhead, act[past, head[1]], NT)
                dscores = (dattn * dscale[h, :, :seen]).astype(BF16)
                dquery = dot(dscores, act[past, head[3]])
                dproj_ref[span, head[2]] = (dquery * slope[span, head[2]]).astype(BF16)
                dkey[past, head[0]] += dot(dscores, act[span, head[2]], TN)
                dval[past, head[0]] += dot(attn[h, :, :seen], dhead, TN)

        dproj_ref[:, width : 2 * width] = (dval[...] * slope[:, width : 2 * width]).astype(BF16)
        dproj_ref[:, 3 * width :] = (dkey[...] * slope[:, 3 * width :]).astype(BF16)

        for at in range(0, length, tile):
            span = slice(at, at + tile)
            hat, scale = norm_of(embedded(span))
            upper = dot(dproj_ref[span, :], wp_ref[...], NT) * gain_ref[...]
            grad = cot_ref[span, :].astype(F32) + norm_back(upper, hat, scale)
            for k in range(count):
                tok[k, span] = grad[:, k * cols : (k + 1) * cols].astype(BF16)

        for k in range(count):
            grad_refs[k][...] = tok[r_ref[0] ^ k]

        other = (core_ref[0] + 1) % cores
        sums = weight_sums(other, normed_ref, dproj_ref, gated_ref, cot_ref, cores, line, count)
        for k in range(count):
            weight_ref[k] = next(sums).astype(BF16)

    return run(
        "sequence",
        body,
        [
            ((length, width), BF16),
            *[((length, cols), BF16)] * count,
            ((length, width), BF16),
            ((length, 4 * width), BF16),
            ((length, width), BF16),
            ((count, width // cores, 5 * width // count), BF16),
        ],
        [replica, core, cotangent, w_out, w_proj, gain, *pieces],
        smem=2,
        vmem=24,
        flops=32 * length * width * width,
        scratch=[
            pltpu.VMEM((count, length, cols), BF16),
            pltpu.VMEM((length, 4 * width), BF16),
            pltpu.VMEM((length, 4 * width), F32),
            pltpu.VMEM((tile, width), F32),
            pltpu.VMEM((HEADS, tile, length), BF16),
            pltpu.VMEM((HEADS, tile, length), F32),
            pltpu.VMEM((length, width), F32),
            pltpu.VMEM((length, width), F32),
            pltpu.VMEM((count, length, cols), BF16),
        ],
    )


def weight_sums(core, n_ref, d_ref, g_ref, c_ref, cores, line, blocks):
    length, width = n_ref.shape
    rows = width // (cores * line)
    half = width // cores
    edge = d_ref.shape[1]
    cols = (edge + c_ref.shape[1]) // blocks
    feature = lax.broadcasted_iota(I32, (width, half), 0)
    column = lax.broadcasted_iota(I32, (width, half), 1)
    wanted = (column // rows * cores + core) * rows + column % rows
    pick = jnp.where(feature == wanted, 1.0, 0.0).astype(BF16)
    n_part = dot(n_ref[...], pick).astype(BF16)
    g_part = dot(g_ref[...], pick).astype(BF16)
    for k in range(blocks):
        first, last = k * cols, (k + 1) * cols
        parts = []
        if first < edge:
            parts.append(dot(n_part, d_ref[:, first : min(last, edge)], TN))
        if last > edge:
            parts.append(dot(g_part, c_ref[:, max(first, edge) - edge : last - edge], TN))
        yield parts[0] if len(parts) == 1 else jnp.concatenate(parts, axis=1)


def weight_grad(replica, core, normed, dproj, gated, cotangent, before, line):
    blocks, half, cols = before.shape
    length, width = normed.shape
    cores = width // half
    bits = blocks.bit_length() - 1
    tall = half // bits

    def body(r_ref, core_ref, n_ref, d_ref, g_ref, c_ref, before_ref, *refs):
        out_refs, scratch = refs[:-1], refs[-1]
        sums = weight_sums(core_ref[0], n_ref, d_ref, g_ref, c_ref, cores, line, blocks)
        for k in range(blocks):
            total = next(sums) + before_ref[k].astype(F32)
            for p in range(bits):
                at = sum((k >> (p + i) % bits & 1) << bits - 1 - i for i in range(bits))
                scratch[p, at] = total[p * tall : (p + 1) * tall]
        for p in range(bits):
            split_halves(scratch.at[p], r_ref[0] >> p & 1, out_refs[2 * p : 2 * p + 2])

    kept = (blocks // 2, tall, cols)
    return run(
        "weight_grad",
        body,
        [(kept, F32), (kept, BF16)] * bits,
        [replica, core, normed, dproj, gated, cotangent, before],
        smem=2,
        scratch=[pltpu.VMEM((bits, blocks, tall, cols), F32)],
        flops=2 * length * half * (blocks * cols + 2 * width),
    )


def split_halves(ref, bit, out_refs):
    count = ref.shape[0] // 2
    for i, out_ref in enumerate(out_refs):
        start = (bit ^ i) * count
        for k in range(count):
            out_ref[k] = ref[start + k].astype(out_ref.dtype)


def fold(replica, kept, came, step):
    count, tall, cols = kept[0].shape
    many = len(kept)

    def body(r_ref, *refs):
        kept_refs, came_refs, out_refs = refs[:many], refs[many : 2 * many], refs[2 * many : -1]
        scratch = refs[-1]
        for p in range(many):
            for k in range(count):
                scratch[p, k] = kept_refs[p][k] + came_refs[p][k].astype(F32)
            split_halves(scratch.at[p], r_ref[0] >> (p + step) % many & 1, out_refs[2 * p : 2 * p + 2])

    half = (count // 2, tall, cols)
    return run(
        "fold",
        body,
        [(half, F32), (half, BF16)] * many,
        [replica, *kept, *came],
        smem=1,
        scratch=[pltpu.VMEM((many, count, tall, cols), F32)],
    )


def cut_line(place, kept, came, line):
    _, tall, cols = kept[0].shape
    many = len(kept)
    rows = many * tall // line

    def body(place_ref, *refs):
        kept_refs, came_refs, out_refs = refs[:many], refs[many : 2 * many], refs[2 * many : -1]
        scratch = refs[-1]
        for p in range(many):
            scratch[p * tall : (p + 1) * tall] = kept_refs[p][0] + came_refs[p][0].astype(F32)
        for k in range(line):
            span = pl.ds(pl.multiple_of((place_ref[0] ^ k) * rows, rows), rows)
            out_refs[k % 2][k // 2] = scratch[span].astype(out_refs[k % 2].dtype)

    half = (line // 2, rows, cols)
    return run(
        "cut_line",
        body,
        [(half, F32), (half, BF16)],
        [place, *kept, *came],
        smem=1,
        scratch=[pltpu.VMEM((many * tall, cols), F32)],
    )


def fold_line(kept, came):
    count, rows, cols = kept.shape

    def body(kept_ref, came_ref, *out_refs):
        for k in range(count):
            total = kept_ref[k] + came_ref[k].astype(F32)
            out_refs[k % 2][k // 2] = total.astype(out_refs[k % 2].dtype)

    half = (count // 2, rows, cols)
    return run("fold_line", body, [(half, F32), (half, BF16)], [kept, came])


def assemble(replica, parts, edge):
    rows, cols = parts[0].shape
    total = cols * len(parts)

    def body(r_ref, *refs):
        part_refs, (left_ref, right_ref, held) = refs[: len(parts)], refs[len(parts) :]
        for k, ref in enumerate(part_refs):
            held[r_ref[0] ^ k] = ref[...].astype(F32)
        for k in range(len(parts)):
            first, last = k * cols, (k + 1) * cols
            cut = min(max(edge - first, 0), cols)
            if cut > 0:
                left_ref[:, first : first + cut] = held[k, :, :cut]
            if cut < cols:
                right_ref[:, first + cut - edge : last - edge] = held[k, :, cut:]

    return run(
        "assemble",
        body,
        [((rows, edge), F32), ((rows, total - edge), F32)],
        [replica, *parts],
        smem=1,
        scratch=[pltpu.VMEM((len(parts), rows, cols), F32)],
    )


def local(
    item_table,
    action_table,
    item_owner,
    item_row,
    action_owner,
    action_row,
    input_norm_gain,
    w_proj,
    w_out,
    cotangent,
):
    grid = Grid()
    rows, width = item_table.shape
    replicas, line, cores = grid.replicas, grid.line, grid.cores
    cols = width // replicas

    bits = replicas.bit_length() - 1
    swaps = [3, 1, 2] if replicas == 4 else list(range(1, replicas))
    replica, place, core = (i.astype(I32).reshape(1) for i in (grid.r, grid.z, grid.c))
    bases = [((place ^ k) * cores + core) * rows for k in range(line)]

    own = jnp.concatenate(
        [
            lax.dynamic_slice_in_dim(item_table, grid.r * cols, cols, 1),
            lax.dynamic_slice_in_dim(action_table, grid.r * cols, cols, 1),
        ],
        axis=0,
    )
    keys = jnp.stack(
        [
            (item_owner * rows + item_row[:, None])[:, 0],
            (action_owner * rows + action_row[:, None])[:, 0],
        ]
    ).astype(I32)

    keys = jnp.stack([keys, grid.over_pair(keys)])
    keys = jnp.stack([keys] + [grid.over_replica(keys, k) for k in range(1, replicas)])

    held = {0: own}
    for low in reversed([1 << i for i in range(line.bit_length() - 1)]):
        for k in range(low, line, 2 * low):
            held[k] = grid.over_line(held[k ^ low], low)
    order = sorted(held, key=lambda k: (bin(k).count("1"), k))

    key_cols = jnp.broadcast_to(keys[..., None], (*keys.shape, LANES))
    both = list(range(cores))

    found = ()
    for k in order[:-1]:
        found = fetch(bases[k], key_cols, both, held[k], found)
    last = order[-1]
    there = fetch(bases[last], key_cols, both[1:], held[last], found[1:])
    here = fetch(bases[last], key_cols, both[:1], held[last], found[:1])
    pieces = combine([here[0], grid.over_pair(there[0])])
    for k in swaps:
        pieces[k] = grid.over_replica(pieces[k], k)

    gain = input_norm_gain.reshape(1, width)
    layer_out, *rest = sequence(
        replica, core, pieces, cotangent, gain, w_proj, w_out, cores, line
    )
    tokens, (normed, dproj, gated, weights) = rest[:replicas], rest[replicas:]
    for k in swaps:
        tokens[k] = grid.over_replica(tokens[k], k)

    weights = grid.over_pair(weights)
    weights = weight_grad(replica, core, normed, dproj, gated, cotangent, weights, line)
    def swap_weights(weights, step):
        kept, sent = weights[0::2], weights[1::2]
        return kept, [grid.over_replica(sent[p], 1 << (p + step) % bits) for p in range(bits)]

    kept, swapped = swap_weights(weights, 0)
    tokens = lax.optimization_barrier((pack(tokens), swapped))[0]
    there = grid.over_pair(tokens)

    sums, raw, both_there = {}, {}, [tokens, there]
    for k in reversed(order):
        low = (k & -k) or line
        steps = [1 << i for i in range(low.bit_length() - 1)]
        out = F32 if steps else BF16
        if k == last:
            first = gather_grad(bases[k], keys, both[:1], [tokens], rows)
            raw[k] = gather_grad(bases[k], keys, both[1:], [there], rows, first, out)
        else:
            after = {1: raw[last], 0: sums.get(line // 2)}.get(k)
            if after is not None:
                both_there = lax.optimization_barrier((both_there, after))[0]
            raw[k] = gather_grad(bases[k], keys, both, both_there, rows, out=out)
        came = [grid.over_line(sums[k ^ step], step) for step in steps]
        if k == 0:
            table = raw[k][0]
            for part in came[:-1]:
                table = table_sums(table, part, 1)[0]
            item_grad, action_grad = table_sums(table, came[-1], 2)
        else:
            sums[k] = add_up(raw[k] + came) if steps else raw[k][0]

    for step in range(1, bits + 1):
        if step < bits:
            kept, swapped = swap_weights(fold(replica, kept, swapped, step), step)
    swapped = lax.optimization_barrier((swapped, raw[1]))[0]
    kept, sent = cut_line(place, kept, swapped, line)
    step = 1
    while step < line // 2:
        came = lax.optimization_barrier((grid.over_line(sent, step), sums[line // 2]))[0]
        kept, sent = fold_line(kept, came)
        step *= 2
    parts = [kept[0], grid.over_line(sent, step)[0]]
    parts = lax.optimization_barrier((parts, raw[0]))[0]
    total = add_up(parts)
    parts = [total] + [grid.over_replica(total, k) for k in range(1, replicas)]
    grad_proj, grad_out = assemble(replica, parts, 4 * width)

    return layer_out, item_grad, action_grad, grad_proj, grad_out


def solution(mesh):
    tokens = ("replica", "sparse")
    in_specs = (
        P("sparse", None),
        P("sparse", None),
        P(tokens, None),
        P(tokens),
        P(tokens, None),
        P(tokens),
        P(),
        P(),
        P(),
        P(tokens, None),
    )
    out_specs = (
        P(tokens, None),
        P("sparse", "replica"),
        P("sparse", "replica"),
        P("sparse", None),
        P("sparse", None),
    )
    return jax.shard_map(local, mesh=mesh, in_specs=in_specs, out_specs=out_specs, check_vma=False)
```

```python
import jax
import jax.numpy as jnp
from jax import lax
from jax.experimental import pallas as pl
from jax.experimental.pallas import tpu as pltpu
from jax.sharding import PartitionSpec as P

HEADS = 4
EPS = 1e-05
LANES = 128
F32 = jnp.float32
BF16 = jnp.bfloat16
I32 = jnp.int32
MIB = 1024 * 1024
EARLY = 6 * 10**9

NN = ((1,), (0,))
NT = ((1,), (1,))
TN = ((0,), (0,))


def dot(left, right, dims=NN):
    return lax.dot_general(left, right, (dims, ((), ())), preferred_element_type=F32)


def sigmoid(value):
    return 0.5 * jnp.tanh(0.5 * value) + 0.5


def run(name, body, outs, args, smem=0, scratch=(), vmem=16, flops=0):
    outs = [jax.ShapeDtypeStruct(shape, dtype) for shape, dtype in outs]
    size = sum(a.size * a.dtype.itemsize for a in [*args, *outs])
    in_smem = pl.BlockSpec(memory_space=pltpu.SMEM)
    in_vmem = pl.BlockSpec(memory_space=pltpu.VMEM)
    places = [in_smem] * smem + [in_vmem] * (len(args) - smem)
    results = pl.pallas_call(
        body,
        out_shape=outs,
        in_specs=places,
        out_specs=[in_vmem] * len(outs),
        scratch_shapes=list(scratch),
        compiler_params=pltpu.CompilerParams(vmem_limit_bytes=vmem * MIB),
        cost_estimate=pl.CostEstimate(flops=flops, bytes_accessed=size, transcendentals=0),
        name=name,
    )(*args)
    return list(results)


class Grid:
    def __init__(self):
        self.replicas = lax.axis_size("replica")
        self.shards = lax.axis_size("sparse")
        self.cores = 2 if self.shards % 2 == 0 else 1
        self.line = self.shards // self.cores
        self.r = lax.axis_index("replica")
        self.s = lax.axis_index("sparse")
        self.z = self.s // self.cores
        self.c = self.s % self.cores

    def over_replica(self, value, step):
        n = self.replicas
        return lax.ppermute(value, "replica", [(i, i ^ step) for i in range(n)])

    def over_line(self, value, step):
        pairs = [(i, i ^ step * self.cores) for i in range(self.shards)]
        return lax.ppermute(value, "sparse", pairs)

    def over_pair(self, value):
        return lax.ppermute(value, "sparse", [(i, i ^ 1) for i in range(self.shards)])


def fetch(base, keys, cohorts, chunk, before=()):
    many = len(cohorts)
    count, _, _, tokens, _ = keys.shape
    rows, cols = chunk.shape[0] // 2, chunk.shape[1]

    def body(base_ref, chunk_ref, key_ref, *refs):
        before_refs, out_refs = refs[:-many], refs[-many:]
        lane = lax.broadcasted_iota(I32, (tokens, LANES), 1)
        for i, m in enumerate(cohorts):
            for k in range(count):
                hot = []
                for table in range(2):
                    place = key_ref[k, m, table] - base_ref[0]
                    for start in range(0, rows, LANES):
                        hot.append(jnp.where(place == lane + start, 1.0, 0.0).astype(BF16))
                found = dot(jnp.concatenate(hot, axis=1), chunk_ref[...])
                if before_refs:
                    found = found + before_refs[i][k].astype(F32)
                out_refs[i][k] = found.astype(BF16)

    return run(
        "fetch",
        body,
        [((count, tokens, cols), BF16)] * many,
        [base, chunk, keys, *before],
        smem=1,
        flops=2 * many * count * tokens * rows * cols,
    )


def combine(parts):
    count, *shape = parts[0].shape

    def body(left_ref, right_ref, *out_refs):
        for k in range(count):
            total = left_ref[k].astype(F32) + right_ref[k].astype(F32)
            out_refs[k][...] = total.astype(BF16)

    return run("combine", body, [(tuple(shape), BF16)] * count, parts)


def pack(parts):
    def body(*refs):
        for k, ref in enumerate(refs[:-1]):
            refs[-1][k] = ref[...]

    shape, dtype = parts[0].shape, parts[0].dtype
    return run("pack", body, [((len(parts), *shape), dtype)], parts)[0]


def add_up(parts):
    def body(*refs):
        total = refs[0][...].astype(F32)
        for ref in refs[1:-1]:
            total = total + ref[...].astype(F32)
        refs[-1][...] = total.astype(BF16)

    return run("add_up", body, [(parts[0].shape, BF16)], parts)[0]


def table_sums(here, came, cuts):
    rows, cols = here.shape[0] // cuts, here.shape[1]

    def body(here_ref, came_ref, *out_refs):
        for i in range(cuts):
            span = slice(i * rows, (i + 1) * rows)
            out_refs[i][...] = here_ref[span, :] + came_ref[span, :].astype(F32)

    outs = [((rows, cols), F32)] * cuts
    return run("table_sums", body, outs, [here, came], flops=EARLY)


def gather_grad(base, keys, cohorts, tokens, rows, before=(), out=BF16):
    many = len(cohorts)
    count, _, _, length = keys.shape
    cols = tokens[0].shape[-1]

    def body(base_ref, key_ref, *refs):
        piece_refs, before_refs = refs[:many], refs[many : many + len(before)]
        out_ref = refs[-1]
        row = lax.broadcasted_iota(I32, (rows, length), 0)
        for table in range(2):
            span = slice(table * rows, (table + 1) * rows)
            sums = None
            for i, m in enumerate(cohorts):
                hot = []
                for k in range(count):
                    place = key_ref[k, m, table : table + 1, :] - base_ref[0]
                    hot.append(jnp.where(place == row, 1.0, 0.0).astype(BF16))
                piece = piece_refs[i][...].reshape(count * length, cols)
                part = dot(jnp.concatenate(hot, axis=1), piece)
                sums = part if sums is None else sums + part
            for ref in before_refs:
                sums = sums + ref[span, :].astype(F32)
            out_ref[span, :] = sums.astype(out)

    return run(
        "gather_grad",
        body,
        [((2 * rows, cols), out)],
        [base, keys, *tokens, *before],
        smem=1,
        flops=4 * many * count * length * 2 * rows * cols,
    )


def sequence(replica, core, pieces, cotangent, gain, w_proj, w_out, cores, line):
    count = len(pieces)
    length, width = cotangent.shape
    cols = width // count
    head_dim = width // HEADS
    factor = head_dim ** (-0.5)
    tile = min(256, length)
    step = min(256, 4 * width)

    def body(r_ref, core_ref, cot_ref, wo_ref, wp_ref, gain_ref, *refs):
        piece_refs, refs = refs[:count], refs[count:]
        out_ref, *grad_refs = refs[: count + 1]
        normed_ref, dproj_ref, gated_ref, weight_ref = refs[count + 1 : count + 5]
        emb, act, slope, att, attn, dscale, dkey, dval, tok = refs[count + 5 :]

        for k in range(count):
            emb[r_ref[0] ^ k] = piece_refs[k][...]

        def embedded(span):
            return jnp.concatenate([emb[k, span] for k in range(count)], axis=1).astype(F32)

        def norm_of(value):
            centred = value - jnp.mean(value, axis=-1, keepdims=True)
            scale = lax.rsqrt(jnp.mean(centred * centred, axis=-1, keepdims=True) + EPS)
            return centred * scale, scale

        def norm_back(upper, hat, scale):
            return scale * (
                upper
                - jnp.mean(upper, axis=-1, keepdims=True)
                - hat * jnp.mean(upper * hat, axis=-1, keepdims=True)
            )

        for at in range(0, length, tile):
            span = slice(at, at + tile)
            hat, _ = norm_of(embedded(span))
            normed_ref[span, :] = (hat * gain_ref[...]).astype(BF16)

        normed = normed_ref[...]

        for at in range(0, 4 * width, step):
            span = slice(at, at + step)
            proj = dot(normed, wp_ref[:, span])
            sig = sigmoid(proj)
            soft = proj * sig
            act[:, span] = soft.astype(BF16)
            slope[:, span] = sig + soft * (1.0 - sig)

        for at in reversed(range(0, length, tile)):
            span = slice(at, at + tile)
            seen = at + tile
            past = slice(0, seen)
            keep = lax.broadcasted_iota(I32, (tile, seen), 1) <= at + lax.broadcasted_iota(
                I32, (tile, seen), 0
            )
            weight = jnp.where(keep, 1.0 / length, 0.0)
            weight_back = jnp.where(keep, factor / length, 0.0)
            for h in range(HEADS):
                head = [slice(p * width + h * head_dim, p * width + (h + 1) * head_dim) for p in range(4)]
                scores = dot(act[span, head[2]], act[past, head[3]], NT) * factor
                sig = sigmoid(scores)
                soft = scores * sig
                attn[h, :, :seen] = (soft * weight).astype(BF16)
                dscale[h, :, :seen] = (sig + soft * (1.0 - sig)) * weight_back
                att[:, head[0]] = dot(attn[h, :, :seen], act[past, head[1]])
            hat, scale = norm_of(att[...])
            gate = act[span, :width].astype(F32)
            gated = (hat * gate).astype(BF16)
            gated_ref[span, :] = gated
            out_ref[span, :] = (embedded(span) + dot(gated, wo_ref[...])).astype(BF16)
            dgated = dot(cot_ref[span, :], wo_ref[...], NT)
            dproj_ref[span, :width] = (dgated * hat * slope[span, :width]).astype(BF16)
            datt = norm_back(dgated * gate, hat, scale).astype(BF16)
            for h in range(HEADS):
                head = [slice(p * width + h * head_dim, p * width + (h + 1) * head_dim) for p in range(4)]
                dhead = datt[:, head[0]]
                dattn = dot(dhead, act[past, head[1]], NT)
                dscores = (dattn * dscale[h, :, :seen]).astype(BF16)
                dquery = dot(dscores, act[past, head[3]])
                dproj_ref[span, head[2]] = (dquery * slope[span, head[2]]).astype(BF16)
                back = dot(dscores, act[span, head[2]], TN), dot(attn[h, :, :seen], dhead, TN)
                for ref, part in zip((dkey, dval), back):
                    if seen == length:
                        ref[past, head[0]] = part
                    else:
                        ref[past, head[0]] += part

        dproj_ref[:, width : 2 * width] = (dval[...] * slope[:, width : 2 * width]).astype(BF16)
        dproj_ref[:, 3 * width :] = (dkey[...] * slope[:, 3 * width :]).astype(BF16)

        dkey[...] = dot(dproj_ref[...], wp_ref[...], NT)
        for at in range(0, length, tile):
            span = slice(at, at + tile)
            hat, scale = norm_of(embedded(span))
            upper = dkey[span, :] * gain_ref[...]
            grad = cot_ref[span, :].astype(F32) + norm_back(upper, hat, scale)
            for k in range(count):
                tok[k, span] = grad[:, k * cols : (k + 1) * cols].astype(BF16)

        for k in range(count):
            grad_refs[k][...] = tok[r_ref[0] ^ k]

        other = (core_ref[0] + 1) % cores
        sums = weight_sums(other, normed_ref, dproj_ref, gated_ref, cot_ref, cores, line, count)
        for k in range(count):
            weight_ref[k] = next(sums).astype(BF16)

    return run(
        "sequence",
        body,
        [
            ((length, width), BF16),
            *[((length, cols), BF16)] * count,
            ((length, width), BF16),
            ((length, 4 * width), BF16),
            ((length, width), BF16),
            ((count, width // cores, 5 * width // count), BF16),
        ],
        [replica, core, cotangent, w_out, w_proj, gain, *pieces],
        smem=2,
        vmem=24,
        flops=32 * length * width * width,
        scratch=[
            pltpu.VMEM((count, length, cols), BF16),
            pltpu.VMEM((length, 4 * width), BF16),
            pltpu.VMEM((length, 4 * width), F32),
            pltpu.VMEM((tile, width), F32),
            pltpu.VMEM((HEADS, tile, length), BF16),
            pltpu.VMEM((HEADS, tile, length), F32),
            pltpu.VMEM((length, width), F32),
            pltpu.VMEM((length, width), F32),
            pltpu.VMEM((count, length, cols), BF16),
        ],
    )


def weight_sums(core, n_ref, d_ref, g_ref, c_ref, cores, line, blocks):
    length, width = n_ref.shape
    rows = width // (cores * line)
    half = width // cores
    edge = d_ref.shape[1]
    cols = (edge + c_ref.shape[1]) // blocks
    feature = lax.broadcasted_iota(I32, (width, half), 0)
    column = lax.broadcasted_iota(I32, (width, half), 1)
    wanted = (column // rows * cores + core) * rows + column % rows
    pick = jnp.where(feature == wanted, 1.0, 0.0).astype(BF16)
    n_part = dot(n_ref[...], pick).astype(BF16)
    g_part = dot(g_ref[...], pick).astype(BF16)
    for k in range(blocks):
        first, last = k * cols, (k + 1) * cols
        parts = []
        if first < edge:
            parts.append(dot(n_part, d_ref[:, first : min(last, edge)], TN))
        if last > edge:
            parts.append(dot(g_part, c_ref[:, max(first, edge) - edge : last - edge], TN))
        yield parts[0] if len(parts) == 1 else jnp.concatenate(parts, axis=1)


def weight_grad(replica, core, normed, dproj, gated, cotangent, before, line):
    blocks, half, cols = before.shape
    length, width = normed.shape
    cores = width // half
    bits = blocks.bit_length() - 1
    tall = half // bits

    def body(r_ref, core_ref, n_ref, d_ref, g_ref, c_ref, before_ref, *refs):
        out_refs, scratch = refs[:-1], refs[-1]
        sums = weight_sums(core_ref[0], n_ref, d_ref, g_ref, c_ref, cores, line, blocks)
        for k in range(blocks):
            total = next(sums) + before_ref[k].astype(F32)
            for p in range(bits):
                at = sum((k >> (p + i) % bits & 1) << bits - 1 - i for i in range(bits))
                scratch[p, at] = total[p * tall : (p + 1) * tall]
        for p in range(bits):
            split_halves(scratch.at[p], r_ref[0] >> p & 1, out_refs[2 * p : 2 * p + 2])

    kept = (blocks // 2, tall, cols)
    return run(
        "weight_grad",
        body,
        [(kept, F32), (kept, BF16)] * bits,
        [replica, core, normed, dproj, gated, cotangent, before],
        smem=2,
        scratch=[pltpu.VMEM((bits, blocks, tall, cols), F32)],
        flops=2 * length * half * (blocks * cols + 2 * width),
    )


def split_halves(ref, bit, out_refs):
    count = ref.shape[0] // 2
    for i, out_ref in enumerate(out_refs):
        start = (bit ^ i) * count
        for k in range(count):
            out_ref[k] = ref[start + k].astype(out_ref.dtype)


def fold(replica, kept, came, step):
    count, tall, cols = kept[0].shape
    many = len(kept)

    def body(r_ref, *refs):
        kept_refs, came_refs, out_refs = refs[:many], refs[many : 2 * many], refs[2 * many : -1]
        scratch = refs[-1]
        for p in range(many):
            for k in range(count):
                scratch[p, k] = kept_refs[p][k] + came_refs[p][k].astype(F32)
            split_halves(scratch.at[p], r_ref[0] >> (p + step) % many & 1, out_refs[2 * p : 2 * p + 2])

    half = (count // 2, tall, cols)
    return run(
        "fold",
        body,
        [(half, F32), (half, BF16)] * many,
        [replica, *kept, *came],
        smem=1,
        scratch=[pltpu.VMEM((many, count, tall, cols), F32)],
    )


def cut_line(place, kept, came, line):
    _, tall, cols = kept[0].shape
    many = len(kept)
    rows = many * tall // line

    def body(place_ref, *refs):
        kept_refs, came_refs, out_refs = refs[:many], refs[many : 2 * many], refs[2 * many : -1]
        scratch = refs[-1]
        for p in range(many):
            scratch[p * tall : (p + 1) * tall] = kept_refs[p][0] + came_refs[p][0].astype(F32)
        for k in range(line):
            span = pl.ds(pl.multiple_of((place_ref[0] ^ k) * rows, rows), rows)
            out_refs[k % 2][k // 2] = scratch[span].astype(out_refs[k % 2].dtype)

    half = (line // 2, rows, cols)
    return run(
        "cut_line",
        body,
        [(half, F32), (half, BF16)],
        [place, *kept, *came],
        smem=1,
        scratch=[pltpu.VMEM((many * tall, cols), F32)],
    )


def fold_line(kept, came):
    count, rows, cols = kept.shape

    def body(kept_ref, came_ref, *out_refs):
        for k in range(count):
            total = kept_ref[k] + came_ref[k].astype(F32)
            out_refs[k % 2][k // 2] = total.astype(out_refs[k % 2].dtype)

    half = (count // 2, rows, cols)
    return run("fold_line", body, [(half, F32), (half, BF16)], [kept, came])


def assemble(replica, parts, edge):
    rows, cols = parts[0].shape
    total = cols * len(parts)

    def body(r_ref, *refs):
        part_refs, (left_ref, right_ref, held) = refs[: len(parts)], refs[len(parts) :]
        for k, ref in enumerate(part_refs):
            held[r_ref[0] ^ k] = ref[...].astype(F32)
        for k in range(len(parts)):
            first, last = k * cols, (k + 1) * cols
            cut = min(max(edge - first, 0), cols)
            if cut > 0:
                left_ref[:, first : first + cut] = held[k, :, :cut]
            if cut < cols:
                right_ref[:, first + cut - edge : last - edge] = held[k, :, cut:]

    return run(
        "assemble",
        body,
        [((rows, edge), F32), ((rows, total - edge), F32)],
        [replica, *parts],
        smem=1,
        scratch=[pltpu.VMEM((len(parts), rows, cols), F32)],
    )


def local(
    item_table,
    action_table,
    item_owner,
    item_row,
    action_owner,
    action_row,
    input_norm_gain,
    w_proj,
    w_out,
    cotangent,
):
    grid = Grid()
    rows, width = item_table.shape
    replicas, line, cores = grid.replicas, grid.line, grid.cores
    cols = width // replicas

    bits = replicas.bit_length() - 1
    swaps = [3, 1, 2] if replicas == 4 else list(range(1, replicas))
    replica, place, core = (i.astype(I32).reshape(1) for i in (grid.r, grid.z, grid.c))
    bases = [((place ^ k) * cores + core) * rows for k in range(line)]

    own = jnp.concatenate(
        [
            lax.dynamic_slice_in_dim(item_table, grid.r * cols, cols, 1),
            lax.dynamic_slice_in_dim(action_table, grid.r * cols, cols, 1),
        ],
        axis=0,
    )
    keys = jnp.stack(
        [
            (item_owner * rows + item_row[:, None])[:, 0],
            (action_owner * rows + action_row[:, None])[:, 0],
        ]
    ).astype(I32)

    keys = jnp.stack([keys, grid.over_pair(keys)])
    keys = jnp.stack([keys] + [grid.over_replica(keys, k) for k in range(1, replicas)])

    held = {0: own}
    for low in reversed([1 << i for i in range(line.bit_length() - 1)]):
        for k in range(low, line, 2 * low):
            held[k] = grid.over_line(held[k ^ low], low)
    order = sorted(held, key=lambda k: (bin(k).count("1"), k))

    key_cols = jnp.broadcast_to(keys[..., None], (*keys.shape, LANES))
    both = list(range(cores))

    found = ()
    for k in order[:-1]:
        found = fetch(bases[k], key_cols, both, held[k], found)
    last = order[-1]
    there = fetch(bases[last], key_cols, both[1:], held[last], found[1:])
    here = fetch(bases[last], key_cols, both[:1], held[last], found[:1])
    pieces = combine([here[0], grid.over_pair(there[0])])
    for k in swaps:
        pieces[k] = grid.over_replica(pieces[k], k)

    gain = input_norm_gain.reshape(1, width)
    layer_out, *rest = sequence(
        replica, core, pieces, cotangent, gain, w_proj, w_out, cores, line
    )
    tokens, (normed, dproj, gated, weights) = rest[:replicas], rest[replicas:]
    for k in swaps:
        tokens[k] = grid.over_replica(tokens[k], k)

    weights = grid.over_pair(weights)
    weights = weight_grad(replica, core, normed, dproj, gated, cotangent, weights, line)
    tokens = lax.optimization_barrier((tokens, weights))[0]
    tokens = pack(tokens)
    there = grid.over_pair(tokens)

    def swap_weights(weights, step):
        kept, sent = weights[0::2], weights[1::2]
        return kept, [grid.over_replica(sent[p], 1 << (p + step) % bits) for p in range(bits)]

    kept, swapped = swap_weights(weights, 0)

    sums, raw, both_there = {}, {}, [tokens, there]
    for k in reversed(order):
        low = (k & -k) or line
        steps = [1 << i for i in range(low.bit_length() - 1)]
        out = F32 if steps else BF16
        if k == last:
            first = gather_grad(bases[k], keys, both[:1], [tokens], rows)
            raw[k] = gather_grad(bases[k], keys, both[1:], [there], rows, first, out)
        else:
            after = {1: raw[last], 0: sums.get(line // 2)}.get(k)
            if after is not None:
                both_there = lax.optimization_barrier((both_there, after))[0]
            raw[k] = gather_grad(bases[k], keys, both, both_there, rows, out=out)
        came = [grid.over_line(sums[k ^ step], step) for step in steps]
        if k == 0:
            table = raw[k][0]
            for part in came[:-1]:
                table = table_sums(table, part, 1)[0]
            item_grad, action_grad = table_sums(table, came[-1], 2)
        else:
            sums[k] = add_up(raw[k] + came) if steps else raw[k][0]

    for step in range(1, bits + 1):
        after = raw[1] if step < bits else [raw[1], sums[line // 2]]
        swapped = lax.optimization_barrier((swapped, after))[0]
        if step < bits:
            kept, swapped = swap_weights(fold(replica, kept, swapped, step), step)
    kept, sent = cut_line(place, kept, swapped, line)
    step = 1
    while step < line // 2:
        came = lax.optimization_barrier((grid.over_line(sent, step), sums[line // 2]))[0]
        kept, sent = fold_line(kept, came)
        step *= 2
    parts = [kept[0], grid.over_line(sent, step)[0]]
    parts = lax.optimization_barrier((parts, raw[0]))[0]
    total = add_up(parts)
    parts = [total] + [grid.over_replica(total, k) for k in range(1, replicas)]
    grad_proj, grad_out = assemble(replica, parts, 4 * width)

    return layer_out, item_grad, action_grad, grad_proj, grad_out


def solution(mesh):
    tokens = ("replica", "sparse")
    in_specs = (
        P("sparse", None),
        P("sparse", None),
        P(tokens, None),
        P(tokens),
        P(tokens, None),
        P(tokens),
        P(),
        P(),
        P(),
        P(tokens, None),
    )
    out_specs = (
        P(tokens, None),
        P("sparse", "replica"),
        P("sparse", "replica"),
        P("sparse", None),
        P("sparse", None),
    )
    return jax.shard_map(local, mesh=mesh, in_specs=in_specs, out_specs=out_specs, check_vma=False)
```

```python
import jax
import jax.numpy as jnp
from jax import lax
from jax.experimental import pallas as pl
from jax.experimental.pallas import tpu as pltpu
from jax.sharding import PartitionSpec as P

HEADS = 4
EPS = 1e-05
LANES = 128
F32 = jnp.float32
BF16 = jnp.bfloat16
I32 = jnp.int32
MIB = 1024 * 1024
EARLY = 6 * 10**9

NN = ((1,), (0,))
NT = ((1,), (1,))
TN = ((0,), (0,))


def dot(left, right, dims=NN):
    return lax.dot_general(left, right, (dims, ((), ())), preferred_element_type=F32)


def sigmoid(value):
    return 0.5 * jnp.tanh(0.5 * value) + 0.5


def run(name, body, outs, args, smem=0, scratch=(), vmem=16, flops=0):
    outs = [jax.ShapeDtypeStruct(shape, dtype) for shape, dtype in outs]
    size = sum(a.size * a.dtype.itemsize for a in [*args, *outs])
    in_smem = pl.BlockSpec(memory_space=pltpu.SMEM)
    in_vmem = pl.BlockSpec(memory_space=pltpu.VMEM)
    places = [in_smem] * smem + [in_vmem] * (len(args) - smem)
    results = pl.pallas_call(
        body,
        out_shape=outs,
        in_specs=places,
        out_specs=[in_vmem] * len(outs),
        scratch_shapes=list(scratch),
        compiler_params=pltpu.CompilerParams(vmem_limit_bytes=vmem * MIB),
        cost_estimate=pl.CostEstimate(flops=flops, bytes_accessed=size, transcendentals=0),
        name=name,
    )(*args)
    return list(results)


class Grid:
    def __init__(self):
        self.replicas = lax.axis_size("replica")
        self.shards = lax.axis_size("sparse")
        self.cores = 2 if self.shards % 2 == 0 else 1
        self.line = self.shards // self.cores
        self.r = lax.axis_index("replica")
        self.s = lax.axis_index("sparse")
        self.z = self.s // self.cores
        self.c = self.s % self.cores

    def over_replica(self, value, step):
        n = self.replicas
        return lax.ppermute(value, "replica", [(i, i ^ step) for i in range(n)])

    def over_line(self, value, step):
        pairs = [(i, i ^ step * self.cores) for i in range(self.shards)]
        return lax.ppermute(value, "sparse", pairs)

    def over_pair(self, value):
        return lax.ppermute(value, "sparse", [(i, i ^ 1) for i in range(self.shards)])


def fetch(base, keys, cohorts, chunk, before=()):
    many = len(cohorts)
    count, _, _, tokens, _ = keys.shape
    rows, cols = chunk.shape[0] // 2, chunk.shape[1]

    def body(base_ref, chunk_ref, key_ref, *refs):
        before_refs, out_refs = refs[:-many], refs[-many:]
        lane = lax.broadcasted_iota(I32, (tokens, LANES), 1)
        for i, m in enumerate(cohorts):
            for k in range(count):
                hot = []
                for table in range(2):
                    place = key_ref[k, m, table] - base_ref[0]
                    for start in range(0, rows, LANES):
                        hot.append(jnp.where(place == lane + start, 1.0, 0.0).astype(BF16))
                found = dot(jnp.concatenate(hot, axis=1), chunk_ref[...])
                if before_refs:
                    found = found + before_refs[i][k].astype(F32)
                out_refs[i][k] = found.astype(BF16)

    return run(
        "fetch",
        body,
        [((count, tokens, cols), BF16)] * many,
        [base, chunk, keys, *before],
        smem=1,
        flops=2 * many * count * tokens * rows * cols,
    )


def combine(parts):
    count, *shape = parts[0].shape

    def body(left_ref, right_ref, *out_refs):
        for k in range(count):
            total = left_ref[k].astype(F32) + right_ref[k].astype(F32)
            out_refs[k][...] = total.astype(BF16)

    return run("combine", body, [(tuple(shape), BF16)] * count, parts)


def pack(parts):
    def body(*refs):
        for k, ref in enumerate(refs[:-1]):
            refs[-1][k] = ref[...]

    shape, dtype = parts[0].shape, parts[0].dtype
    return run("pack", body, [((len(parts), *shape), dtype)], parts)[0]


def add_up(parts):
    def body(*refs):
        total = refs[0][...].astype(F32)
        for ref in refs[1:-1]:
            total = total + ref[...].astype(F32)
        refs[-1][...] = total.astype(BF16)

    return run("add_up", body, [(parts[0].shape, BF16)], parts)[0]


def table_sums(here, came, cuts):
    rows, cols = here.shape[0] // cuts, here.shape[1]

    def body(here_ref, came_ref, *out_refs):
        for i in range(cuts):
            span = slice(i * rows, (i + 1) * rows)
            out_refs[i][...] = here_ref[span, :] + came_ref[span, :].astype(F32)

    outs = [((rows, cols), F32)] * cuts
    return run("table_sums", body, outs, [here, came], flops=EARLY)


def gather_grad(base, keys, cohorts, tokens, rows, before=(), out=BF16):
    many = len(cohorts)
    count, _, _, length = keys.shape
    cols = tokens[0].shape[-1]

    def body(base_ref, key_ref, *refs):
        piece_refs, before_refs = refs[:many], refs[many : many + len(before)]
        out_ref = refs[-1]
        row = lax.broadcasted_iota(I32, (rows, length), 0)
        for table in range(2):
            span = slice(table * rows, (table + 1) * rows)
            sums = None
            for i, m in enumerate(cohorts):
                hot = []
                for k in range(count):
                    place = key_ref[k, m, table : table + 1, :] - base_ref[0]
                    hot.append(jnp.where(place == row, 1.0, 0.0).astype(BF16))
                piece = piece_refs[i][...].reshape(count * length, cols)
                part = dot(jnp.concatenate(hot, axis=1), piece)
                sums = part if sums is None else sums + part
            for ref in before_refs:
                sums = sums + ref[span, :].astype(F32)
            out_ref[span, :] = sums.astype(out)

    return run(
        "gather_grad",
        body,
        [((2 * rows, cols), out)],
        [base, keys, *tokens, *before],
        smem=1,
        flops=4 * many * count * length * 2 * rows * cols,
    )


def sequence(replica, core, pieces, cotangent, gain, w_proj, w_out, cores, line):
    count = len(pieces)
    length, width = cotangent.shape
    cols = width // count
    head_dim = width // HEADS
    factor = head_dim ** (-0.5)
    tile = min(256, length)
    step = min(256, 4 * width)

    def body(r_ref, core_ref, cot_ref, wo_ref, wp_ref, gain_ref, *refs):
        piece_refs, refs = refs[:count], refs[count:]
        out_ref, *grad_refs = refs[: count + 1]
        normed_ref, dproj_ref, gated_ref, weight_ref = refs[count + 1 : count + 5]
        emb, act, slope, att, attn, dscale, dkey, dval, tok = refs[count + 5 :]

        for k in range(count):
            emb[r_ref[0] ^ k] = piece_refs[k][...]

        def embedded(span):
            return jnp.concatenate([emb[k, span] for k in range(count)], axis=1).astype(F32)

        def norm_of(value):
            centred = value - jnp.mean(value, axis=-1, keepdims=True)
            scale = lax.rsqrt(jnp.mean(centred * centred, axis=-1, keepdims=True) + EPS)
            return centred * scale, scale

        def norm_back(upper, hat, scale):
            return scale * (
                upper
                - jnp.mean(upper, axis=-1, keepdims=True)
                - hat * jnp.mean(upper * hat, axis=-1, keepdims=True)
            )

        for at in range(0, length, tile):
            span = slice(at, at + tile)
            hat, _ = norm_of(embedded(span))
            normed_ref[span, :] = (hat * gain_ref[...]).astype(BF16)

        normed = normed_ref[...]

        for at in range(0, 4 * width, step):
            span = slice(at, at + step)
            proj = dot(normed, wp_ref[:, span])
            sig = sigmoid(proj)
            soft = proj * sig
            act[:, span] = soft.astype(BF16)
            slope[:, span] = sig + soft * (1.0 - sig)

        for at in reversed(range(0, length, tile)):
            span = slice(at, at + tile)
            seen = at + tile
            past = slice(0, seen)
            keep = lax.broadcasted_iota(I32, (tile, seen), 1) <= at + lax.broadcasted_iota(
                I32, (tile, seen), 0
            )
            weight = jnp.where(keep, 1.0 / length, 0.0)
            weight_back = jnp.where(keep, factor / length, 0.0)
            for h in range(HEADS):
                head = [slice(p * width + h * head_dim, p * width + (h + 1) * head_dim) for p in range(4)]
                scores = dot(act[span, head[2]], act[past, head[3]], NT) * factor
                sig = sigmoid(scores)
                soft = scores * sig
                attn[h, :, :seen] = (soft * weight).astype(BF16)
                dscale[h, :, :seen] = (sig + soft * (1.0 - sig)) * weight_back
                att[:, head[0]] = dot(attn[h, :, :seen], act[past, head[1]])
            hat, scale = norm_of(att[...])
            gate = act[span, :width].astype(F32)
            gated = (hat * gate).astype(BF16)
            gated_ref[span, :] = gated
            out_ref[span, :] = (embedded(span) + dot(gated, wo_ref[...])).astype(BF16)
            dgated = dot(cot_ref[span, :], wo_ref[...], NT)
            dproj_ref[span, :width] = (dgated * hat * slope[span, :width]).astype(BF16)
            datt = norm_back(dgated * gate, hat, scale).astype(BF16)
            for h in range(HEADS):
                head = [slice(p * width + h * head_dim, p * width + (h + 1) * head_dim) for p in range(4)]
                dhead = datt[:, head[0]]
                dattn = dot(dhead, act[past, head[1]], NT)
                dscores = (dattn * dscale[h, :, :seen]).astype(BF16)
                dquery = dot(dscores, act[past, head[3]])
                dproj_ref[span, head[2]] = (dquery * slope[span, head[2]]).astype(BF16)
                back = dot(dscores, act[span, head[2]], TN), dot(attn[h, :, :seen], dhead, TN)
                for ref, part in zip((dkey, dval), back):
                    if seen == length:
                        ref[past, head[0]] = part
                    else:
                        ref[past, head[0]] += part

        dproj_ref[:, width : 2 * width] = (dval[...] * slope[:, width : 2 * width]).astype(BF16)
        dproj_ref[:, 3 * width :] = (dkey[...] * slope[:, 3 * width :]).astype(BF16)

        dkey[...] = dot(dproj_ref[...], wp_ref[...], NT)
        for at in range(0, length, tile):
            span = slice(at, at + tile)
            hat, scale = norm_of(embedded(span))
            upper = dkey[span, :] * gain_ref[...]
            grad = cot_ref[span, :].astype(F32) + norm_back(upper, hat, scale)
            for k in range(count):
                tok[k, span] = grad[:, k * cols : (k + 1) * cols].astype(BF16)

        for k in range(count):
            grad_refs[k][...] = tok[r_ref[0] ^ k]

        other = (core_ref[0] + 1) % cores
        sums = weight_sums(other, normed_ref, dproj_ref, gated_ref, cot_ref, cores, line, count)
        for k in range(count):
            weight_ref[k] = next(sums).astype(BF16)

    return run(
        "sequence",
        body,
        [
            ((length, width), BF16),
            *[((length, cols), BF16)] * count,
            ((length, width), BF16),
            ((length, 4 * width), BF16),
            ((length, width), BF16),
            ((count, width // cores, 5 * width // count), BF16),
        ],
        [replica, core, cotangent, w_out, w_proj, gain, *pieces],
        smem=2,
        vmem=24,
        flops=32 * length * width * width,
        scratch=[
            pltpu.VMEM((count, length, cols), BF16),
            pltpu.VMEM((length, 4 * width), BF16),
            pltpu.VMEM((length, 4 * width), F32),
            pltpu.VMEM((tile, width), F32),
            pltpu.VMEM((HEADS, tile, length), BF16),
            pltpu.VMEM((HEADS, tile, length), F32),
            pltpu.VMEM((length, width), F32),
            pltpu.VMEM((length, width), F32),
            pltpu.VMEM((count, length, cols), BF16),
        ],
    )


def weight_sums(core, n_ref, d_ref, g_ref, c_ref, cores, line, blocks):
    length, width = n_ref.shape
    rows = width // (cores * line)
    half = width // cores
    edge = d_ref.shape[1]
    cols = (edge + c_ref.shape[1]) // blocks
    feature = lax.broadcasted_iota(I32, (width, half), 0)
    column = lax.broadcasted_iota(I32, (width, half), 1)
    wanted = (column // rows * cores + core) * rows + column % rows
    pick = jnp.where(feature == wanted, 1.0, 0.0).astype(BF16)
    n_part = dot(n_ref[...], pick).astype(BF16)
    g_part = dot(g_ref[...], pick).astype(BF16)
    for k in range(blocks):
        first, last = k * cols, (k + 1) * cols
        parts = []
        if first < edge:
            parts.append(dot(n_part, d_ref[:, first : min(last, edge)], TN))
        if last > edge:
            parts.append(dot(g_part, c_ref[:, max(first, edge) - edge : last - edge], TN))
        yield parts[0] if len(parts) == 1 else jnp.concatenate(parts, axis=1)


def weight_grad(replica, core, normed, dproj, gated, cotangent, before, line):
    blocks, half, cols = before.shape
    length, width = normed.shape
    cores = width // half
    bits = blocks.bit_length() - 1
    tall = half // bits

    def body(r_ref, core_ref, n_ref, d_ref, g_ref, c_ref, before_ref, *refs):
        out_refs, scratch = refs[:-1], refs[-1]
        sums = weight_sums(core_ref[0], n_ref, d_ref, g_ref, c_ref, cores, line, blocks)
        for k in range(blocks):
            total = next(sums) + before_ref[k].astype(F32)
            for p in range(bits):
                at = sum((k >> (p + i) % bits & 1) << bits - 1 - i for i in range(bits))
                scratch[p, at] = total[p * tall : (p + 1) * tall]
        for p in range(bits):
            split_halves(scratch.at[p], r_ref[0] >> p & 1, out_refs[2 * p : 2 * p + 2])

    kept = (blocks // 2, tall, cols)
    return run(
        "weight_grad",
        body,
        [(kept, F32), (kept, BF16)] * bits,
        [replica, core, normed, dproj, gated, cotangent, before],
        smem=2,
        scratch=[pltpu.VMEM((bits, blocks, tall, cols), F32)],
        flops=2 * length * half * (blocks * cols + 2 * width),
    )


def split_halves(ref, bit, out_refs):
    count = ref.shape[0] // 2
    for i, out_ref in enumerate(out_refs):
        start = (bit ^ i) * count
        for k in range(count):
            out_ref[k] = ref[start + k].astype(out_ref.dtype)


def fold(replica, kept, came, step):
    count, tall, cols = kept[0].shape
    many = len(kept)

    def body(r_ref, *refs):
        kept_refs, came_refs, out_refs = refs[:many], refs[many : 2 * many], refs[2 * many : -1]
        scratch = refs[-1]
        for p in range(many):
            for k in range(count):
                scratch[p, k] = kept_refs[p][k] + came_refs[p][k].astype(F32)
            split_halves(scratch.at[p], r_ref[0] >> (p + step) % many & 1, out_refs[2 * p : 2 * p + 2])

    half = (count // 2, tall, cols)
    return run(
        "fold",
        body,
        [(half, F32), (half, BF16)] * many,
        [replica, *kept, *came],
        smem=1,
        scratch=[pltpu.VMEM((many, count, tall, cols), F32)],
    )


def cut_line(place, kept, came, line):
    _, tall, cols = kept[0].shape
    many = len(kept)
    rows = many * tall // line

    def body(place_ref, *refs):
        kept_refs, came_refs, out_refs = refs[:many], refs[many : 2 * many], refs[2 * many : -1]
        scratch = refs[-1]
        for p in range(many):
            scratch[p * tall : (p + 1) * tall] = kept_refs[p][0] + came_refs[p][0].astype(F32)
        for k in range(line):
            span = pl.ds(pl.multiple_of((place_ref[0] ^ k) * rows, rows), rows)
            out_refs[k % 2][k // 2] = scratch[span].astype(out_refs[k % 2].dtype)

    half = (line // 2, rows, cols)
    return run(
        "cut_line",
        body,
        [(half, F32), (half, BF16)],
        [place, *kept, *came],
        smem=1,
        scratch=[pltpu.VMEM((many * tall, cols), F32)],
    )


def fold_line(kept, came):
    count, rows, cols = kept.shape

    def body(kept_ref, came_ref, *out_refs):
        for k in range(count):
            total = kept_ref[k] + came_ref[k].astype(F32)
            out_refs[k % 2][k // 2] = total.astype(out_refs[k % 2].dtype)

    half = (count // 2, rows, cols)
    return run("fold_line", body, [(half, F32), (half, BF16)], [kept, came])


def assemble(replica, parts, edge):
    rows, cols = parts[0].shape
    total = cols * len(parts)

    def body(r_ref, *refs):
        part_refs, (left_ref, right_ref, held) = refs[: len(parts)], refs[len(parts) :]
        for k, ref in enumerate(part_refs):
            held[r_ref[0] ^ k] = ref[...].astype(F32)
        for k in range(len(parts)):
            first, last = k * cols, (k + 1) * cols
            cut = min(max(edge - first, 0), cols)
            if cut > 0:
                left_ref[:, first : first + cut] = held[k, :, :cut]
            if cut < cols:
                right_ref[:, first + cut - edge : last - edge] = held[k, :, cut:]

    return run(
        "assemble",
        body,
        [((rows, edge), F32), ((rows, total - edge), F32)],
        [replica, *parts],
        smem=1,
        scratch=[pltpu.VMEM((len(parts), rows, cols), F32)],
    )


def local(
    item_table,
    action_table,
    item_owner,
    item_row,
    action_owner,
    action_row,
    input_norm_gain,
    w_proj,
    w_out,
    cotangent,
):
    grid = Grid()
    rows, width = item_table.shape
    replicas, line, cores = grid.replicas, grid.line, grid.cores
    cols = width // replicas

    bits = replicas.bit_length() - 1
    swaps = [3, 1, 2] if replicas == 4 else list(range(1, replicas))
    replica, place, core = (i.astype(I32).reshape(1) for i in (grid.r, grid.z, grid.c))
    bases = [((place ^ k) * cores + core) * rows for k in range(line)]

    own = jnp.concatenate(
        [
            lax.dynamic_slice_in_dim(item_table, grid.r * cols, cols, 1),
            lax.dynamic_slice_in_dim(action_table, grid.r * cols, cols, 1),
        ],
        axis=0,
    )
    keys = jnp.stack(
        [
            (item_owner * rows + item_row[:, None])[:, 0],
            (action_owner * rows + action_row[:, None])[:, 0],
        ]
    ).astype(I32)

    keys = jnp.stack([keys, grid.over_pair(keys)])
    keys = jnp.stack([keys] + [grid.over_replica(keys, k) for k in range(1, replicas)])

    held = {0: own}
    for low in reversed([1 << i for i in range(line.bit_length() - 1)]):
        for k in range(low, line, 2 * low):
            held[k] = grid.over_line(held[k ^ low], low)
    order = sorted(held, key=lambda k: (bin(k).count("1"), k))

    key_cols = jnp.broadcast_to(keys[..., None], (*keys.shape, LANES))
    both = list(range(cores))

    found = ()
    for k in order[:-1]:
        found = fetch(bases[k], key_cols, both, held[k], found)
    last = order[-1]
    there = fetch(bases[last], key_cols, both[1:], held[last], found[1:])
    here = fetch(bases[last], key_cols, both[:1], held[last], found[:1])
    pieces = combine([here[0], grid.over_pair(there[0])])
    for k in swaps:
        pieces[k] = grid.over_replica(pieces[k], k)

    gain = input_norm_gain.reshape(1, width)
    layer_out, *rest = sequence(
        replica, core, pieces, cotangent, gain, w_proj, w_out, cores, line
    )
    tokens, (normed, dproj, gated, weights) = rest[:replicas], rest[replicas:]
    for k in swaps:
        tokens[k] = grid.over_replica(tokens[k], k)

    weights = grid.over_pair(weights)
    weights = weight_grad(replica, core, normed, dproj, gated, cotangent, weights, line)
    tokens = lax.optimization_barrier((tokens, weights))[0]
    tokens = pack(tokens)
    there = grid.over_pair(tokens)

    def swap_weights(weights, step):
        kept, sent = weights[0::2], weights[1::2]
        return kept, [grid.over_replica(sent[p], 1 << (p + step) % bits) for p in range(bits)]

    kept, swapped = swap_weights(weights, 0)

    sums, raw, both_there = {}, {}, [tokens, there]
    for k in reversed(order):
        low = (k & -k) or line
        steps = [1 << i for i in range(low.bit_length() - 1)]
        out = F32 if steps else BF16
        if k == last:
            first = gather_grad(bases[k], keys, both[:1], [tokens], rows)
            raw[k] = gather_grad(bases[k], keys, both[1:], [there], rows, first, out)
        else:
            after = {1: raw[last], 0: sums.get(line // 2)}.get(k)
            if after is not None:
                both_there = lax.optimization_barrier((both_there, after))[0]
            raw[k] = gather_grad(bases[k], keys, both, both_there, rows, out=out)
        came = [grid.over_line(sums[k ^ step], step) for step in steps]
        if k == 0:
            table = raw[k][0]
            for part in came[:-1]:
                table = table_sums(table, part, 1)[0]
            item_grad, action_grad = table_sums(table, came[-1], 2)
        else:
            sums[k] = add_up(raw[k] + came) if steps else raw[k][0]

    for step in range(1, bits + 1):
        after = raw[1] if step < bits else [raw[1], raw[line // 2]]
        swapped = lax.optimization_barrier((swapped, after))[0]
        if step < bits:
            kept, swapped = swap_weights(fold(replica, kept, swapped, step), step)
    kept, sent = cut_line(place, kept, swapped, line)
    step = 1
    while step < line // 2:
        came = lax.optimization_barrier((grid.over_line(sent, step), sums[line // 2]))[0]
        kept, sent = fold_line(kept, came)
        step *= 2
    parts = [kept[0], grid.over_line(sent, step)[0]]
    parts = lax.optimization_barrier((parts, table))[0]
    total = add_up(parts)
    parts = [total] + [grid.over_replica(total, k) for k in range(1, replicas)]
    grad_proj, grad_out = assemble(replica, parts, 4 * width)

    return layer_out, item_grad, action_grad, grad_proj, grad_out


def solution(mesh):
    tokens = ("replica", "sparse")
    in_specs = (
        P("sparse", None),
        P("sparse", None),
        P(tokens, None),
        P(tokens),
        P(tokens, None),
        P(tokens),
        P(),
        P(),
        P(),
        P(tokens, None),
    )
    out_specs = (
        P(tokens, None),
        P("sparse", "replica"),
        P("sparse", "replica"),
        P("sparse", None),
        P("sparse", None),
    )
    return jax.shard_map(local, mesh=mesh, in_specs=in_specs, out_specs=out_specs, check_vma=False)
```

```python
import jax
import jax.numpy as jnp
from jax import lax
from jax.experimental import pallas as pl
from jax.experimental.pallas import tpu as pltpu
from jax.sharding import PartitionSpec as P

HEADS = 4
EPS = 1e-05
LANES = 128
F32 = jnp.float32
BF16 = jnp.bfloat16
I32 = jnp.int32
MIB = 1024 * 1024
EARLY = 6 * 10**9

NN = ((1,), (0,))
NT = ((1,), (1,))
TN = ((0,), (0,))


def dot(left, right, dims=NN):
    return lax.dot_general(left, right, (dims, ((), ())), preferred_element_type=F32)


def sigmoid(value):
    return 0.5 * jnp.tanh(0.5 * value) + 0.5


def run(name, body, outs, args, smem=0, scratch=(), vmem=16, flops=0):
    outs = [jax.ShapeDtypeStruct(shape, dtype) for shape, dtype in outs]
    size = sum(a.size * a.dtype.itemsize for a in [*args, *outs])
    in_smem = pl.BlockSpec(memory_space=pltpu.SMEM)
    in_vmem = pl.BlockSpec(memory_space=pltpu.VMEM)
    places = [in_smem] * smem + [in_vmem] * (len(args) - smem)
    results = pl.pallas_call(
        body,
        out_shape=outs,
        in_specs=places,
        out_specs=[in_vmem] * len(outs),
        scratch_shapes=list(scratch),
        compiler_params=pltpu.CompilerParams(vmem_limit_bytes=vmem * MIB),
        cost_estimate=pl.CostEstimate(flops=flops, bytes_accessed=size, transcendentals=0),
        name=name,
    )(*args)
    return list(results)


class Grid:
    def __init__(self):
        self.replicas = lax.axis_size("replica")
        self.shards = lax.axis_size("sparse")
        self.cores = 2 if self.shards % 2 == 0 else 1
        self.line = self.shards // self.cores
        self.r = lax.axis_index("replica")
        self.s = lax.axis_index("sparse")
        self.z = self.s // self.cores
        self.c = self.s % self.cores

    def over_replica(self, value, step):
        n = self.replicas
        return lax.ppermute(value, "replica", [(i, i ^ step) for i in range(n)])

    def over_line(self, value, step):
        pairs = [(i, i ^ step * self.cores) for i in range(self.shards)]
        return lax.ppermute(value, "sparse", pairs)

    def over_pair(self, value):
        return lax.ppermute(value, "sparse", [(i, i ^ 1) for i in range(self.shards)])


def fetch(base, keys, cohorts, chunk, before=()):
    many = len(cohorts)
    count, _, _, tokens, _ = keys.shape
    rows, cols = chunk.shape[0] // 2, chunk.shape[1]

    def body(base_ref, chunk_ref, key_ref, *refs):
        before_refs, out_refs = refs[:-many], refs[-many:]
        lane = lax.broadcasted_iota(I32, (tokens, LANES), 1)
        for i, m in enumerate(cohorts):
            for k in range(count):
                hot = []
                for table in range(2):
                    place = key_ref[k, m, table] - base_ref[0]
                    for start in range(0, rows, LANES):
                        hot.append(jnp.where(place == lane + start, 1.0, 0.0).astype(BF16))
                found = dot(jnp.concatenate(hot, axis=1), chunk_ref[...])
                if before_refs:
                    found = found + before_refs[i][k].astype(F32)
                out_refs[i][k] = found.astype(BF16)

    return run(
        "fetch",
        body,
        [((count, tokens, cols), BF16)] * many,
        [base, chunk, keys, *before],
        smem=1,
        flops=(4 if before else 0) * many * count * tokens * rows * cols,
    )


def combine(parts):
    count, *shape = parts[0].shape

    def body(left_ref, right_ref, *out_refs):
        for k in range(count):
            total = left_ref[k].astype(F32) + right_ref[k].astype(F32)
            out_refs[k][...] = total.astype(BF16)

    return run("combine", body, [(tuple(shape), BF16)] * count, parts)


def pack(parts):
    def body(*refs):
        for k, ref in enumerate(refs[:-1]):
            refs[-1][k] = ref[...]

    shape, dtype = parts[0].shape, parts[0].dtype
    return run("pack", body, [((len(parts), *shape), dtype)], parts)[0]


def add_up(parts):
    def body(*refs):
        total = refs[0][...].astype(F32)
        for ref in refs[1:-1]:
            total = total + ref[...].astype(F32)
        refs[-1][...] = total.astype(BF16)

    return run("add_up", body, [(parts[0].shape, BF16)], parts)[0]


def table_sums(here, came, cuts):
    rows, cols = here.shape[0] // cuts, here.shape[1]

    def body(here_ref, came_ref, *out_refs):
        for i in range(cuts):
            span = slice(i * rows, (i + 1) * rows)
            out_refs[i][...] = here_ref[span, :] + came_ref[span, :].astype(F32)

    outs = [((rows, cols), F32)] * cuts
    return run("table_sums", body, outs, [here, came], flops=EARLY)


def gather_grad(base, keys, cohorts, tokens, rows, before=(), out=BF16):
    many = len(cohorts)
    count, _, _, length = keys.shape
    cols = tokens[0].shape[-1]

    def body(base_ref, key_ref, *refs):
        piece_refs, before_refs = refs[:many], refs[many : many + len(before)]
        out_ref = refs[-1]
        row = lax.broadcasted_iota(I32, (rows, length), 0)
        for table in range(2):
            span = slice(table * rows, (table + 1) * rows)
            sums = None
            for i, m in enumerate(cohorts):
                hot = []
                for k in range(count):
                    place = key_ref[k, m, table : table + 1, :] - base_ref[0]
                    hot.append(jnp.where(place == row, 1.0, 0.0).astype(BF16))
                piece = piece_refs[i][...].reshape(count * length, cols)
                part = dot(jnp.concatenate(hot, axis=1), piece)
                sums = part if sums is None else sums + part
            for ref in before_refs:
                sums = sums + ref[span, :].astype(F32)
            out_ref[span, :] = sums.astype(out)

    return run(
        "gather_grad",
        body,
        [((2 * rows, cols), out)],
        [base, keys, *tokens, *before],
        smem=1,
        flops=4 * many * count * length * 2 * rows * cols,
    )


def sequence(replica, core, pieces, cotangent, gain, w_proj, w_out, cores, line):
    count = len(pieces)
    length, width = cotangent.shape
    cols = width // count
    head_dim = width // HEADS
    factor = head_dim ** (-0.5)
    tile = min(256, length)
    step = min(256, 4 * width)

    def body(r_ref, core_ref, cot_ref, wo_ref, wp_ref, gain_ref, *refs):
        piece_refs, refs = refs[:count], refs[count:]
        out_ref, *grad_refs = refs[: count + 1]
        normed_ref, dproj_ref, gated_ref, weight_ref = refs[count + 1 : count + 5]
        emb, act, slope, att, attn, dscale, dkey, dval, tok = refs[count + 5 :]

        for k in range(count):
            emb[r_ref[0] ^ k] = piece_refs[k][...]

        def embedded(span):
            return jnp.concatenate([emb[k, span] for k in range(count)], axis=1).astype(F32)

        def norm_of(value):
            centred = value - jnp.mean(value, axis=-1, keepdims=True)
            scale = lax.rsqrt(jnp.mean(centred * centred, axis=-1, keepdims=True) + EPS)
            return centred * scale, scale

        def norm_back(upper, hat, scale):
            return scale * (
                upper
                - jnp.mean(upper, axis=-1, keepdims=True)
                - hat * jnp.mean(upper * hat, axis=-1, keepdims=True)
            )

        for at in range(0, length, tile):
            span = slice(at, at + tile)
            hat, _ = norm_of(embedded(span))
            normed_ref[span, :] = (hat * gain_ref[...]).astype(BF16)

        normed = normed_ref[...]

        for at in range(0, 4 * width, step):
            span = slice(at, at + step)
            proj = dot(normed, wp_ref[:, span])
            sig = sigmoid(proj)
            soft = proj * sig
            act[:, span] = soft.astype(BF16)
            slope[:, span] = sig + soft * (1.0 - sig)

        for at in reversed(range(0, length, tile)):
            span = slice(at, at + tile)
            seen = at + tile
            past = slice(0, seen)
            keep = lax.broadcasted_iota(I32, (tile, seen), 1) <= at + lax.broadcasted_iota(
                I32, (tile, seen), 0
            )
            weight = jnp.where(keep, 1.0 / length, 0.0)
            weight_back = jnp.where(keep, factor / length, 0.0)
            for h in range(HEADS):
                head = [slice(p * width + h * head_dim, p * width + (h + 1) * head_dim) for p in range(4)]
                scores = dot(act[span, head[2]], act[past, head[3]], NT) * factor
                sig = sigmoid(scores)
                soft = scores * sig
                attn[h, :, :seen] = (soft * weight).astype(BF16)
                dscale[h, :, :seen] = (sig + soft * (1.0 - sig)) * weight_back
                att[:, head[0]] = dot(attn[h, :, :seen], act[past, head[1]])
            hat, scale = norm_of(att[...])
            gate = act[span, :width].astype(F32)
            gated = (hat * gate).astype(BF16)
            gated_ref[span, :] = gated
            out_ref[span, :] = (embedded(span) + dot(gated, wo_ref[...])).astype(BF16)
            dgated = dot(cot_ref[span, :], wo_ref[...], NT)
            dproj_ref[span, :width] = (dgated * hat * slope[span, :width]).astype(BF16)
            datt = norm_back(dgated * gate, hat, scale).astype(BF16)
            for h in range(HEADS):
                head = [slice(p * width + h * head_dim, p * width + (h + 1) * head_dim) for p in range(4)]
                dhead = datt[:, head[0]]
                dattn = dot(dhead, act[past, head[1]], NT)
                dscores = (dattn * dscale[h, :, :seen]).astype(BF16)
                dquery = dot(dscores, act[past, head[3]])
                dproj_ref[span, head[2]] = (dquery * slope[span, head[2]]).astype(BF16)
                back = dot(dscores, act[span, head[2]], TN), dot(attn[h, :, :seen], dhead, TN)
                for ref, part in zip((dkey, dval), back):
                    if seen == length:
                        ref[past, head[0]] = part
                    else:
                        ref[past, head[0]] += part

        dproj_ref[:, width : 2 * width] = (dval[...] * slope[:, width : 2 * width]).astype(BF16)
        dproj_ref[:, 3 * width :] = (dkey[...] * slope[:, 3 * width :]).astype(BF16)

        dkey[...] = dot(dproj_ref[...], wp_ref[...], NT)
        for at in range(0, length, tile):
            span = slice(at, at + tile)
            hat, scale = norm_of(embedded(span))
            upper = dkey[span, :] * gain_ref[...]
            grad = cot_ref[span, :].astype(F32) + norm_back(upper, hat, scale)
            for k in range(count):
                tok[k, span] = grad[:, k * cols : (k + 1) * cols].astype(BF16)

        for k in range(count):
            grad_refs[k][...] = tok[r_ref[0] ^ k]

        other = (core_ref[0] + 1) % cores
        sums = weight_sums(other, normed_ref, dproj_ref, gated_ref, cot_ref, cores, line, count)
        for k in range(count):
            weight_ref[k] = next(sums).astype(BF16)

    return run(
        "sequence",
        body,
        [
            ((length, width), BF16),
            *[((length, cols), BF16)] * count,
            ((length, width), BF16),
            ((length, 4 * width), BF16),
            ((length, width), BF16),
            ((count, width // cores, 5 * width // count), BF16),
        ],
        [replica, core, cotangent, w_out, w_proj, gain, *pieces],
        smem=2,
        vmem=24,
        flops=32 * length * width * width,
        scratch=[
            pltpu.VMEM((count, length, cols), BF16),
            pltpu.VMEM((length, 4 * width), BF16),
            pltpu.VMEM((length, 4 * width), F32),
            pltpu.VMEM((tile, width), F32),
            pltpu.VMEM((HEADS, tile, length), BF16),
            pltpu.VMEM((HEADS, tile, length), F32),
            pltpu.VMEM((length, width), F32),
            pltpu.VMEM((length, width), F32),
            pltpu.VMEM((count, length, cols), BF16),
        ],
    )


def weight_sums(core, n_ref, d_ref, g_ref, c_ref, cores, line, blocks):
    length, width = n_ref.shape
    rows = width // (cores * line)
    half = width // cores
    edge = d_ref.shape[1]
    cols = (edge + c_ref.shape[1]) // blocks
    feature = lax.broadcasted_iota(I32, (width, half), 0)
    column = lax.broadcasted_iota(I32, (width, half), 1)
    wanted = (column // rows * cores + core) * rows + column % rows
    pick = jnp.where(feature == wanted, 1.0, 0.0).astype(BF16)
    n_part = dot(n_ref[...], pick).astype(BF16)
    g_part = dot(g_ref[...], pick).astype(BF16)
    for k in range(blocks):
        first, last = k * cols, (k + 1) * cols
        parts = []
        if first < edge:
            parts.append(dot(n_part, d_ref[:, first : min(last, edge)], TN))
        if last > edge:
            parts.append(dot(g_part, c_ref[:, max(first, edge) - edge : last - edge], TN))
        yield parts[0] if len(parts) == 1 else jnp.concatenate(parts, axis=1)


def weight_grad(replica, core, normed, dproj, gated, cotangent, before, line):
    blocks, half, cols = before.shape
    length, width = normed.shape
    cores = width // half
    bits = blocks.bit_length() - 1
    tall = half // bits

    def body(r_ref, core_ref, n_ref, d_ref, g_ref, c_ref, before_ref, *refs):
        out_refs, scratch = refs[:-1], refs[-1]
        sums = weight_sums(core_ref[0], n_ref, d_ref, g_ref, c_ref, cores, line, blocks)
        for k in range(blocks):
            total = next(sums) + before_ref[k].astype(F32)
            for p in range(bits):
                at = sum((k >> (p + i) % bits & 1) << bits - 1 - i for i in range(bits))
                scratch[p, at] = total[p * tall : (p + 1) * tall]
        for p in range(bits):
            split_halves(scratch.at[p], r_ref[0] >> p & 1, out_refs[2 * p : 2 * p + 2])

    kept = (blocks // 2, tall, cols)
    return run(
        "weight_grad",
        body,
        [(kept, F32), (kept, BF16)] * bits,
        [replica, core, normed, dproj, gated, cotangent, before],
        smem=2,
        scratch=[pltpu.VMEM((bits, blocks, tall, cols), F32)],
        flops=2 * length * half * (blocks * cols + 2 * width),
    )


def split_halves(ref, bit, out_refs):
    count = ref.shape[0] // 2
    for i, out_ref in enumerate(out_refs):
        start = (bit ^ i) * count
        for k in range(count):
            out_ref[k] = ref[start + k].astype(out_ref.dtype)


def fold(replica, kept, came, step):
    count, tall, cols = kept[0].shape
    many = len(kept)

    def body(r_ref, *refs):
        kept_refs, came_refs, out_refs = refs[:many], refs[many : 2 * many], refs[2 * many : -1]
        scratch = refs[-1]
        for p in range(many):
            for k in range(count):
                scratch[p, k] = kept_refs[p][k] + came_refs[p][k].astype(F32)
            split_halves(scratch.at[p], r_ref[0] >> (p + step) % many & 1, out_refs[2 * p : 2 * p + 2])

    half = (count // 2, tall, cols)
    return run(
        "fold",
        body,
        [(half, F32), (half, BF16)] * many,
        [replica, *kept, *came],
        smem=1,
        scratch=[pltpu.VMEM((many, count, tall, cols), F32)],
    )


def cut_line(place, kept, came, line):
    _, tall, cols = kept[0].shape
    many = len(kept)
    rows = many * tall // line

    def body(place_ref, *refs):
        kept_refs, came_refs, out_refs = refs[:many], refs[many : 2 * many], refs[2 * many : -1]
        scratch = refs[-1]
        for p in range(many):
            scratch[p * tall : (p + 1) * tall] = kept_refs[p][0] + came_refs[p][0].astype(F32)
        for k in range(line):
            span = pl.ds(pl.multiple_of((place_ref[0] ^ k) * rows, rows), rows)
            out_refs[k % 2][k // 2] = scratch[span].astype(out_refs[k % 2].dtype)

    half = (line // 2, rows, cols)
    return run(
        "cut_line",
        body,
        [(half, F32), (half, BF16)],
        [place, *kept, *came],
        smem=1,
        scratch=[pltpu.VMEM((many * tall, cols), F32)],
    )


def fold_line(kept, came):
    count, rows, cols = kept.shape

    def body(kept_ref, came_ref, *out_refs):
        for k in range(count):
            total = kept_ref[k] + came_ref[k].astype(F32)
            out_refs[k % 2][k // 2] = total.astype(out_refs[k % 2].dtype)

    half = (count // 2, rows, cols)
    return run("fold_line", body, [(half, F32), (half, BF16)], [kept, came])


def assemble(replica, parts, edge):
    rows, cols = parts[0].shape
    total = cols * len(parts)

    def body(r_ref, *refs):
        part_refs, (left_ref, right_ref, held) = refs[: len(parts)], refs[len(parts) :]
        for k, ref in enumerate(part_refs):
            held[r_ref[0] ^ k] = ref[...].astype(F32)
        for k in range(len(parts)):
            first, last = k * cols, (k + 1) * cols
            cut = min(max(edge - first, 0), cols)
            if cut > 0:
                left_ref[:, first : first + cut] = held[k, :, :cut]
            if cut < cols:
                right_ref[:, first + cut - edge : last - edge] = held[k, :, cut:]

    return run(
        "assemble",
        body,
        [((rows, edge), F32), ((rows, total - edge), F32)],
        [replica, *parts],
        smem=1,
        scratch=[pltpu.VMEM((len(parts), rows, cols), F32)],
    )


def local(
    item_table,
    action_table,
    item_owner,
    item_row,
    action_owner,
    action_row,
    input_norm_gain,
    w_proj,
    w_out,
    cotangent,
):
    grid = Grid()
    rows, width = item_table.shape
    replicas, line, cores = grid.replicas, grid.line, grid.cores
    cols = width // replicas

    bits = replicas.bit_length() - 1
    swaps = [3, 1, 2] if replicas == 4 else list(range(1, replicas))
    replica, place, core = (i.astype(I32).reshape(1) for i in (grid.r, grid.z, grid.c))
    bases = [((place ^ k) * cores + core) * rows for k in range(line)]

    own = jnp.concatenate(
        [
            lax.dynamic_slice_in_dim(item_table, grid.r * cols, cols, 1),
            lax.dynamic_slice_in_dim(action_table, grid.r * cols, cols, 1),
        ],
        axis=0,
    )
    keys = jnp.stack(
        [
            (item_owner * rows + item_row[:, None])[:, 0],
            (action_owner * rows + action_row[:, None])[:, 0],
        ]
    ).astype(I32)

    keys = jnp.stack([keys, grid.over_pair(keys)])
    keys = jnp.stack([keys] + [grid.over_replica(keys, k) for k in range(1, replicas)])

    key_cols = jnp.broadcast_to(keys[..., None], (*keys.shape, LANES))
    both = list(range(cores))
    found = fetch(bases[0], key_cols, both, own)

    held = {0: own}
    for low in reversed([1 << i for i in range(line.bit_length() - 1)]):
        for k in range(low, line, 2 * low):
            source = held[k ^ low]
            if k != low:
                source = lax.optimization_barrier((source, found))[0]
            held[k] = grid.over_line(source, low)
    order = sorted(held, key=lambda k: (bin(k).count("1"), k))

    for k in order[1:-1]:
        found = fetch(bases[k], key_cols, both, held[k], found)
    last = order[-1]
    there = fetch(bases[last], key_cols, both[1:], held[last], found[1:])
    here = fetch(bases[last], key_cols, both[:1], held[last], found[:1])
    pieces = combine([here[0], grid.over_pair(there[0])])
    for k in swaps:
        pieces[k] = grid.over_replica(pieces[k], k)

    gain = input_norm_gain.reshape(1, width)
    layer_out, *rest = sequence(
        replica, core, pieces, cotangent, gain, w_proj, w_out, cores, line
    )
    tokens, (normed, dproj, gated, weights) = rest[:replicas], rest[replicas:]
    for k in swaps:
        tokens[k] = grid.over_replica(tokens[k], k)

    weights = grid.over_pair(weights)
    weights = weight_grad(replica, core, normed, dproj, gated, cotangent, weights, line)
    tokens = lax.optimization_barrier((tokens, weights))[0]
    tokens = pack(tokens)
    there = grid.over_pair(tokens)

    def swap_weights(weights, step):
        kept, sent = weights[0::2], weights[1::2]
        return kept, [grid.over_replica(sent[p], 1 << (p + step) % bits) for p in range(bits)]

    kept, swapped = swap_weights(weights, 0)

    sums, raw, both_there = {}, {}, [tokens, there]
    for k in reversed(order):
        low = (k & -k) or line
        steps = [1 << i for i in range(low.bit_length() - 1)]
        out = F32 if steps else BF16
        if k == last:
            first = gather_grad(bases[k], keys, both[:1], [tokens], rows)
            raw[k] = gather_grad(bases[k], keys, both[1:], [there], rows, first, out)
        else:
            after = {1: raw[last], 0: sums.get(line // 2)}.get(k)
            if after is not None:
                both_there = lax.optimization_barrier((both_there, after))[0]
            raw[k] = gather_grad(bases[k], keys, both, both_there, rows, out=out)
        came = [grid.over_line(sums[k ^ step], step) for step in steps]
        if k == 0:
            table = raw[k][0]
            for part in came[:-1]:
                table = table_sums(table, part, 1)[0]
            item_grad, action_grad = table_sums(table, came[-1], 2)
        else:
            sums[k] = add_up(raw[k] + came) if steps else raw[k][0]

    for step in range(1, bits + 1):
        after = raw[1] if step < bits else [raw[1], sums[line // 2]]
        swapped = lax.optimization_barrier((swapped, after))[0]
        if step < bits:
            kept, swapped = swap_weights(fold(replica, kept, swapped, step), step)
    kept, sent = cut_line(place, kept, swapped, line)
    step = 1
    while step < line // 2:
        came = lax.optimization_barrier((grid.over_line(sent, step), sums[line // 2]))[0]
        kept, sent = fold_line(kept, came)
        step *= 2
    parts = [kept[0], grid.over_line(sent, step)[0]]
    parts = lax.optimization_barrier((parts, raw[0]))[0]
    total = add_up(parts)
    parts = [total] + [grid.over_replica(total, k) for k in range(1, replicas)]
    grad_proj, grad_out = assemble(replica, parts, 4 * width)

    return layer_out, item_grad, action_grad, grad_proj, grad_out


def solution(mesh):
    tokens = ("replica", "sparse")
    in_specs = (
        P("sparse", None),
        P("sparse", None),
        P(tokens, None),
        P(tokens),
        P(tokens, None),
        P(tokens),
        P(),
        P(),
        P(),
        P(tokens, None),
    )
    out_specs = (
        P(tokens, None),
        P("sparse", "replica"),
        P("sparse", "replica"),
        P("sparse", None),
        P("sparse", None),
    )
    return jax.shard_map(local, mesh=mesh, in_specs=in_specs, out_specs=out_specs, check_vma=False)
```
